32 devices in a mesh: section: 2 (over core), seq: 16 (over z, y, x).
Axes of the slice: x: 2, y: 2, z: 4, core: 2. Of those that a mesh axis runs over, the one named last changes fastest.
Arguments:
- hidden_in: bfloat16 [2, 2048, 2048], P(None, 'seq'), may hold values from -6 to 6
- cotangent: float32 [2, 2048, 2048], P(None, 'seq'), may hold values from -6 to 6
- norm_gain: bfloat16 [2, 2048], P('section', 'seq'), may hold values from 0.5 to 1.5
- in_weight: bfloat16 [2, 2048, 8192], P('section', 'seq'), may hold values from -0.125 to 0.125
- conv_weight: bfloat16 [2, 4, 4096], P('section', None, 'seq'), may hold values from -3 to 3
- conv_bias: bfloat16 [2, 4096], P('section', 'seq'), may hold values from -3 to 3
- xproj_weight: bfloat16 [2, 4096, 160], P('section', 'seq'), may hold values from -0.09375 to 0.09375
- dt_weight: bfloat16 [2, 128, 4096], P('section', None, 'seq'), may hold values from -0.5 to 0.5
- dt_bias: bfloat16 [2, 4096], P('section', 'seq'), may hold values from -12 to -2
- skip_gain: bfloat16 [2, 4096], P('section', 'seq'), may hold values from 0.5 to 1.5
- out_weight: bfloat16 [2, 4096, 2048], P('section', 'seq'), may hold values from -0.25 to 0.25
Outputs:
- layer_outputs: float32 [2, 2, 2048, 2048], P('section', None, 'seq')
- input_grads: float32 [2, 2, 2048, 2048], P('section', None, 'seq')
- norm_gain_grad: float32 [2, 2048], P('section', 'seq')
- in_weight_grad: float32 [2, 2048, 8192], P('section', 'seq')
- conv_weight_grad: float32 [2, 4, 4096], P('section', None, 'seq')
- conv_bias_grad: float32 [2, 4096], P('section', 'seq')
- xproj_weight_grad: float32 [2, 4096, 160], P('section', 'seq')
- dt_weight_grad: float32 [2, 128, 4096], P('section', None, 'seq')
- dt_bias_grad: float32 [2, 4096], P('section', 'seq')
- skip_gain_grad: float32 [2, 4096], P('section', 'seq')
- out_weight_grad: float32 [2, 4096, 2048], P('section', 'seq')
The draws below stay inside these ranges and needn't reach their ends.
All inputs are finite; a program needn't handle non-finite values.
Results may differ from the reference program's by a relative error of at most 0.018.
Values may be sent and summed in bfloat16 or wider, within the bound.
A program may use at most 384 MiB of HBM per device.

```python
import jax
import jax.numpy as jnp
from jax import lax

D = 2048
E = 4096
N = 16
R = 128
KC = 4
MB = 2
LAYERS = 2
TOKENS = 2048


def draw_dt_bias(key, part):
    key = jax.random.fold_in(key, 11)
    return jax.random.uniform(key, (LAYERS, E), jnp.float32, -12.0, -2.0).astype(jnp.bfloat16)


def shard_levels(own_key, shape, shards, low, largest):
    def one(axis_at, shards_of):
        steps = jax.random.uniform(jax.random.fold_in(jax.random.fold_in(own_key, 6), axis_at), (shards_of,), jnp.float32, low / len(shards), largest / len(shards))
        return jnp.repeat(jnp.exp(steps), shape[axis_at] // shards_of).reshape((-1,) + (1,) * (len(shape) - axis_at - 1))

    factor_of = one(*shards[0])
    for cut in shards[1:]:
        factor_of = factor_of * one(*cut)
    return factor_of


def centred(key, shape, spread, bound, shards=(), kind=jnp.bfloat16):
    array = jax.random.normal(key, shape, jnp.float32) * spread
    if len(shards) > 0:
        array = shard_levels(key, shape, shards, -0.22, 0.18) * array
    return jnp.clip(array, min=-bound, max=bound).astype(kind)


def setup_inputs(seed: int = 0) -> dict:
    key_of = jax.random.split(jax.random.key(seed), 12)
    hidden_in = centred(key_of[0], (MB, TOKENS, D), 1.0, 6.0, ((1, 16),))
    cotangent = centred(key_of[1], (MB, TOKENS, D), 1.0, 6.0, ((1, 16),), jnp.float32)
    norm_gain = jnp.clip(1.0 + 0.1 * jax.random.normal(key_of[2], (LAYERS, D), jnp.float32), 0.5, 1.5).astype(jnp.bfloat16)
    in_weight = centred(key_of[3], (LAYERS, D, 2 * E), D ** -0.5, 0.125, ((0, 2), (1, 16)))
    conv_weight = centred(key_of[4], (LAYERS, KC, E), KC ** -0.5, 3.0, ((0, 2), (2, 16)))
    conv_bias = centred(key_of[5], (LAYERS, E), 0.5, 3.0, ((0, 2), (1, 16)))
    xproj_weight = centred(key_of[6], (LAYERS, E, R + 2 * N), E ** -0.5, 0.09375, ((0, 2), (1, 16)))
    dt_weight = centred(key_of[7], (LAYERS, R, E), R ** -0.5, 0.5, ((0, 2), (2, 16)))
    dt_bias = draw_dt_bias(jax.random.fold_in(key_of[11], 71), 0)
    skip_gain = jnp.clip(0.5 + 1.0 * jax.random.uniform(key_of[9], (LAYERS, E), jnp.float32) ** shard_levels(key_of[9], (LAYERS, E), ((0, 2), (1, 16)), -0.2, 0.2), 0.5, 1.5).astype(jnp.bfloat16)
    out_weight = centred(key_of[10], (LAYERS, E, D), (E // 8) ** -0.5, 0.25, ((0, 2), (1, 16)))
    return {"hidden_in": hidden_in, "cotangent": cotangent, "norm_gain": norm_gain, "in_weight": in_weight, "conv_weight": conv_weight, "conv_bias": conv_bias, "xproj_weight": xproj_weight, "dt_weight": dt_weight, "dt_bias": dt_bias, "skip_gain": skip_gain, "out_weight": out_weight}


block_len = 16
norm_eps = 1e-05

@jax.custom_vjp
def low(v):
    return lax.optimization_barrier(v.astype(jnp.bfloat16)).astype(jnp.float32)

@jax.custom_vjp
def low_back(v):
    return v

def low_keep(v):
    return (low(v), None)

def low_pass(kept, grad):
    return (grad,)

def back_keep(v):
    return (v, None)

def back_low(kept, grad):
    return (low(grad),)
low.defvjp(low_keep, low_pass)
low_back.defvjp(back_keep, back_low)

def matmul(operand, factor):
    return jnp.dot(operand, factor, precision=lax.Precision.HIGHEST, preferred_element_type=jnp.float32)

def rms_norm(stream, norm_gain):
    inverse_rms = lax.rsqrt(lax.optimization_barrier(jnp.mean(stream * stream, axis=-1, keepdims=True)) + norm_eps)
    return stream * inverse_rms * norm_gain[None, :]

def causal_conv(extended, conv_taps, conv_shift):
    length = extended.shape[0] - conv_taps.shape[0] + 1
    summed = jnp.broadcast_to(conv_shift[None, :], (length, conv_shift.shape[0]))
    for offset in range(conv_taps.shape[0]):
        summed = summed + conv_taps[offset][None, :] * extended[offset:offset + length]
    return jax.nn.silu(summed)

def step_rates(delta_dot, delta_bias, key_vec):
    write_gate = jax.nn.sigmoid(delta_dot + delta_bias[None, :])
    return write_gate / (1.0 + write_gate * lax.optimization_barrier(jnp.sum(key_vec * key_vec, axis=-1, keepdims=True)))

def run_block(memory, strengths, key_blk, inner_blk, query_blk):
    outputs = []
    for position in range(strengths.shape[0]):
        square = key_blk[position] * key_blk[position]
        fading = 1.0 - strengths[position][:, None] * square[None, :]
        memory = fading * memory + (strengths[position] * inner_blk[position])[:, None] * key_blk[position][None, :]
        outputs.append(lax.optimization_barrier(jnp.sum(memory * query_blk[position][None, :], axis=1)))
    return (memory, jnp.stack(outputs))

def recurrence(strengths, key_vec, inner_act, query_vec):
    blocks = strengths.shape[0] // block_len

    def shaped(values):
        return values.reshape((blocks, block_len) + values.shape[1:])

    def advance(memory, pieces):
        return run_block(memory, pieces[0], pieces[1], pieces[2], pieces[3])
    opening = jnp.zeros((strengths.shape[1], key_vec.shape[1]), jnp.float32)
    closing, outputs = lax.scan(jax.checkpoint(advance), opening, (shaped(strengths), shaped(key_vec), shaped(inner_act), shaped(query_vec)))
    return outputs.reshape(strengths.shape)

def layer_apply(stream, norm_gain, in_weight, conv_weight, conv_bias, xproj_weight, dt_weight, dt_bias, skip_gain, out_weight):
    normed = low(rms_norm(stream, norm_gain))
    projected = low(low_back(matmul(normed, in_weight)))
    inner = projected[:, :E]
    gate_in = projected[:, E:]
    extended = jnp.concatenate([jnp.zeros((KC - 1, E), jnp.float32), inner], axis=0)
    inner_act = causal_conv(extended, conv_weight, conv_bias)
    xproj_out = low(low_back(matmul(low(inner_act), xproj_weight)))
    delta_low = xproj_out[:, :R]
    key_vec = xproj_out[:, R:R + N]
    query_vec = xproj_out[:, R + N:]
    strengths = step_rates(low_back(matmul(delta_low, dt_weight)), dt_bias, key_vec)
    recur_out = recurrence(strengths, key_vec, inner_act, query_vec) + skip_gain[None, :] * inner_act
    gated = low(low_back(recur_out * jax.nn.silu(gate_in)))
    return stream + low_back(matmul(gated, out_weight))

def reference(hidden_in, cotangent, norm_gain, in_weight, conv_weight, conv_bias, xproj_weight, dt_weight, dt_bias, skip_gain, out_weight):
    params = tuple((piece.astype(jnp.float32) for piece in (norm_gain, in_weight, conv_weight, conv_bias, xproj_weight, dt_weight, dt_bias, skip_gain, out_weight)))
    hidden = hidden_in.astype(jnp.float32)
    extra_in = jnp.zeros_like(hidden)

    def forward_model(hidden, extra_in, params):
        lower_layer = tuple((piece[0] for piece in params))
        upper_layer = tuple((piece[1] for piece in params))

        def one_sequence(sequence_pair):
            first_out = low(low_back(layer_apply(sequence_pair[0], *lower_layer)))
            second_out = layer_apply(first_out + sequence_pair[1], *upper_layer)
            return (first_out, second_out)
        return lax.map(one_sequence, (hidden, extra_in))
    (first_outs, second_outs), pullback = jax.vjp(forward_model, hidden, extra_in, params)
    d_hidden, d_extra, d_params = pullback((jnp.zeros_like(first_outs), cotangent.astype(jnp.float32)))
    return (jnp.stack([first_outs, second_outs]), jnp.stack([d_hidden, d_extra]), d_params[0], d_params[1], d_params[2], d_params[3], d_params[4], d_params[5], d_params[6], d_params[7], d_params[8])
```

```python
import functools

import jax
import jax.numpy as jnp
from jax import lax
from jax.experimental import pallas as pl
from jax.experimental.pallas import tpu as pltpu
from jax.sharding import Mesh, PartitionSpec as P


N = 16
R = 128
KC = 4
BLOCK = 128
norm_eps = 1e-05
BF = jnp.bfloat16
F32 = jnp.float32
MESH = pl.DeviceIdType.MESH


def forward_dot(operand, factor):
    return jnp.dot(operand, factor, preferred_element_type=F32)


def cross_dot(operand, factor):
    return lax.dot_general(operand, factor, (((0,), (0,)), ((), ())), preferred_element_type=F32)


def back_dot(operand, factor):
    return lax.dot_general(operand, factor, (((1,), (1,)), ((), ())), preferred_element_type=F32)


def widths(channels):
    wide = min(channels, 128)
    return wide, channels // wide


def sum_rows(pieces):
    row = lax.broadcasted_iota(jnp.int32, pieces[0].shape, 0)
    shift = 1
    while len(pieces) > 1:
        keep = (row & shift) == 0
        pieces = [
            jnp.where(keep, a, b) + pltpu.roll(jnp.where(keep, b, a), shift, 0)
            for a, b in zip(pieces[0::2], pieces[1::2])
        ]
        shift *= 2
    return pieces[0]


def halves(v):
    return v[:8] + v[8:]


def lanes_of(p, wide):
    return slice(p * wide, (p + 1) * wide)


def recur_forward_kernel(rate_ref, act_ref, key_ref, query_ref, out_ref, before_ref, last_ref, memory_ref):
    wide, parts = widths(rate_ref.shape[1])

    @pl.when(pl.program_id(0) == 0)
    def _():
        memory_ref[...] = jnp.zeros_like(memory_ref)

    memory = [memory_ref[:, lanes_of(p, wide)] for p in range(parts)]
    for base in range(0, rate_ref.shape[0], 8):
        rates = rate_ref[base : base + 8, :]
        feeds = rates * act_ref[base : base + 8, :]
        sums = [[] for _ in range(parts)]
        for i in range(8):
            key = jnp.broadcast_to(key_ref[:, base + i : base + i + 1], (N, wide))
            query = jnp.broadcast_to(query_ref[:, base + i : base + i + 1], (N, wide))
            square = key * key
            for p in range(parts):
                lanes = lanes_of(p, wide)
                before_ref[base + i, :, lanes] = memory[p]
                memory[p] = (1.0 - rates[i : i + 1, lanes] * square) * memory[p] + key * feeds[i : i + 1, lanes]
                sums[p].append(halves(memory[p] * query))
        for p in range(parts):
            out_ref[base : base + 8, lanes_of(p, wide)] = sum_rows(sums[p])
    for p in range(parts):
        memory_ref[:, lanes_of(p, wide)] = memory[p]

    @pl.when(pl.program_id(0) == pl.num_programs(0) - 1)
    def _():
        last_ref[...] = memory_ref[...]


def recur_forward(rate, act, key_t, query_t):
    tokens, channels = rate.shape
    rows = pl.BlockSpec((BLOCK, channels), lambda i: (i, 0))
    cols = pl.BlockSpec((N, BLOCK), lambda i: (0, i))
    return pl.pallas_call(
        recur_forward_kernel,
        grid=(tokens // BLOCK,),
        in_specs=[rows, rows, cols, cols],
        out_specs=[
            rows,
            pl.BlockSpec((BLOCK, N, channels), lambda i: (i, 0, 0)),
            pl.BlockSpec((N, channels), lambda i: (0, 0)),
        ],
        out_shape=[
            jax.ShapeDtypeStruct((tokens, channels), F32),
            jax.ShapeDtypeStruct((tokens, N, channels), F32),
            jax.ShapeDtypeStruct((N, channels), F32),
        ],
        scratch_shapes=[pltpu.VMEM((N, channels), F32)],
        compiler_params=pltpu.CompilerParams(
            dimension_semantics=("arbitrary",), vmem_limit_bytes=40 * 2**20
        ),
        cost_estimate=pl.CostEstimate(
            flops=10 * tokens * N * channels, bytes_accessed=4 * tokens * channels * (N + 3), transcendentals=0
        ),
    )(rate, act, key_t, query_t)


def recur_backward_kernel(
    rate_ref, act_ref, grad_ref, key_ref, query_ref, before_ref, last_ref,
    d_rate_ref, d_act_ref, d_key_ref, d_query_ref, lam_ref, memory_ref, key_rows, query_rows,
):
    wide, parts = widths(rate_ref.shape[1])
    block = rate_ref.shape[0]

    @pl.when(pl.program_id(0) == 0)
    def _():
        lam_ref[...] = jnp.zeros_like(lam_ref)
        memory_ref[...] = last_ref[...]

    lam = [lam_ref[:, lanes_of(p, wide)] for p in range(parts)]
    memory = [memory_ref[:, lanes_of(p, wide)] for p in range(parts)]
    for base in reversed(range(0, block, 8)):
        rates = rate_ref[base : base + 8, :]
        acts = act_ref[base : base + 8, :]
        grads = grad_ref[base : base + 8, :]
        d_rates = [[None] * 8 for _ in range(parts)]
        d_acts = [[None] * 8 for _ in range(parts)]
        for i in reversed(range(8)):
            at = base + i
            key = jnp.broadcast_to(key_ref[:, at : at + 1], (N, wide))
            query = jnp.broadcast_to(query_ref[:, at : at + 1], (N, wide))
            square = key * key
            key_sum = query_sum = None
            for p in range(parts):
                lanes = lanes_of(p, wide)
                grad = grads[i : i + 1, lanes]
                before = before_ref[at, :, lanes]
                pulled = query * grad + lam[p]
                kept = key * before
                missing = acts[i : i + 1, lanes] - kept
                keyed = pulled * key
                scaled = pulled * rates[i : i + 1, lanes]
                d_acts[p][i] = halves(keyed)
                d_rates[p][i] = halves(keyed * missing)
                to_key = scaled * (missing - kept)
                to_query = memory[p] * grad
                key_sum = to_key if key_sum is None else key_sum + to_key
                query_sum = to_query if query_sum is None else query_sum + to_query
                lam[p] = pulled - scaled * square
                memory[p] = before
            key_rows[at * N : (at + 1) * N, :] = key_sum.astype(BF)
            query_rows[at * N : (at + 1) * N, :] = query_sum.astype(BF)
        for p in range(parts):
            lanes = lanes_of(p, wide)
            d_rate_ref[base : base + 8, lanes] = sum_rows(d_rates[p])
            d_act_ref[base : base + 8, lanes] = rates[:, lanes] * sum_rows(d_acts[p])
    for p in range(parts):
        lam_ref[:, lanes_of(p, wide)] = lam[p]
        memory_ref[:, lanes_of(p, wide)] = memory[p]

    ones = jnp.ones((wide, block), BF)
    token = lax.broadcasted_iota(jnp.int32, (block, N, block), 0)
    own = token == lax.broadcasted_iota(jnp.int32, (block, N, block), 2)
    for rows, result in ((key_rows, d_key_ref), (query_rows, d_query_ref)):
        sums = forward_dot(rows[...], ones).reshape(block, N, block)
        result[...] = jnp.sum(jnp.where(own, sums, 0.0), axis=0)


def recur_backward(rate, act, grad, key_t, query_t, before, last):
    tokens, channels = rate.shape
    count = tokens // BLOCK
    rows = pl.BlockSpec((BLOCK, channels), lambda i: (count - 1 - i, 0))
    cols = pl.BlockSpec((N, BLOCK), lambda i: (0, count - 1 - i))
    products = pltpu.VMEM((BLOCK * N, widths(channels)[0]), BF)
    return pl.pallas_call(
        recur_backward_kernel,
        grid=(count,),
        in_specs=[
            rows, rows, rows, cols, cols,
            pl.BlockSpec((BLOCK, N, channels), lambda i: (count - 1 - i, 0, 0)),
            pl.BlockSpec((N, channels), lambda i: (0, 0)),
        ],
        out_specs=[rows, rows, cols, cols],
        out_shape=[
            jax.ShapeDtypeStruct((tokens, channels), F32),
            jax.ShapeDtypeStruct((tokens, channels), F32),
            jax.ShapeDtypeStruct((N, tokens), F32),
            jax.ShapeDtypeStruct((N, tokens), F32),
        ],
        scratch_shapes=[pltpu.VMEM((N, channels), F32), pltpu.VMEM((N, channels), F32), products, products],
        compiler_params=pltpu.CompilerParams(
            dimension_semantics=("arbitrary",), vmem_limit_bytes=40 * 2**20
        ),
        cost_estimate=pl.CostEstimate(
            flops=30 * tokens * N * channels, bytes_accessed=4 * tokens * channels * (N + 5), transcendentals=0
        ),
    )(rate, act, grad, key_t, query_t, before, last)


def swap(value, axis):
    return lax.ppermute(value, axis, [(0, 1), (1, 0)])


def meet(z, count):
    barrier = pltpu.get_barrier_semaphore()

    def greet(where):
        pl.semaphore_signal(barrier, inc=1, device_id=where, device_id_type=MESH)

    greet({"y": 1 - lax.axis_index("y")})
    greet({"section": 1 - lax.axis_index("section")})
    pl.when(z > 0)(lambda: greet({"z": z - 1}))
    pl.when(z < count - 1)(lambda: greet({"z": z + 1}))
    inside = jnp.logical_and(z > 0, z < count - 1)
    pl.semaphore_wait(barrier, 2 + min(count - 1, 1) + inside.astype(jnp.int32))


def gather_kernel(
    count, shard_ref, out_ref, local_sem, right_send, right_recv, left_send, left_recv, y_send, y_recv, core_send, core_recv
):
    z, y, s = lax.axis_index("z"), lax.axis_index("y"), lax.axis_index("section")

    def at(z_of, y_of, s_of):
        return out_ref.at[(z_of * 2 + y_of) * 2 + s_of]

    def move(origin, y_of, send, recv, where, own=False):
        place = at(origin, y_of, s)
        return pltpu.make_async_remote_copy(
            src_ref=shard_ref if own else place,
            dst_ref=place,
            send_sem=send,
            recv_sem=recv,
            device_id=where,
            device_id_type=MESH,
        )

    def right(j, own=False):
        return move(z - j, y, right_send.at[j], right_recv.at[j], {"z": z + 1}, own)

    def left(j, own=False):
        return move(z + j, y, left_send.at[j], left_recv.at[j], {"z": z - 1}, own)

    def across(origin, own=False):
        return move(origin, y, y_send.at[origin], y_recv.at[origin], {"y": 1 - y}, own)

    def core(origin, y_of, own=False):
        k = origin * 2 + y_of
        return move(origin, y_of, core_send.at[k], core_recv.at[k], {"section": 1 - s}, own)

    def arrived(origin, y_of, s_of, recv):
        place = at(origin, y_of, s_of)
        pltpu.make_async_copy(place, place, recv).wait()

    meet(z, count)
    pl.when(z < count - 1)(lambda: right(0, True).start())
    pl.when(z > 0)(lambda: left(0, True).start())
    across(z, True).start()
    core(z, y, True).start()
    own = pltpu.make_async_copy(shard_ref, at(z, y, s), local_sem)
    own.start()

    def from_y(origin):
        arrived(origin, 1 - y, s, y_recv.at[origin])
        core(origin, 1 - y).start()

    for j in range(count - 1):

        @pl.when(z - 1 - j >= 0)
        def _(j=j):
            origin = z - 1 - j
            arrived(origin, y, s, right_recv.at[j])
            pl.when(z < count - 1)(lambda: right(j + 1).start())
            across(origin).start()
            core(origin, y).start()

        @pl.when(z + 1 + j <= count - 1)
        def _(j=j):
            origin = z + 1 + j
            arrived(origin, y, s, left_recv.at[j])
            pl.when(z > 0)(lambda: left(j + 1).start())
            across(origin).start()
            core(origin, y).start()

        if j == 0:
            from_y(z)
        else:
            pl.when(z - j >= 0)(lambda j=j: from_y(z - j))
            pl.when(z + j <= count - 1)(lambda j=j: from_y(z + j))

    last = count - 1
    if count > 1:
        pl.when(z - last >= 0)(lambda: from_y(z - last))
        pl.when(z + last <= count - 1)(lambda: from_y(z + last))
    else:
        from_y(z)

    own.wait()
    for k in range(count):
        for y_of in range(2):
            arrived(k, y_of, 1 - s, core_recv.at[k * 2 + y_of])
            core(k, y_of).wait_send()
        across(k).wait_send()
    for j in range(count - 1):
        pl.when((z - j >= 0) & (z < count - 1))(lambda j=j: right(j).wait_send())
        pl.when((z + j <= count - 1) & (z > 0))(lambda j=j: left(j).wait_send())


def gather_tokens(shard):
    count = lax.axis_size("z")
    rows, width = shard.shape
    dma = pltpu.SemaphoreType.DMA
    out = pl.pallas_call(
        functools.partial(gather_kernel, count),
        out_shape=jax.ShapeDtypeStruct((4 * count, rows, width), shard.dtype),
        in_specs=[pl.BlockSpec(memory_space=pl.ANY)],
        out_specs=pl.BlockSpec(memory_space=pl.ANY),
        scratch_shapes=[dma]
        + [dma((count,))] * 6
        + [dma((2 * count,))] * 2,
        compiler_params=pltpu.CompilerParams(collective_id=0, has_side_effects=True),
    )(shard)
    return out.reshape((-1, width))


def target_at(i, z, count):
    rights, lefts = count - 1 - z, z
    right_first = rights >= lefts
    fewer = jnp.minimum(rights, lefts)
    half = i // 2
    paired = i < 2 * fewer
    longer = jnp.logical_or(jnp.logical_not(paired), i % 2 == 0)
    index = jnp.where(paired, half, i - fewer)
    is_right = longer == right_first
    return jnp.where(i == count - 1, z, jnp.where(is_right, count - 1 - index, index))


def scatter_kernel(
    count, turned, a_ref, b_ref, out_ref, part, core_in, y_in, right_in, left_in,
    core_send, core_recv, y_send, y_recv, right_send, right_recv, left_send, left_recv,
):
    z, y, s = lax.axis_index("z"), lax.axis_index("y"), lax.axis_index("section")
    rows, width = out_ref.shape
    tile = min(width, 512)
    step = 32

    def core(slot):
        return pltpu.make_async_remote_copy(
            src_ref=part.at[slot, 1 - s], dst_ref=core_in.at[slot], send_sem=core_send.at[slot],
            recv_sem=core_recv.at[slot], device_id={"section": 1 - s}, device_id_type=MESH,
        )

    def across(k):
        return pltpu.make_async_remote_copy(
            src_ref=part.at[k * 2 + 1 - y, s], dst_ref=y_in.at[k], send_sem=y_send.at[k],
            recv_sem=y_recv.at[k], device_id={"y": 1 - y}, device_id_type=MESH,
        )

    def right(k):
        return pltpu.make_async_remote_copy(
            src_ref=part.at[k * 2 + y, s], dst_ref=right_in.at[k], send_sem=right_send.at[k],
            recv_sem=right_recv.at[k], device_id={"z": z + 1}, device_id_type=MESH,
        )

    def left(k):
        return pltpu.make_async_remote_copy(
            src_ref=part.at[k * 2 + y, s], dst_ref=left_in.at[k], send_sem=left_send.at[k],
            recv_sem=left_recv.at[k], device_id={"z": z - 1}, device_id_type=MESH,
        )

    def arrived(place, sem):
        pltpu.make_async_copy(place, place, sem).wait()

    def add_into(place, terms):
        @pl.loop(0, rows // step)
        def _(r):
            lines = pl.ds(pl.multiple_of(r * step, step), step)
            total = place[lines, :].astype(F32)
            for term in terms:
                total = total + term[lines, :].astype(F32)
            place[lines, :] = total.astype(place.dtype)

    meet(z, count)

    @pl.loop(0, count + 1)
    def _(i):
        @pl.when(i < count)
        def _():
            k = target_at(i, z, count)
            for turn in range(2):
                slot = k * 2 + (1 - y if turn == 0 else y)
                lines = pl.ds(pl.multiple_of(slot * 2 * rows, 2 * rows), 2 * rows)
                for c in range(0, width, tile):
                    if turned:
                        value = back_dot(a_ref[lines, :], b_ref[c : c + tile, :])
                    else:
                        value = forward_dot(a_ref[lines, :], b_ref[:, c : c + tile])
                    part[slot, :, :, c : c + tile] = value.astype(BF).reshape(2, rows, tile)
                core(slot).start()

        @pl.when(i > 0)
        def _():
            k = target_at(i - 1, z, count)
            slot = k * 2 + 1 - y
            arrived(core_in.at[slot], core_recv.at[slot])
            add_into(part.at[slot, s], [core_in.at[slot]])
            across(k).start()

    @pl.loop(0, count - 1)
    def _(i):
        k = target_at(i, z, count)
        slot = k * 2 + y
        arrived(core_in.at[slot], core_recv.at[slot])
        arrived(y_in.at[k], y_recv.at[k])
        add_into(part.at[slot, s], [core_in.at[slot], y_in.at[k]])

        @pl.when(k > z)
        def _():
            @pl.when(z > 0)
            def _():
                arrived(right_in.at[k], right_recv.at[k])
                add_into(part.at[slot, s], [right_in.at[k]])

            right(k).start()

        @pl.when(k < z)
        def _():
            @pl.when(z < count - 1)
            def _():
                arrived(left_in.at[k], left_recv.at[k])
                add_into(part.at[slot, s], [left_in.at[k]])

            left(k).start()

    slot = z * 2 + y
    arrived(core_in.at[slot], core_recv.at[slot])
    arrived(y_in.at[z], y_recv.at[z])

    @pl.loop(0, rows // step)
    def _(r):
        lines = pl.ds(pl.multiple_of(r * step, step), step)
        total = part[slot, s, lines, :].astype(F32)
        total = total + core_in[slot, lines, :].astype(F32)
        out_ref[lines, :] = total + y_in[z, lines, :].astype(F32)

    def add_out(place):
        @pl.loop(0, rows // step)
        def _(r):
            lines = pl.ds(pl.multiple_of(r * step, step), step)
            out_ref[lines, :] += place[z, lines, :].astype(F32)

    @pl.when(z > 0)
    def _():
        arrived(right_in.at[z], right_recv.at[z])
        add_out(right_in)

    @pl.when(z < count - 1)
    def _():
        arrived(left_in.at[z], left_recv.at[z])
        add_out(left_in)

    @pl.loop(0, count)
    def _(k):
        core(k * 2).wait_send()
        core(k * 2 + 1).wait_send()
        across(k).wait_send()
        pl.when(k > z)(lambda: right(k).wait_send())
        pl.when(k < z)(lambda: left(k).wait_send())


def scatter_columns(a, b, turned):
    count = lax.axis_size("z")
    tokens, width = a.shape[0], b.shape[0 if turned else 1]
    rows = tokens // (4 * count)
    dma = pltpu.SemaphoreType.DMA
    block = (rows, width)
    return pl.pallas_call(
        functools.partial(scatter_kernel, count, turned),
        out_shape=jax.ShapeDtypeStruct(block, F32),
        in_specs=[pl.BlockSpec(memory_space=pltpu.VMEM)] * 2,
        out_specs=pl.BlockSpec(memory_space=pltpu.VMEM),
        scratch_shapes=[
            pltpu.VMEM((2 * count, 2) + block, BF),
            pltpu.VMEM((2 * count,) + block, BF),
            pltpu.VMEM((count,) + block, BF),
            pltpu.VMEM((count,) + block, BF),
            pltpu.VMEM((count,) + block, BF),
            dma((2 * count,)), dma((2 * count,)),
        ]
        + [dma((count,))] * 6,
        compiler_params=pltpu.CompilerParams(
            collective_id=1 + turned, has_side_effects=True, vmem_limit_bytes=56 * 2**20
        ),
    )(a, b)


def scatter_dot(a, b, turned):
    tokens, width = a.shape[0], b.shape[0 if turned else 1]
    pieces = max(1, tokens * width // 2**22)
    size = width // pieces
    parts = [slice(i * size, (i + 1) * size) for i in range(pieces)]
    return jnp.concatenate([scatter_columns(a, b[at] if turned else b[:, at], turned) for at in parts], axis=1)


def total_kernel(
    count, x_ref, out_ref, part, core_in, y_out, y_in, z_out, z_in, done,
    core_send, core_recv, y_send, y_recv, z_send, z_recv, zb_send, zb_recv, yb_send, yb_recv, cb_send, cb_recv,
):
    z, y, s = lax.axis_index("z"), lax.axis_index("y"), lax.axis_index("section")
    lanes = part.shape[4]

    def span(k, y_of, s_of):
        at = ((k * 2 + y_of) * 2 + s_of) * lanes
        return slice(at, at + lanes)

    def remote(src, dst, send, recv, where):
        return pltpu.make_async_remote_copy(
            src_ref=src, dst_ref=dst, send_sem=send, recv_sem=recv, device_id=where, device_id_type=MESH
        )

    barrier = pltpu.get_barrier_semaphore()

    def greet(where):
        pl.semaphore_signal(barrier, inc=1, device_id=where, device_id_type=MESH)

    greet({"y": 1 - y})
    greet({"section": 1 - s})
    for hop in range(1, count):
        greet({"z": lax.rem(z + hop, count)})

    for k in range(count):
        for y_of in range(2):
            for s_of in range(2):
                part[s_of, y_of, k] = x_ref[:, span(k, y_of, s_of)]
    pl.semaphore_wait(barrier, count + 1)

    first = remote(part.at[1 - s], core_in, core_send, core_recv, {"section": 1 - s})
    first.start()
    first.wait_recv()
    for k in range(count):
        y_out[k] = (part[s, 1 - y, k] + core_in[1 - y, k]).astype(BF)
    second = remote(y_out, y_in, y_send, y_recv, {"y": 1 - y})
    second.start()
    for k in range(count):
        part[s, y, k] = part[s, y, k] + core_in[y, k]
    second.wait_recv()
    for k in range(count):
        total = part[s, y, k] + y_in[k].astype(F32)
        part[s, y, k] = total
        z_out[k] = total.astype(BF)

    def third(hop):
        to = lax.rem(z + hop, count)
        return remote(z_out.at[to], z_in.at[hop], z_send.at[hop], z_recv.at[hop], {"z": to})

    for hop in range(1, count):
        third(hop).start()
    total = part[s, y, z]
    for hop in range(1, count):
        third(hop).wait_recv()
        total = total + z_in[hop].astype(F32)
    done[s, y, z] = total.astype(BF)

    def fourth(hop):
        to = lax.rem(z + hop, count)
        return remote(done.at[s, y, z], done.at[s, y, z], zb_send.at[hop], zb_recv.at[hop], {"z": to})

    for hop in range(1, count):
        fourth(hop).start()
    for hop in range(1, count):
        fourth(hop).wait_recv()
    fifth = remote(done.at[s, y], done.at[s, y], yb_send, yb_recv, {"y": 1 - y})
    fifth.start()
    fifth.wait_recv()
    sixth = remote(done.at[s], done.at[s], cb_send, cb_recv, {"section": 1 - s})
    sixth.start()
    sixth.wait_recv()
    for k in range(count):
        for y_of in range(2):
            for s_of in range(2):
                out_ref[:, span(k, y_of, s_of)] = done[s_of, y_of, k]
    first.wait_send()
    second.wait_send()
    for hop in range(1, count):
        third(hop).wait_send()
        fourth(hop).wait_send()
    fifth.wait_send()
    sixth.wait_send()


def sum_columns(x):
    count = lax.axis_size("z")
    rows, tokens = x.shape
    lanes = tokens // (4 * count)
    dma = pltpu.SemaphoreType.DMA
    vmem = pltpu.VMEM
    return pl.pallas_call(
        functools.partial(total_kernel, count),
        out_shape=jax.ShapeDtypeStruct((rows, tokens), BF),
        in_specs=[pl.BlockSpec(memory_space=pltpu.VMEM)],
        out_specs=pl.BlockSpec(memory_space=pltpu.VMEM),
        scratch_shapes=[
            vmem((2, 2, count, rows, lanes), F32),
            vmem((2, count, rows, lanes), F32),
            vmem((count, rows, lanes), BF),
            vmem((count, rows, lanes), BF),
            vmem((count, rows, lanes), BF),
            vmem((count, rows, lanes), BF),
            vmem((2, 2, count, rows, lanes), BF),
            dma, dma, dma, dma, dma((count,)), dma((count,)), dma((count,)), dma((count,)), dma, dma, dma, dma,
        ],
        compiler_params=pltpu.CompilerParams(
            collective_id=3, has_side_effects=True, vmem_limit_bytes=56 * 2**20
        ),
    )(x)


def spread_kernel(count, shard_ref, out_ref, z_send, z_recv, pair_send, pair_recv):
    z, y, x, s = (lax.axis_index(name) for name in ("z", "y", "x", "section"))

    def remote(place, send, recv, where):
        return pltpu.make_async_remote_copy(
            src_ref=place, dst_ref=place, send_sem=send, recv_sem=recv, device_id=where, device_id_type=MESH
        )

    barrier = pltpu.get_barrier_semaphore()
    peers = [{"y": 1 - y}, {"x": 1 - x}, {"section": 1 - s}]
    peers += [{"z": lax.rem(z + hop, count)} for hop in range(1, count)]
    for where in peers:
        pl.semaphore_signal(barrier, inc=1, device_id=where, device_id_type=MESH)
    out_ref[s, x, y, z] = shard_ref[...]
    pl.semaphore_wait(barrier, len(peers))
    along = [
        remote(out_ref.at[s, x, y, z], z_send.at[hop], z_recv.at[hop], {"z": lax.rem(z + hop, count)})
        for hop in range(1, count)
    ]
    steps = [
        remote(out_ref.at[s, x, y], pair_send.at[0], pair_recv.at[0], {"y": 1 - y}),
        remote(out_ref.at[s, x], pair_send.at[1], pair_recv.at[1], {"x": 1 - x}),
        remote(out_ref.at[s], pair_send.at[2], pair_recv.at[2], {"section": 1 - s}),
    ]
    for copy in along:
        copy.start()
    for copy in along:
        copy.wait_recv()
    for copy in steps:
        copy.start()
        copy.wait_recv()
    for copy in along + steps:
        copy.wait_send()


def spread(shard):
    count, width = lax.axis_size("z"), shard.shape[0]
    block = (16, max(width, 128))
    padded = jnp.pad(shard[None, :], ((0, block[0] - 1), (0, block[1] - width)))
    dma = pltpu.SemaphoreType.DMA
    out = pl.pallas_call(
        functools.partial(spread_kernel, count),
        out_shape=jax.ShapeDtypeStruct((2, 2, 2, count) + block, shard.dtype),
        in_specs=[pl.BlockSpec(memory_space=pltpu.VMEM)],
        out_specs=pl.BlockSpec(memory_space=pltpu.VMEM),
        scratch_shapes=[dma((count,)), dma((count,)), dma((3,)), dma((3,))],
        compiler_params=pltpu.CompilerParams(collective_id=4, has_side_effects=True),
    )(padded)
    return jnp.transpose(out[:, :, :, :, 0, :width], (0, 3, 2, 1, 4)).reshape((2, -1))


def send(value, axes, pairs):
    return lax.ppermute(value, axes, pairs)


def at_home():
    return lax.axis_index("x") == lax.axis_index("section")


def to_home(value):
    return lax.ppermute(value, ("section", "x"), [(1, 0), (2, 3)])


def from_home(value):
    return lax.ppermute(value, ("section", "x"), [(0, 1), (3, 2)])


def own_tokens(pair):
    low = lax.axis_index("x") == 0
    keep = jnp.where(low, pair[0], pair[1])
    return jnp.where(at_home(), keep, from_home(jnp.where(low, pair[1], pair[0])))


def own_block(piece, layer):
    other = 1 - layer
    sent = lax.ppermute(piece, ("section", "x"), [(layer * 2 + other, other * 2 + other)])
    held = jnp.where(lax.axis_index("section") == layer, piece, sent)
    return jnp.where(at_home(), held, from_home(held))


def own_columns(rows, layer):
    count = 2 * lax.axis_size("z")
    depth = rows.shape[0]
    blocks = jnp.transpose(rows.reshape((depth, 2, count, 2, -1)), (3, 2, 0, 1, 4)).reshape((2, count, depth, -1))
    sent = lax.ppermute(blocks[1 - layer], "section", [(layer, 1 - layer)])
    mine = jnp.where(lax.axis_index("section") == layer, blocks[layer], sent)
    mine = lax.all_to_all(mine, ("z", "y"), split_axis=0, concat_axis=0, tiled=True)
    other = swap(mine, "x")
    low = lax.axis_index("x") == 0
    both = jnp.stack([jnp.where(low, mine, other), jnp.where(low, other, mine)], axis=1)
    return both.reshape((2 * count * depth, -1))


def home_rows(grad, layer):
    count = 2 * lax.axis_size("z")
    pieces = grad.reshape((count, 2, -1, grad.shape[1]))
    low = lax.axis_index("x") == 0
    give = jnp.where(low, pieces[:, 1], pieces[:, 0])
    total = jnp.where(low, pieces[:, 0], pieces[:, 1]).astype(F32) + swap(give, "x").astype(F32)
    mine = lax.all_to_all(total.astype(BF), ("z", "y"), split_axis=0, concat_axis=0, tiled=True)
    return mine, lax.ppermute(mine, "section", [(1 - layer, layer)])


def home_block(piece, layer):
    total = piece + to_home(piece.astype(BF)).astype(F32)
    other = 1 - layer
    sent = lax.ppermute(total.astype(BF), ("section", "x"), [(other * 2 + other, layer * 2 + other)])
    return total, sent


def home_tokens(rows, layer):
    got = to_home(rows)
    low = lax.axis_index("x") == 0
    both = jnp.stack([jnp.where(low, rows, got), jnp.where(low, got, rows)])
    other = 1 - layer
    sent = lax.ppermute(both, ("section", "x"), [(other * 2 + other, layer * 2 + other)])
    return jnp.where(at_home(), both, sent)


def silu_slope(v):
    gate = jax.nn.sigmoid(v)
    return gate, gate * (1.0 + v * (1.0 - gate))


def layer_forward(stream, weights, hidden):
    gain, in_weight, conv_weight, conv_bias, xproj_weight, dt_weight, dt_bias, skip, out_weight = weights
    channels = conv_bias.shape[0]
    inverse = lax.rsqrt(jnp.mean(stream * stream, axis=-1, keepdims=True) + norm_eps)
    normed = gather_tokens((stream * inverse * gain[None, :]).astype(BF))
    projected = forward_dot(normed, in_weight).astype(BF)
    inner = projected[:, :channels].astype(F32)
    gate_in = projected[:, channels:].astype(F32)
    tokens = inner.shape[0]
    extended = jnp.concatenate([jnp.zeros((KC - 1, channels), F32), inner], axis=0)
    conv = jnp.broadcast_to(conv_bias[None, :], (tokens, channels))
    for tap in range(KC):
        conv = conv + conv_weight[tap][None, :] * extended[tap : tap + tokens]
    act = jax.nn.silu(conv)
    xproj = sum_columns(back_dot(xproj_weight, act.astype(BF)))
    key_t, query_t = xproj[R : R + N].astype(F32), xproj[R + N :].astype(F32)
    key_norm = jnp.sum(key_t * key_t, axis=0)[:, None]
    write = jax.nn.sigmoid(cross_dot(xproj[:R], dt_weight) + dt_bias[None, :])
    rate = write / (1.0 + write * key_norm)
    recur, before, last = recur_forward(rate, act, key_t, query_t)
    recur = recur + skip[None, :] * act
    gated = (recur * jax.nn.silu(gate_in)).astype(BF)
    if hidden:
        partial = forward_dot(gated, out_weight).astype(BF)
        out = lax.psum_scatter(partial, ("z", "y", "section"), scatter_dimension=0, tiled=True).astype(F32)
    else:
        out = scatter_dot(gated, out_weight, False)
    saved = (stream, inverse, normed, extended, gate_in, conv, act, xproj, key_t, query_t, key_norm, write, rate, recur, gated, before, last)
    return stream + out, saved


def layer_backward(grad_out, grad_low, saved, weights):
    gain, in_weight, conv_weight, conv_bias, xproj_weight, dt_weight, dt_bias, skip, out_weight = weights
    stream, inverse, normed, extended, gate_in, conv, act, xproj, key_t, query_t, key_norm, write, rate, recur, gated, before, last = saved
    tokens = act.shape[0]
    d_out_weight = cross_dot(gated, grad_low)
    d_gated = back_dot(grad_low, out_weight).astype(BF).astype(F32)
    gate, slope = silu_slope(gate_in)
    d_recur = d_gated * (gate_in * gate)
    d_gate_in = d_gated * recur * slope
    d_skip = jnp.sum(d_recur * act, axis=0)
    d_rate, d_act_rec, d_key_t, d_query_t = recur_backward(rate, act, d_recur, key_t, query_t, before, last)
    share = 1.0 / (1.0 + write * key_norm)
    pulled = d_rate * share * share
    d_pre = pulled * write * (1.0 - write)
    d_key_rate = -2.0 * key_t * jnp.sum(pulled * write * write, axis=1)[None, :]
    d_dt_bias = jnp.sum(d_pre, axis=0)
    d_delta = d_pre.astype(BF)
    d_dt_weight = forward_dot(xproj[:R], d_delta)
    d_xproj = jnp.concatenate([back_dot(dt_weight, d_delta), d_key_t + d_key_rate, d_query_t], axis=0)
    d_xproj = sum_columns(d_xproj)
    d_xproj_weight = forward_dot(d_xproj, act.astype(BF))
    d_act = cross_dot(d_xproj, xproj_weight) + skip[None, :] * d_recur + d_act_rec
    d_conv = d_act * silu_slope(conv)[1]
    d_conv_weight = jnp.stack([jnp.sum(d_conv * extended[tap : tap + tokens], axis=0) for tap in range(KC)])
    d_conv_bias = jnp.sum(d_conv, axis=0)
    later = jnp.concatenate([d_conv, jnp.zeros((KC - 1, d_conv.shape[1]), F32)], axis=0)
    d_inner = sum(conv_weight[tap][None, :] * later[KC - 1 - tap : KC - 1 - tap + tokens] for tap in range(KC))
    d_projected = jnp.concatenate([d_inner, d_gate_in], axis=1).astype(BF)
    d_in_weight = cross_dot(normed, d_projected)
    d_normed = scatter_dot(d_projected, in_weight, True)
    scaled = gain[None, :] * d_normed
    mean = jnp.mean(stream * scaled, axis=-1, keepdims=True)
    d_stream = grad_out + inverse * scaled - stream * inverse**3 * mean
    small = jnp.concatenate(
        [d_conv_weight, d_conv_bias[None], d_dt_bias[None], d_skip[None], d_dt_weight, d_xproj_weight],
        axis=0,
    )
    return d_stream, (d_in_weight.astype(BF), small, d_out_weight)


def on_device(
    hidden_in, cotangent, norm_gain, in_weight, conv_weight, conv_bias, xproj_weight, dt_weight, dt_bias, skip_gain, out_weight
):
    small = jnp.concatenate(
        [conv_weight[0], conv_bias, dt_bias, skip_gain, dt_weight[0], jnp.swapaxes(xproj_weight[0], 0, 1)], axis=0
    )
    gains = spread(norm_gain[0]).astype(F32)
    weights = []
    for layer in range(2):
        part = own_block(small, layer)
        part_f = part.astype(F32)
        weights.append(
            (
                gains[layer],
                own_columns(in_weight[0], layer),
                part_f[:KC],
                part_f[KC],
                part[KC + 3 + R :],
                part[KC + 3 : KC + 3 + R],
                part_f[KC + 1],
                part_f[KC + 2],
                own_block(out_weight[0], layer),
            )
        )

    stream = own_tokens(hidden_in).astype(F32)
    grad = own_tokens(cotangent)
    first, saved_first = layer_forward(stream, weights[0], False)
    first = first.astype(BF)
    grad_low, _ = lax.optimization_barrier((grad.astype(BF), saved_first[2]))
    grad_low = lax.all_gather(grad_low, ("z", "y", "section"), axis=0, tiled=True)
    second, saved_second = layer_forward(first.astype(F32), weights[1], True)
    grad_second, grads_second = layer_backward(grad, grad_low, saved_second, weights[1])
    grad_low = grad_second.astype(BF)
    grad_first, grads_first = layer_backward(grad_low.astype(F32), gather_tokens(grad_low), saved_first, weights[0])

    upper = lax.axis_index("section") == 1

    def of_layer(pair):
        return jnp.where(upper, pair[1], pair[0])

    layer_outputs = of_layer((home_tokens(first, 0), home_tokens(second.astype(BF), 1))).astype(F32)
    input_grads = of_layer((home_tokens(grad_first.astype(BF), 0), home_tokens(grad_second.astype(BF), 1))).astype(F32)
    columns = [home_rows(grads[0], layer) for layer, grads in enumerate((grads_first, grads_second))]
    mine, sent = of_layer([c[0] for c in columns]), of_layer([c[1] for c in columns])
    both = jnp.stack([jnp.where(upper, sent, mine), jnp.where(upper, mine, sent)])
    both = both.reshape((2, mine.shape[0], mine.shape[1], 2, -1))
    d_in = jnp.transpose(both, (2, 3, 1, 0, 4)).reshape((mine.shape[1], -1)).astype(F32)
    d_gain = jnp.sum(d_in * in_weight[0].astype(F32), axis=1) / norm_gain[0].astype(F32)

    def block_of(which):
        pieces = [home_block(grads[which], layer) for layer, grads in enumerate((grads_first, grads_second))]
        held, sent = of_layer([p[0] for p in pieces]), of_layer([p[1] for p in pieces])
        return jnp.where(at_home(), held, sent.astype(F32))

    small, d_out = block_of(1), block_of(2)
    return (
        layer_outputs[None],
        input_grads[None],
        d_gain[None],
        d_in[None],
        small[None, :KC],
        small[None, KC],
        jnp.swapaxes(small[KC + 3 + R :], 0, 1)[None],
        small[None, KC + 3 : KC + 3 + R],
        small[None, KC + 1],
        small[None, KC + 2],
        d_out[None],
    )


def solution(mesh):
    sections, seq = mesh.devices.shape
    split = Mesh(mesh.devices.reshape((sections, seq // 4, 2, 2)), ("section", "z", "y", "x"))
    seq = ("z", "y", "x")
    placed = (
        P(None, seq, None),
        P(None, seq, None),
        P("section", seq),
        P("section", seq, None),
        P("section", None, seq),
        P("section", seq),
        P("section", seq, None),
        P("section", None, seq),
        P("section", seq),
        P("section", seq),
        P("section", seq, None),
    )
    return jax.shard_map(
        on_device,
        mesh=split,
        in_specs=placed,
        out_specs=(P("section", None, seq, None), P("section", None, seq, None)) + placed[2:],
        check_vma=False,
    )
```

```python
import functools

import jax
import jax.numpy as jnp
from jax import lax
from jax.experimental import pallas as pl
from jax.experimental.pallas import tpu as pltpu
from jax.sharding import Mesh, PartitionSpec as P


N = 16
R = 128
KC = 4
BLOCK = 128
norm_eps = 1e-05
BF = jnp.bfloat16
F32 = jnp.float32
MESH = pl.DeviceIdType.MESH


def forward_dot(operand, factor):
    return jnp.dot(operand, factor, preferred_element_type=F32)


def cross_dot(operand, factor):
    return lax.dot_general(operand, factor, (((0,), (0,)), ((), ())), preferred_element_type=F32)


def back_dot(operand, factor):
    return lax.dot_general(operand, factor, (((1,), (1,)), ((), ())), preferred_element_type=F32)


def widths(channels):
    wide = min(channels, 128)
    return wide, channels // wide


def sum_rows(pieces):
    row = lax.broadcasted_iota(jnp.int32, pieces[0].shape, 0)
    shift = 1
    while len(pieces) > 1:
        keep = (row & shift) == 0
        pieces = [
            jnp.where(keep, a, b) + pltpu.roll(jnp.where(keep, b, a), shift, 0)
            for a, b in zip(pieces[0::2], pieces[1::2])
        ]
        shift *= 2
    return pieces[0]


def halves(v):
    return v[:8] + v[8:]


def lanes_of(p, wide):
    return slice(p * wide, (p + 1) * wide)


def recur_forward_kernel(rate_ref, act_ref, key_ref, query_ref, out_ref, before_ref, last_ref, memory_ref):
    wide, parts = widths(rate_ref.shape[1])

    @pl.when(pl.program_id(0) == 0)
    def _():
        memory_ref[...] = jnp.zeros_like(memory_ref)

    memory = [memory_ref[:, lanes_of(p, wide)] for p in range(parts)]
    for base in range(0, rate_ref.shape[0], 8):
        rates = rate_ref[base : base + 8, :]
        feeds = rates * act_ref[base : base + 8, :]
        sums = [[] for _ in range(parts)]
        for i in range(8):
            key = jnp.broadcast_to(key_ref[:, base + i : base + i + 1], (N, wide))
            query = jnp.broadcast_to(query_ref[:, base + i : base + i + 1], (N, wide))
            square = key * key
            for p in range(parts):
                lanes = lanes_of(p, wide)
                before_ref[base + i, :, lanes] = memory[p]
                memory[p] = (1.0 - rates[i : i + 1, lanes] * square) * memory[p] + key * feeds[i : i + 1, lanes]
                sums[p].append(halves(memory[p] * query))
        for p in range(parts):
            out_ref[base : base + 8, lanes_of(p, wide)] = sum_rows(sums[p])
    for p in range(parts):
        memory_ref[:, lanes_of(p, wide)] = memory[p]

    @pl.when(pl.program_id(0) == pl.num_programs(0) - 1)
    def _():
        last_ref[...] = memory_ref[...]


def recur_forward(rate, act, key_t, query_t):
    tokens, channels = rate.shape
    rows = pl.BlockSpec((BLOCK, channels), lambda i: (i, 0))
    cols = pl.BlockSpec((N, BLOCK), lambda i: (0, i))
    return pl.pallas_call(
        recur_forward_kernel,
        grid=(tokens // BLOCK,),
        in_specs=[rows, rows, cols, cols],
        out_specs=[
            rows,
            pl.BlockSpec((BLOCK, N, channels), lambda i: (i, 0, 0)),
            pl.BlockSpec((N, channels), lambda i: (0, 0)),
        ],
        out_shape=[
            jax.ShapeDtypeStruct((tokens, channels), F32),
            jax.ShapeDtypeStruct((tokens, N, channels), F32),
            jax.ShapeDtypeStruct((N, channels), F32),
        ],
        scratch_shapes=[pltpu.VMEM((N, channels), F32)],
        compiler_params=pltpu.CompilerParams(
            dimension_semantics=("arbitrary",), vmem_limit_bytes=40 * 2**20
        ),
        cost_estimate=pl.CostEstimate(
            flops=10 * tokens * N * channels, bytes_accessed=4 * tokens * channels * (N + 3), transcendentals=0
        ),
    )(rate, act, key_t, query_t)


def recur_backward_kernel(
    rate_ref, act_ref, grad_ref, key_ref, query_ref, before_ref, last_ref,
    d_rate_ref, d_act_ref, d_key_ref, d_query_ref, lam_ref, memory_ref, key_rows, query_rows,
):
    wide, parts = widths(rate_ref.shape[1])
    block = rate_ref.shape[0]

    @pl.when(pl.program_id(0) == 0)
    def _():
        lam_ref[...] = jnp.zeros_like(lam_ref)
        memory_ref[...] = last_ref[...]

    lam = [lam_ref[:, lanes_of(p, wide)] for p in range(parts)]
    memory = [memory_ref[:, lanes_of(p, wide)] for p in range(parts)]
    for base in reversed(range(0, block, 8)):
        rates = rate_ref[base : base + 8, :]
        acts = act_ref[base : base + 8, :]
        grads = grad_ref[base : base + 8, :]
        d_rates = [[None] * 8 for _ in range(parts)]
        d_acts = [[None] * 8 for _ in range(parts)]
        for i in reversed(range(8)):
            at = base + i
            key = jnp.broadcast_to(key_ref[:, at : at + 1], (N, wide))
            query = jnp.broadcast_to(query_ref[:, at : at + 1], (N, wide))
            square = key * key
            key_sum = query_sum = None
            for p in range(parts):
                lanes = lanes_of(p, wide)
                grad = grads[i : i + 1, lanes]
                before = before_ref[at, :, lanes]
                pulled = query * grad + lam[p]
                kept = key * before
                missing = acts[i : i + 1, lanes] - kept
                keyed = pulled * key
                scaled = pulled * rates[i : i + 1, lanes]
                d_acts[p][i] = halves(keyed)
                d_rates[p][i] = halves(keyed * missing)
                to_key = scaled * (missing - kept)
                to_query = memory[p] * grad
                key_sum = to_key if key_sum is None else key_sum + to_key
                query_sum = to_query if query_sum is None else query_sum + to_query
                lam[p] = pulled - scaled * square
                memory[p] = before
            key_rows[at * N : (at + 1) * N, :] = key_sum.astype(BF)
            query_rows[at * N : (at + 1) * N, :] = query_sum.astype(BF)
        for p in range(parts):
            lanes = lanes_of(p, wide)
            d_rate_ref[base : base + 8, lanes] = sum_rows(d_rates[p])
            d_act_ref[base : base + 8, lanes] = rates[:, lanes] * sum_rows(d_acts[p])
    for p in range(parts):
        lam_ref[:, lanes_of(p, wide)] = lam[p]
        memory_ref[:, lanes_of(p, wide)] = memory[p]

    ones = jnp.ones((wide, block), BF)
    token = lax.broadcasted_iota(jnp.int32, (block, N, block), 0)
    own = token == lax.broadcasted_iota(jnp.int32, (block, N, block), 2)
    for rows, result in ((key_rows, d_key_ref), (query_rows, d_query_ref)):
        sums = forward_dot(rows[...], ones).reshape(block, N, block)
        result[...] = jnp.sum(jnp.where(own, sums, 0.0), axis=0)


def recur_backward(rate, act, grad, key_t, query_t, before, last):
    tokens, channels = rate.shape
    count = tokens // BLOCK
    rows = pl.BlockSpec((BLOCK, channels), lambda i: (count - 1 - i, 0))
    cols = pl.BlockSpec((N, BLOCK), lambda i: (0, count - 1 - i))
    products = pltpu.VMEM((BLOCK * N, widths(channels)[0]), BF)
    return pl.pallas_call(
        recur_backward_kernel,
        grid=(count,),
        in_specs=[
            rows, rows, rows, cols, cols,
            pl.BlockSpec((BLOCK, N, channels), lambda i: (count - 1 - i, 0, 0)),
            pl.BlockSpec((N, channels), lambda i: (0, 0)),
        ],
        out_specs=[rows, rows, cols, cols],
        out_shape=[
            jax.ShapeDtypeStruct((tokens, channels), F32),
            jax.ShapeDtypeStruct((tokens, channels), F32),
            jax.ShapeDtypeStruct((N, tokens), F32),
            jax.ShapeDtypeStruct((N, tokens), F32),
        ],
        scratch_shapes=[pltpu.VMEM((N, channels), F32), pltpu.VMEM((N, channels), F32), products, products],
        compiler_params=pltpu.CompilerParams(
            dimension_semantics=("arbitrary",), vmem_limit_bytes=40 * 2**20
        ),
        cost_estimate=pl.CostEstimate(
            flops=30 * tokens * N * channels, bytes_accessed=4 * tokens * channels * (N + 5), transcendentals=0
        ),
    )(rate, act, grad, key_t, query_t, before, last)


class Place:
    def __init__(self, bits):
        self.bits = bits
        self.n = len(bits)
        self.count = 2**self.n
        self.at = [lax.axis_index(name) for name in bits]
        self.s = lax.axis_index("section")

    def other(self, e):
        return sum(2**d * (c + e // 2**d % 2 * (1 - 2 * c)) for d, c in enumerate(self.at))

    def toward(self, e):
        return {self.bits[d]: 1 - self.at[d] for d in range(self.n) if e // 2**d % 2}

    def dims(self, p, m):
        return sum(2 ** ((p + t) % self.n) for t in range(self.n) if m // 2**t % 2)

    def positions(self, p, e):
        return sum(2**t * (e // 2 ** ((p + t) % self.n) % 2) for t in range(self.n))

    def meet(self, peers):
        barrier = pltpu.get_barrier_semaphore()
        for where in peers:
            pl.semaphore_signal(barrier, inc=1, device_id=where, device_id_type=MESH)
        pl.semaphore_wait(barrier, len(peers))


def spans_of(width, n):
    tiles = width // 128
    sizes = [(tiles // n + (p < tiles % n)) * 128 for p in range(n)]
    return [(sum(sizes[:p]), size) for p, size in enumerate(sizes)]


def remote(src, dst, send, recv, where):
    return pltpu.make_async_remote_copy(
        src_ref=src, dst_ref=dst, send_sem=send, recv_sem=recv, device_id=where, device_id_type=MESH
    )


def arrived(place, sem):
    pltpu.make_async_copy(place, place, sem).wait()


def lasting(us):
    return pl.CostEstimate(flops=0, bytes_accessed=int(us * 3.4e6), transcendentals=0)


def gather_kernel(bits, total, layer, *refs):
    here = Place(bits)
    n, s, count = here.n, here.s, here.count
    q, chip = lax.axis_index("q"), here.other(0)
    given, refs = refs[: total + (0 if layer is None else 2)], refs[total + (0 if layer is None else 2) :]
    made, refs = refs[: len(given)], refs[len(given) :]
    local_sem, send, recv, core_send, core_recv = refs[:5]
    spans = spans_of(given[0].shape[1], n)
    parts = [(k, p) for k in range(total) for p in range(n) if spans[p][1]]

    def block(k, e, p, s_of):
        return made[k].at[s_of, here.other(e), :, pl.ds(*spans[p])]

    def source(k, e, p):
        return block(k, e, p, s) if e else given[k].at[:, pl.ds(*spans[p])]

    def deliver(k, p, m):
        t = m.bit_length() - 1
        held = here.dims(p, m - 2**t)
        where = here.toward(2 ** ((p + t) % n))
        return remote(source(k, held, p), block(k, held, p, s), send.at[k, p, m], recv.at[k, p, m], where)

    def core(k, p, m):
        held = here.dims(p, m)
        sems = core_send.at[k, p, m], core_recv.at[k, p, m]
        return remote(source(k, held, p), block(k, held, p, s), *sems, {"section": 1 - s})

    if layer is None:
        here.meet([here.toward(2**d) for d in range(n)] + [{"section": 1 - s}])
    else:
        blocks, small = given[total:]
        rows, own_small = made[total:]
        piece_send, piece_recv, q_send, q_recv, small_send, small_recv = refs[5:]
        peers = [dict(here.toward(e), **extra) for e in range(count) for extra in ({}, {"section": 1 - s}) if e or extra]
        here.meet(peers + [{"q": 1 - q}, {"q": 1 - q, "section": 1 - s}])

        def piece(r, e):
            where = dict(here.toward(e), **({"section": 1 - s} if r else {}))
            src = blocks.at[1 - s if r else s, here.other(e)]
            return remote(src, rows.at[q, chip], piece_send.at[r, e], piece_recv.at[e], where)

        def pass_on(e):
            place = rows.at[q, here.other(e)]
            return remote(place, place, q_send.at[e], q_recv.at[e], {"q": 1 - q})

        def hand_small(k, where):
            return remote(small, own_small, small_send.at[k], small_recv, where)

        keep_piece = pltpu.make_async_copy(blocks.at[s, chip], rows.at[q, chip], piece_recv.at[0])
        keep_small = pltpu.make_async_copy(small, own_small, small_recv)
        at_layer = s == layer
        stays, leaves = jnp.logical_and(at_layer, q == s), jnp.logical_and(at_layer, q != s)

        @pl.when(at_layer)
        def _():
            keep_piece.start()
            for e in range(count):
                for r in range(2):
                    if e or r:
                        piece(r, e).start()

        @pl.when(stays)
        def _():
            keep_small.start()
            hand_small(0, {"q": 1 - q}).start()

        @pl.when(leaves)
        def _():
            hand_small(0, {"section": 1 - s}).start()
            hand_small(1, {"section": 1 - s, "q": 1 - q}).start()

    own = [pltpu.make_async_copy(given[k], made[k].at[s, chip], local_sem.at[k]) for k in range(total)]
    for k in range(total):
        for t in range(n):
            for p in range(n):
                if spans[p][1]:
                    deliver(k, p, 2**t).start()
        own[k].start()
    for k, p in parts:
        core(k, p, 0).start()
    for m in range(1, count):
        if layer is not None:
            for e in range(count * (m - 1) // (count - 1), count * m // (count - 1)):
                arrived(rows.at[q, here.other(e)], piece_recv.at[e])
                pass_on(e).start()
        for k, p in parts:
            arrived(block(k, here.dims(p, m), p, s), recv.at[k, p, m])
            for t in range(m.bit_length(), n):
                deliver(k, p, m + 2**t).start()
            core(k, p, m).start()
    for copy in own:
        copy.wait()
    for m in range(count):
        for k, p in parts:
            arrived(block(k, here.dims(p, m), p, 1 - s), core_recv.at[k, p, m])
    for m in range(count):
        for k, p in parts:
            core(k, p, m).wait_send()
            if m:
                deliver(k, p, m).wait_send()
    if layer is not None:
        arrived(own_small, small_recv)
        for e in range(count):
            arrived(rows.at[1 - q, here.other(e)], q_recv.at[e])
            pass_on(e).wait_send()

        @pl.when(at_layer)
        def _():
            for e in range(count):
                for r in range(2):
                    if e or r:
                        piece(r, e).wait_send()

        pl.when(stays)(lambda: hand_small(0, {"q": 1 - q}).wait_send())

        @pl.when(leaves)
        def _():
            hand_small(0, {"section": 1 - s}).wait_send()
            hand_small(1, {"section": 1 - s, "q": 1 - q}).wait_send()


def gather_call(bits, shards, layer=None, extras=(), us=35):
    rows, width = shards[0].shape
    n = len(bits)
    count = 2**n
    dma = pltpu.SemaphoreType.DMA
    sems = dma((len(shards), n, count))
    shapes = [jax.ShapeDtypeStruct((2, count, rows, width), shard.dtype) for shard in shards]
    scratch = [dma((len(shards),)), sems, sems, sems, sems]
    if layer is not None:
        shapes += [jax.ShapeDtypeStruct(extra.shape, extra.dtype) for extra in extras]
        scratch += [dma((2, count)), dma((count,)), dma((count,)), dma((count,)), dma((2,)), dma]
    out = pl.pallas_call(
        functools.partial(gather_kernel, bits, len(shards), layer),
        out_shape=shapes,
        in_specs=[pl.BlockSpec(memory_space=pl.ANY)] * len(shapes),
        out_specs=[pl.BlockSpec(memory_space=pl.ANY)] * len(shapes),
        scratch_shapes=scratch,
        compiler_params=pltpu.CompilerParams(
            collective_id=0 if layer is None else 5, has_side_effects=True
        ),
        cost_estimate=lasting(us),
    )(*shards, *extras)
    return [o.reshape((-1, width)) for o in out[: len(shards)]] + list(out[len(shards) :])


def gather_tokens(bits, shard):
    return gather_call(bits, [shard])[0]


def add_rows(place, terms, out=None):
    step = 32
    out = place if out is None else out

    @pl.loop(0, place.shape[0] // step)
    def _(r):
        lines = pl.ds(pl.multiple_of(r * step, step), step)
        total = place[lines, :].astype(F32)
        for term in terms:
            total = total + term[lines, :].astype(F32)
        out[lines, :] = total.astype(out.dtype)


def scatter_kernel(bits, turned, homing, a_ref, b_ref, *refs):
    if homing:
        grad, out_ref, home, other_home = refs[:4]
        q_in, ready, q_send, q_recv, home_send, home_recv, over_send, over_recv = refs[-8:]
        refs = refs[4:]
    else:
        out_ref, refs = refs[0], refs[1:]
    mine, give, core_in, landed, core_send, core_recv, send, recv = refs[:8]
    here = Place(bits)
    n, s, count = here.n, here.s, here.count
    rows, width = out_ref.shape
    tile = min(width, 512)
    spans = spans_of(width, n)
    parts = [p for p in range(n) if spans[p][1]]

    def core(chip):
        return remote(give.at[chip], core_in.at[chip], core_send.at[chip], core_recv.at[chip], {"section": 1 - s})

    def hand(p, m, t):
        e = here.dims(p, m) if isinstance(m, int) else sum(
            2 ** ((p + u) % n) * (m // 2**u % 2) for u in range(n)
        )
        cols = pl.ds(*spans[p])
        return remote(
            mine.at[here.other(e), :, cols], landed.at[m, :, cols], send.at[p, m], recv.at[p, m],
            here.toward(2 ** ((p + t) % n)),
        )

    def to_q(e):
        q, chip = lax.axis_index("q"), here.other(e)
        return remote(grad.at[1 - q, chip], q_in.at[chip], q_send.at[e], q_recv.at[e], {"q": 1 - q})

    def to_chip(e):
        return remote(ready.at[here.other(e)], home.at[here.other(0)], home_send.at[e], home_recv.at[e], here.toward(e))

    def to_core(e):
        chip = here.other(e)
        return remote(home.at[chip], other_home.at[chip], over_send.at[e], over_recv.at[e], {"section": 1 - s})

    def home_step(e):
        chip = here.other(e)
        arrived(q_in.at[chip], q_recv.at[e])
        place = ready.at[chip] if e else home.at[chip]
        add_rows(q_in.at[chip], [grad.at[lax.axis_index("q"), chip]], place)
        (to_chip(e) if e else to_core(0)).start()

    def home_end(e):
        if e:
            arrived(home.at[here.other(e)], home_recv.at[e])
            to_core(e).start()

    peers = [here.toward(2**d) for d in range(n)] + [{"section": 1 - s}]
    if homing:
        peers = [here.toward(e) for e in range(1, count)] + [{"section": 1 - s}, {"q": 1 - lax.axis_index("q")}]
    here.meet(peers)
    if homing:
        for e in range(count):
            to_q(e).start()

    @pl.loop(0, count + 1)
    def _(i):
        @pl.when(i < count)
        def _():
            chip = here.other(count - 1 - i)

            def lines(s_of):
                return pl.ds(pl.multiple_of((s_of * count + chip) * rows, rows), rows)

            left = jnp.concatenate([a_ref[lines(1 - s), :], a_ref[lines(s), :]], axis=0)
            for c in range(0, width, tile):
                if turned:
                    value = back_dot(left, b_ref[c : c + tile, :])
                else:
                    value = forward_dot(left, b_ref[:, c : c + tile])
                value = value.astype(BF)
                give[chip, :, c : c + tile] = value[:rows]
                mine[chip, :, c : c + tile] = value[rows:]
            core(chip).start()

        @pl.when(i > 0)
        def _():
            e = count - i
            chip = here.other(e)
            arrived(core_in.at[chip], core_recv.at[chip])
            add_rows(mine.at[chip], [core_in.at[chip]])
            for p in parts:
                pl.when(e // 2 ** ((p + n - 1) % n) % 2 == 1)(
                    lambda p=p: hand(p, here.positions(p, e), n - 1).start()
                )

    def waiting(p, m):
        cols = pl.ds(*spans[p])
        terms = [m + 2**t for t in range(m.bit_length(), n)]
        for term in terms:
            arrived(landed.at[term, :, cols], recv.at[p, term])
        return mine.at[here.other(here.dims(p, m)), :, cols], [landed.at[term, :, cols] for term in terms]

    steps = count // 2
    for m in range(steps - 1, 0, -1):
        if homing:
            home_step(steps - 1 - m)
        for p in parts:
            add_rows(*waiting(p, m))
            hand(p, m, m.bit_length() - 1).start()
    for p in parts:
        place, terms = waiting(p, 0)
        add_rows(place, terms, out_ref.at[:, pl.ds(*spans[p])])
    if homing:
        for e in range(steps - 1, count):
            home_step(e)
        for e in range(count):
            home_end(e)
        for e in range(count):
            arrived(other_home.at[here.other(e)], over_recv.at[e])
            to_core(e).wait_send()
            to_q(e).wait_send()
            if e:
                to_chip(e).wait_send()
    for chip in range(count):
        core(chip).wait_send()
    for m in range(1, count):
        for p in parts:
            hand(p, m, m.bit_length() - 1).wait_send()


def scatter_columns(bits, a, b, turned, grad=None):
    tokens, width = a.shape[0], b.shape[0 if turned else 1]
    n = len(bits)
    count = 2**n
    block = (tokens // (2 * count), width)
    dma = pltpu.SemaphoreType.DMA
    blocks = pltpu.VMEM((count,) + block, BF)
    shapes = [jax.ShapeDtypeStruct(block, F32)]
    scratch = [blocks] * 4 + [dma((count,))] * 2 + [dma((n, count))] * 2
    if grad is not None:
        shapes += [jax.ShapeDtypeStruct(grad.shape[1:], BF)] * 2
        scratch += [pltpu.VMEM(grad.shape[1:], BF)] * 2 + [dma((count,))] * 6
    return pl.pallas_call(
        functools.partial(scatter_kernel, bits, turned, grad is not None),
        out_shape=shapes,
        in_specs=[pl.BlockSpec(memory_space=pltpu.VMEM)] * (2 if grad is None else 3),
        out_specs=[pl.BlockSpec(memory_space=pltpu.VMEM)] * len(shapes),
        scratch_shapes=scratch,
        compiler_params=pltpu.CompilerParams(
            collective_id=(1 + turned) if grad is None else 6, has_side_effects=True, vmem_limit_bytes=56 * 2**20
        ),
        cost_estimate=lasting(40 if grad is None else 60),
    )(*((a, b) if grad is None else (a, b, grad)))


def scatter_dot(bits, a, b, turned, grad=None):
    tokens, width = a.shape[0], b.shape[0 if turned else 1]
    pieces = max(1, tokens * width // 2**22)
    size = width // pieces
    cuts = [slice(i * size, (i + 1) * size) for i in range(pieces)]
    done = [
        scatter_columns(bits, a, b[at] if turned else b[:, at], turned, grad if i == 0 else None)
        for i, at in enumerate(cuts)
    ]
    total = jnp.concatenate([d[0] for d in done], axis=1)
    return total if grad is None else (total, done[0][1], done[0][2])


def total_kernel(bits, x_ref, out_ref, part, core_in, ready, landed, done, pair_send, pair_recv, send, recv, back_send, back_recv):
    here = Place(bits)
    s, count = here.s, here.count
    lanes = part.shape[3]

    def span(s_of, chip):
        at = (s_of * count + chip) * lanes
        return slice(at, at + lanes)

    for s_of in range(2):
        for chip in range(count):
            part[s_of, chip] = x_ref[:, span(s_of, chip)]
    here.meet([here.toward(e) for e in range(1, count)] + [{"section": 1 - s}])
    first = remote(part.at[1 - s], core_in, pair_send.at[0], pair_recv.at[0], {"section": 1 - s})
    first.start()
    first.wait_recv()
    for chip in range(count):
        total = part[s, chip] + core_in[chip]
        part[s, chip] = total
        ready[chip] = total.astype(BF)

    def out(e):
        return remote(ready.at[here.other(e)], landed.at[e], send.at[e], recv.at[e], here.toward(e))

    def back(e):
        place = done.at[s, here.other(0)]
        return remote(place, place, back_send.at[e], back_recv.at[e], here.toward(e))

    others = range(1, count)
    for e in others:
        out(e).start()
    total = part[s, here.other(0)]
    for e in others:
        out(e).wait_recv()
        total = total + landed[e].astype(F32)
    done[s, here.other(0)] = total.astype(BF)
    for e in others:
        back(e).start()
    for e in others:
        place = done.at[s, here.other(e)]
        arrived(place, back_recv.at[e])
    last = remote(done.at[s], done.at[s], pair_send.at[1], pair_recv.at[1], {"section": 1 - s})
    last.start()
    last.wait_recv()
    for s_of in range(2):
        for chip in range(count):
            out_ref[:, span(s_of, chip)] = done[s_of, chip]
    first.wait_send()
    last.wait_send()
    for e in others:
        out(e).wait_send()
        back(e).wait_send()


def sum_columns(bits, x):
    rows, tokens = x.shape
    count = 2 ** len(bits)
    block = (rows, tokens // (2 * count))
    dma, vmem = pltpu.SemaphoreType.DMA, pltpu.VMEM
    return pl.pallas_call(
        functools.partial(total_kernel, bits),
        out_shape=jax.ShapeDtypeStruct((rows, tokens), BF),
        in_specs=[pl.BlockSpec(memory_space=pltpu.VMEM)],
        out_specs=pl.BlockSpec(memory_space=pltpu.VMEM),
        scratch_shapes=[
            vmem((2, count) + block, F32),
            vmem((count,) + block, F32),
            vmem((count,) + block, BF),
            vmem((count,) + block, BF),
            vmem((2, count) + block, BF),
        ]
        + [dma((2,))] * 2
        + [dma((count,))] * 4,
        compiler_params=pltpu.CompilerParams(
            collective_id=3, has_side_effects=True, vmem_limit_bytes=56 * 2**20
        ),
        cost_estimate=lasting(22),
    )(x)


def spread_kernel(bits, shard_ref, out_ref, send, recv, pair_send, pair_recv):
    here = Place(bits)
    s, q, chip = here.s, lax.axis_index("q"), here.other(0)
    others = range(1, here.count)
    here.meet([here.toward(e) for e in others] + [{"section": 1 - s}, {"q": 1 - q}])
    out_ref[s, q, chip] = shard_ref[...]
    own = out_ref.at[s, q, chip]
    copies = [remote(own, own, send.at[e], recv.at[e], here.toward(e)) for e in others]
    for copy in copies:
        copy.start()
    for e in others:
        arrived(out_ref.at[s, q, here.other(e)], recv.at[e])
    place = out_ref.at[s, q]
    first = remote(place, place, pair_send.at[0], pair_recv.at[0], {"q": 1 - q})
    first.start()
    first.wait_recv()
    place = out_ref.at[s]
    second = remote(place, place, pair_send.at[1], pair_recv.at[1], {"section": 1 - s})
    second.start()
    second.wait_recv()
    for copy in copies + [first, second]:
        copy.wait_send()


def spread(bits, shard):
    width, count = shard.shape[0], 2 ** len(bits)
    block = (16, max(width, 128))
    padded = jnp.pad(shard[None, :], ((0, block[0] - 1), (0, block[1] - width)))
    dma = pltpu.SemaphoreType.DMA
    out = pl.pallas_call(
        functools.partial(spread_kernel, bits),
        out_shape=jax.ShapeDtypeStruct((2, 2, count) + block, shard.dtype),
        in_specs=[pl.BlockSpec(memory_space=pltpu.VMEM)],
        out_specs=pl.BlockSpec(memory_space=pltpu.VMEM),
        scratch_shapes=[dma((count,)), dma((count,)), dma((2,)), dma((2,))],
        compiler_params=pltpu.CompilerParams(collective_id=4, has_side_effects=True),
        cost_estimate=lasting(12),
    )(padded)
    return out[:, :, :, 0, :width].reshape((2, -1))


def chips(bits):
    return tuple(reversed(bits))


def swap(value, axis):
    return lax.ppermute(value, axis, [(0, 1), (1, 0)])


def at_home():
    return lax.axis_index("q") == lax.axis_index("section")


def to_home(value):
    return lax.ppermute(value, ("section", "q"), [(1, 0), (2, 3)])


def from_home(value):
    return lax.ppermute(value, ("section", "q"), [(0, 1), (3, 2)])


def own_tokens(pair):
    low = lax.axis_index("q") == 0
    keep = jnp.where(low, pair[0], pair[1])
    return jnp.where(at_home(), keep, from_home(jnp.where(low, pair[1], pair[0])))


def own_block(piece, layer):
    other = 1 - layer
    sent = lax.ppermute(piece, ("section", "q"), [(layer * 2 + other, other * 2 + other)])
    held = jnp.where(lax.axis_index("section") == layer, piece, sent)
    return jnp.where(at_home(), held, from_home(held))


def column_blocks(bits, rows):
    depth = rows.shape[0]
    blocks = jnp.transpose(rows.reshape((depth, 2, 2, 2 ** len(bits), -1)), (2, 3, 0, 1, 4))
    return blocks.reshape((2, 2 ** len(bits), depth, -1))


def own_columns(bits, blocks, layer):
    sent = lax.ppermute(blocks[1 - layer], "section", [(layer, 1 - layer)])
    mine = jnp.where(lax.axis_index("section") == layer, blocks[layer], sent)
    mine = lax.all_to_all(mine, chips(bits), split_axis=0, concat_axis=0, tiled=True)
    other = swap(mine, "q")
    low = lax.axis_index("q") == 0
    both = jnp.stack([jnp.where(low, mine, other), jnp.where(low, other, mine)])
    return both.reshape((-1, blocks.shape[3]))


def home_rows(bits, grad, layer):
    pieces = grad.reshape((2, 2 ** len(bits), -1, grad.shape[1]))
    low = lax.axis_index("q") == 0
    give = jnp.where(low, pieces[1], pieces[0])
    total = jnp.where(low, pieces[0], pieces[1]).astype(F32) + swap(give, "q").astype(F32)
    mine = lax.all_to_all(total.astype(BF), chips(bits), split_axis=0, concat_axis=0, tiled=True)
    return mine, lax.ppermute(mine, "section", [(1 - layer, layer)])


def home_block(piece, layer):
    total = piece + to_home(piece.astype(BF)).astype(F32)
    other = 1 - layer
    sent = lax.ppermute(total.astype(BF), ("section", "q"), [(other * 2 + other, layer * 2 + other)])
    return total, sent


def home_tokens(rows, layer):
    got = to_home(rows)
    low = lax.axis_index("q") == 0
    both = jnp.stack([jnp.where(low, rows, got), jnp.where(low, got, rows)])
    other = 1 - layer
    sent = lax.ppermute(both, ("section", "q"), [(other * 2 + other, layer * 2 + other)])
    return jnp.where(at_home(), both, sent)


def silu_slope(v):
    gate = jax.nn.sigmoid(v)
    return gate, gate * (1.0 + v * (1.0 - gate))


def normalize(stream, gain):
    inverse = lax.rsqrt(jnp.mean(stream * stream, axis=-1, keepdims=True) + norm_eps)
    return inverse, (stream * inverse * gain[None, :]).astype(BF)


def layer_forward(bits, stream, inverse, normed, weights):
    gain, in_weight, conv_weight, conv_bias, xproj_weight, dt_weight, dt_bias, skip, out_weight = weights
    channels = conv_bias.shape[0]
    projected = forward_dot(normed, in_weight).astype(BF)
    inner = projected[:, :channels].astype(F32)
    gate_in = projected[:, channels:].astype(F32)
    tokens = inner.shape[0]
    extended = jnp.concatenate([jnp.zeros((KC - 1, channels), F32), inner], axis=0)
    conv = jnp.broadcast_to(conv_bias[None, :], (tokens, channels))
    for tap in range(KC):
        conv = conv + conv_weight[tap][None, :] * extended[tap : tap + tokens]
    act = jax.nn.silu(conv)
    xproj = sum_columns(bits, back_dot(xproj_weight, act.astype(BF)))
    key_t, query_t = xproj[R : R + N].astype(F32), xproj[R + N :].astype(F32)
    key_norm = jnp.sum(key_t * key_t, axis=0)[:, None]
    write = jax.nn.sigmoid(cross_dot(xproj[:R], dt_weight) + dt_bias[None, :])
    rate = write / (1.0 + write * key_norm)
    recur, before, last = recur_forward(rate, act, key_t, query_t)
    recur = recur + skip[None, :] * act
    gated = (recur * jax.nn.silu(gate_in)).astype(BF)
    out = scatter_dot(bits, gated, out_weight, False)
    saved = (stream, inverse, normed, extended, gate_in, conv, act, xproj, key_t, query_t, key_norm, write, rate, recur, gated, before, last)
    return stream + out, saved


def layer_backward(bits, grad_out, grad_low, saved, weights, homing):
    gain, in_weight, conv_weight, conv_bias, xproj_weight, dt_weight, dt_bias, skip, out_weight = weights
    stream, inverse, normed, extended, gate_in, conv, act, xproj, key_t, query_t, key_norm, write, rate, recur, gated, before, last = saved
    tokens = act.shape[0]
    d_out_weight = cross_dot(gated, grad_low)
    d_gated = back_dot(grad_low, out_weight).astype(BF).astype(F32)
    gate, slope = silu_slope(gate_in)
    d_recur = d_gated * (gate_in * gate)
    d_gate_in = d_gated * recur * slope
    d_skip = jnp.sum(d_recur * act, axis=0)
    d_rate, d_act_rec, d_key_t, d_query_t = recur_backward(rate, act, d_recur, key_t, query_t, before, last)
    share = 1.0 / (1.0 + write * key_norm)
    pulled = d_rate * share * share
    d_pre = pulled * write * (1.0 - write)
    d_key_rate = -2.0 * key_t * jnp.sum(pulled * write * write, axis=1)[None, :]
    d_dt_bias = jnp.sum(d_pre, axis=0)
    d_delta = d_pre.astype(BF)
    d_dt_weight = forward_dot(xproj[:R], d_delta)
    d_xproj = jnp.concatenate([back_dot(dt_weight, d_delta), d_key_t + d_key_rate, d_query_t], axis=0)
    d_xproj = sum_columns(bits, d_xproj)
    d_xproj_weight = forward_dot(d_xproj, act.astype(BF))
    d_act = cross_dot(d_xproj, xproj_weight) + skip[None, :] * d_recur + d_act_rec
    d_conv = d_act * silu_slope(conv)[1]
    d_conv_weight = jnp.stack([jnp.sum(d_conv * extended[tap : tap + tokens], axis=0) for tap in range(KC)])
    d_conv_bias = jnp.sum(d_conv, axis=0)
    later = jnp.concatenate([d_conv, jnp.zeros((KC - 1, d_conv.shape[1]), F32)], axis=0)
    d_inner = sum(conv_weight[tap][None, :] * later[KC - 1 - tap : KC - 1 - tap + tokens] for tap in range(KC))
    d_projected = jnp.concatenate([d_inner, d_gate_in], axis=1).astype(BF)
    d_in_weight = cross_dot(normed, d_projected).astype(BF)
    if homing:
        pieces = d_in_weight.reshape((2, 2 ** len(bits), -1, d_in_weight.shape[1]))
        d_normed, *d_in_weight = scatter_dot(bits, d_projected, in_weight, True, pieces)
    else:
        d_normed = scatter_dot(bits, d_projected, in_weight, True)
    scaled = gain[None, :] * d_normed
    mean = jnp.mean(stream * scaled, axis=-1, keepdims=True)
    d_stream = grad_out + inverse * scaled - stream * inverse**3 * mean
    small = jnp.concatenate(
        [d_conv_weight, d_conv_bias[None], d_dt_bias[None], d_skip[None], d_dt_weight, d_xproj_weight],
        axis=0,
    )
    return d_stream, (d_in_weight, small, d_out_weight)


def on_device(
    bits, hidden_in, cotangent, norm_gain, in_weight, conv_weight, conv_bias, xproj_weight, dt_weight, dt_bias, skip_gain, out_weight
):
    small = jnp.concatenate(
        [conv_weight[0], conv_bias, dt_bias, skip_gain, dt_weight[0], jnp.swapaxes(xproj_weight[0], 0, 1)], axis=0
    )
    small = jnp.pad(small, ((0, -small.shape[0] % 16), (0, 0)))
    blocks = column_blocks(bits, in_weight[0])
    stream = own_tokens(hidden_in).astype(F32)
    grad = own_tokens(cotangent)
    gains = spread(bits, norm_gain[0]).astype(F32)
    inverse, normed = normalize(stream, gains[0])
    normed, grad_low, columns, own_small = gather_call(
        bits, [normed, grad.astype(BF)], 0, (blocks, small), us=70
    )
    own_small, blocks, small, out_block = lax.optimization_barrier((own_small, blocks, small, out_weight[0]))
    weights = []
    for layer in range(2):
        part = own_small if layer == 0 else own_block(small, layer)
        part_f = part.astype(F32)
        weights.append(
            (
                gains[layer],
                columns.reshape((-1, columns.shape[3])) if layer == 0 else own_columns(bits, blocks, layer),
                part_f[:KC],
                part_f[KC],
                part[KC + 3 + R : KC + 3 + 2 * R + 2 * N],
                part[KC + 3 : KC + 3 + R],
                part_f[KC + 1],
                part_f[KC + 2],
                own_block(out_block, layer),
            )
        )

    first, saved_first = layer_forward(bits, stream, inverse, normed, weights[0])
    first = first.astype(BF)
    stream = first.astype(F32)
    inverse, normed = normalize(stream, gains[1])
    second, saved_second = layer_forward(bits, stream, inverse, gather_tokens(bits, normed), weights[1])
    grad_second, grads_second = layer_backward(bits, grad, grad_low, saved_second, weights[1], False)
    grad_low = grad_second.astype(BF)
    grad_first, grads_first = layer_backward(
        bits, grad_low.astype(F32), gather_tokens(bits, grad_low), saved_first, weights[0], True
    )

    upper = lax.axis_index("section") == 1

    def of_layer(pair):
        return jnp.where(upper, pair[1], pair[0])

    layer_outputs = of_layer((home_tokens(first, 0), home_tokens(second.astype(BF), 1))).astype(F32)
    input_grads = of_layer((home_tokens(grad_first.astype(BF), 0), home_tokens(grad_second.astype(BF), 1))).astype(F32)
    columns = [grads_first[0], home_rows(bits, grads_second[0], 1)]
    mine, sent = of_layer([c[0] for c in columns]), of_layer([c[1] for c in columns])
    both = jnp.stack([jnp.where(upper, sent, mine), jnp.where(upper, mine, sent)])
    both = both.reshape((2, mine.shape[0], mine.shape[1], 2, -1))
    d_in = jnp.transpose(both, (2, 3, 0, 1, 4)).reshape((mine.shape[1], -1)).astype(F32)
    d_gain = jnp.sum(d_in * in_weight[0].astype(F32), axis=1) / norm_gain[0].astype(F32)

    def block_of(which):
        pieces = [home_block(grads[which], layer) for layer, grads in enumerate((grads_first, grads_second))]
        held, sent = of_layer([p[0] for p in pieces]), of_layer([p[1] for p in pieces])
        return jnp.where(at_home(), held, sent.astype(F32))

    small, d_out = block_of(1), block_of(2)
    return (
        layer_outputs[None],
        input_grads[None],
        d_gain[None],
        d_in[None],
        small[None, :KC],
        small[None, KC],
        jnp.swapaxes(small[KC + 3 + R :], 0, 1)[None],
        small[None, KC + 3 : KC + 3 + R],
        small[None, KC + 1],
        small[None, KC + 2],
        d_out[None],
    )


def solution(mesh):
    sections, chip_count = mesh.devices.shape
    n = chip_count.bit_length() - 2
    bits = tuple("c%d" % d for d in range(n))
    split = Mesh(mesh.devices.reshape((sections,) + (2,) * (n + 1)), ("section", "q") + chips(bits))
    seq = ("q",) + chips(bits)
    placed = (
        P(None, seq, None),
        P(None, seq, None),
        P("section", seq),
        P("section", seq, None),
        P("section", None, seq),
        P("section", seq),
        P("section", seq, None),
        P("section", None, seq),
        P("section", seq),
        P("section", seq),
        P("section", seq, None),
    )
    return jax.shard_map(
        functools.partial(on_device, bits),
        mesh=split,
        in_specs=placed,
        out_specs=(P("section", None, seq, None), P("section", None, seq, None)) + placed[2:],
        check_vma=False,
    )
```

```python
import functools

import jax
import jax.numpy as jnp
from jax import lax
from jax.experimental import pallas as pl
from jax.experimental.pallas import tpu as pltpu
from jax.sharding import Mesh, PartitionSpec as P


N = 16
R = 128
KC = 4
BLOCK = 128
norm_eps = 1e-05
BF = jnp.bfloat16
F32 = jnp.float32
MESH = pl.DeviceIdType.MESH


def forward_dot(operand, factor):
    return jnp.dot(operand, factor, preferred_element_type=F32)


def cross_dot(operand, factor):
    return lax.dot_general(operand, factor, (((0,), (0,)), ((), ())), preferred_element_type=F32)


def back_dot(operand, factor):
    return lax.dot_general(operand, factor, (((1,), (1,)), ((), ())), preferred_element_type=F32)


def lasting(us):
    return pl.CostEstimate(flops=0, bytes_accessed=int(us * 3.4e6), transcendentals=0)


def widths(channels):
    wide = min(channels, 128)
    return wide, channels // wide


def sum_rows(pieces):
    row = lax.broadcasted_iota(jnp.int32, pieces[0].shape, 0)
    shift = 1
    while len(pieces) > 1:
        keep = (row & shift) == 0
        pieces = [
            jnp.where(keep, a, b) + pltpu.roll(jnp.where(keep, b, a), shift, 0)
            for a, b in zip(pieces[0::2], pieces[1::2])
        ]
        shift *= 2
    return pieces[0]


def halves(v):
    return v[:8] + v[8:]


def lanes_of(p, wide):
    return slice(p * wide, (p + 1) * wide)


def recur_forward_kernel(rate_ref, act_ref, key_ref, query_ref, out_ref, before_ref, last_ref, memory_ref):
    wide, parts = widths(rate_ref.shape[1])

    @pl.when(pl.program_id(0) == 0)
    def _():
        memory_ref[...] = jnp.zeros_like(memory_ref)

    memory = [memory_ref[:, lanes_of(p, wide)] for p in range(parts)]
    for base in range(0, rate_ref.shape[0], 8):
        rates = rate_ref[base : base + 8, :]
        feeds = rates * act_ref[base : base + 8, :]
        sums = [[] for _ in range(parts)]
        for i in range(8):
            key = jnp.broadcast_to(key_ref[:, base + i : base + i + 1], (N, wide))
            query = jnp.broadcast_to(query_ref[:, base + i : base + i + 1], (N, wide))
            square = key * key
            for p in range(parts):
                lanes = lanes_of(p, wide)
                before_ref[base + i, :, lanes] = memory[p]
                memory[p] = (1.0 - rates[i : i + 1, lanes] * square) * memory[p] + key * feeds[i : i + 1, lanes]
                sums[p].append(halves(memory[p] * query))
        for p in range(parts):
            out_ref[base : base + 8, lanes_of(p, wide)] = sum_rows(sums[p])
    for p in range(parts):
        memory_ref[:, lanes_of(p, wide)] = memory[p]

    @pl.when(pl.program_id(0) == pl.num_programs(0) - 1)
    def _():
        last_ref[...] = memory_ref[...]


def recur_forward(rate, act, key_t, query_t):
    tokens, channels = rate.shape
    rows = pl.BlockSpec((BLOCK, channels), lambda i: (i, 0))
    cols = pl.BlockSpec((N, BLOCK), lambda i: (0, i))
    return pl.pallas_call(
        recur_forward_kernel,
        grid=(tokens // BLOCK,),
        in_specs=[rows, rows, cols, cols],
        out_specs=[
            rows,
            pl.BlockSpec((BLOCK, N, channels), lambda i: (i, 0, 0)),
            pl.BlockSpec((N, channels), lambda i: (0, 0)),
        ],
        out_shape=[
            jax.ShapeDtypeStruct((tokens, channels), F32),
            jax.ShapeDtypeStruct((tokens, N, channels), F32),
            jax.ShapeDtypeStruct((N, channels), F32),
        ],
        scratch_shapes=[pltpu.VMEM((N, channels), F32)],
        compiler_params=pltpu.CompilerParams(
            dimension_semantics=("arbitrary",), vmem_limit_bytes=40 * 2**20
        ),
        cost_estimate=lasting(1),
    )(rate, act, key_t, query_t)


def recur_backward_kernel(bits, kinds, rate_ref, act_ref, grad_ref, key_ref, query_ref, before_ref, last_ref, *refs):
    along = len(kinds)
    rider_in, refs = refs[:along], refs[along:]
    d_rate_ref, d_act_ref, d_key_ref, d_query_ref = refs[:4]
    rider_out, refs = refs[4 : 4 + along], refs[4 + along :]
    lam_ref, memory_ref, key_rows, query_rows = refs[:4]
    here = Place(bits)
    ride_start, ride_end = ride(here, kinds, rider_in + rider_out + refs[4:])
    wide, parts = widths(rate_ref.shape[1])
    block = rate_ref.shape[0]

    @pl.when(pl.program_id(0) == 0)
    def _():
        here.meet(rider_peers(here, kinds))
        ride_start()
        lam_ref[...] = jnp.zeros_like(lam_ref)
        memory_ref[...] = last_ref[...]

    lam = [lam_ref[:, lanes_of(p, wide)] for p in range(parts)]
    memory = [memory_ref[:, lanes_of(p, wide)] for p in range(parts)]
    for base in reversed(range(0, block, 8)):
        rates = rate_ref[base : base + 8, :]
        acts = act_ref[base : base + 8, :]
        grads = grad_ref[base : base + 8, :]
        d_rates = [[None] * 8 for _ in range(parts)]
        d_acts = [[None] * 8 for _ in range(parts)]
        for i in reversed(range(8)):
            at = base + i
            key = jnp.broadcast_to(key_ref[:, at : at + 1], (N, wide))
            query = jnp.broadcast_to(query_ref[:, at : at + 1], (N, wide))
            square = key * key
            key_sum = query_sum = None
            for p in range(parts):
                lanes = lanes_of(p, wide)
                grad = grads[i : i + 1, lanes]
                before = before_ref[at, :, lanes]
                pulled = query * grad + lam[p]
                kept = key * before
                missing = acts[i : i + 1, lanes] - kept
                keyed = pulled * key
                scaled = pulled * rates[i : i + 1, lanes]
                d_acts[p][i] = halves(keyed)
                d_rates[p][i] = halves(keyed * missing)
                to_key = scaled * (missing - kept)
                to_query = memory[p] * grad
                key_sum = to_key if key_sum is None else key_sum + to_key
                query_sum = to_query if query_sum is None else query_sum + to_query
                lam[p] = pulled - scaled * square
                memory[p] = before
            key_rows[at * N : (at + 1) * N, :] = key_sum.astype(BF)
            query_rows[at * N : (at + 1) * N, :] = query_sum.astype(BF)
        for p in range(parts):
            lanes = lanes_of(p, wide)
            d_rate_ref[base : base + 8, lanes] = sum_rows(d_rates[p])
            d_act_ref[base : base + 8, lanes] = rates[:, lanes] * sum_rows(d_acts[p])
    for p in range(parts):
        lam_ref[:, lanes_of(p, wide)] = lam[p]
        memory_ref[:, lanes_of(p, wide)] = memory[p]

    ones = jnp.ones((wide, block), BF)
    token = lax.broadcasted_iota(jnp.int32, (block, N, block), 0)
    own = token == lax.broadcasted_iota(jnp.int32, (block, N, block), 2)
    for rows, result in ((key_rows, d_key_ref), (query_rows, d_query_ref)):
        sums = forward_dot(rows[...], ones).reshape(block, N, block)
        result[...] = jnp.sum(jnp.where(own, sums, 0.0), axis=0)

    pl.when(pl.program_id(0) == pl.num_programs(0) - 1)(ride_end)


def recur_backward(bits, cid, rate, act, grad, key_t, query_t, before, last, riders):
    tokens, channels = rate.shape
    count = tokens // BLOCK
    rows = pl.BlockSpec((BLOCK, channels), lambda i: (count - 1 - i, 0))
    cols = pl.BlockSpec((N, BLOCK), lambda i: (0, count - 1 - i))
    products = pltpu.VMEM((BLOCK * N, widths(channels)[0]), BF)
    arrays, more_shapes, more_scratch = rider_shapes(bits, riders)
    outside = [pl.BlockSpec(memory_space=pl.ANY)] * len(arrays)
    return pl.pallas_call(
        functools.partial(recur_backward_kernel, bits, tuple(kind for kind, _ in riders)),
        grid=(count,),
        in_specs=[
            rows, rows, rows, cols, cols,
            pl.BlockSpec((BLOCK, N, channels), lambda i: (count - 1 - i, 0, 0)),
            pl.BlockSpec((N, channels), lambda i: (0, 0)),
        ] + outside,
        out_specs=[rows, rows, cols, cols] + outside,
        out_shape=[
            jax.ShapeDtypeStruct((tokens, channels), F32),
            jax.ShapeDtypeStruct((tokens, channels), F32),
            jax.ShapeDtypeStruct((N, tokens), F32),
            jax.ShapeDtypeStruct((N, tokens), F32),
        ] + more_shapes,
        scratch_shapes=[pltpu.VMEM((N, channels), F32), pltpu.VMEM((N, channels), F32), products, products]
        + more_scratch,
        compiler_params=pltpu.CompilerParams(
            dimension_semantics=("arbitrary",), vmem_limit_bytes=40 * 2**20, collective_id=cid, has_side_effects=True
        ),
        cost_estimate=lasting(1),
    )(rate, act, grad, key_t, query_t, before, last, *arrays)


class Place:
    def __init__(self, bits):
        self.bits = bits
        self.n = len(bits)
        self.count = 2**self.n
        self.at = [lax.axis_index(name) for name in bits]
        self.s = lax.axis_index("section")

    def other(self, e):
        return sum(2**d * (c + e // 2**d % 2 * (1 - 2 * c)) for d, c in enumerate(self.at))

    def toward(self, e):
        return {self.bits[d]: 1 - self.at[d] for d in range(self.n) if e // 2**d % 2}

    def dims(self, p, m):
        return sum(2 ** ((p + t) % self.n) for t in range(self.n) if m // 2**t % 2)

    def positions(self, p, e):
        return sum(2**t * (e // 2 ** ((p + t) % self.n) % 2) for t in range(self.n))

    def names(self, e):
        return tuple(self.bits[d] for d in range(self.n) if e // 2**d % 2)

    def meet(self, peers):
        barrier = pltpu.get_barrier_semaphore()
        peers = list(dict.fromkeys(peers))
        for axes in peers:
            where = {name: 1 - lax.axis_index(name) for name in axes}
            pl.semaphore_signal(barrier, inc=1, device_id=where, device_id_type=MESH)
        pl.semaphore_wait(barrier, len(peers))


def spans_of(width, n, shares=None):
    tiles = width // 128
    sizes = [(tiles // n + (p < tiles % n)) * 128 for p in range(n)]
    if shares is not None and len(shares) == n and sum(shares) == tiles:
        sizes = [share * 128 for share in shares]
    return [(sum(sizes[:p]), size) for p, size in enumerate(sizes)]


def remote(src, dst, send, recv, where):
    return pltpu.make_async_remote_copy(
        src_ref=src, dst_ref=dst, send_sem=send, recv_sem=recv, device_id=where, device_id_type=MESH
    )


def arrived(place, sem):
    pltpu.make_async_copy(place, place, sem).wait()


def rider_peers(here, kinds):
    peers = [here.names(e) for e in range(1, here.count)] if "cube" in kinds else []
    return peers + ([("q",)] if set(kinds) - {"cube"} else [])


def ride(here, kinds, refs):
    k = len(kinds)
    riders = list(zip(kinds, refs[:k], refs[k : 2 * k], refs[2 * k : 3 * k], refs[3 * k :]))
    q, chip = lax.axis_index("q"), here.other(0)

    def copies(kind, src, dst, send, recv):
        if kind == "cube":
            return [
                remote(src.at[here.other(e)], dst.at[chip], send.at[e], recv.at[e], here.toward(e))
                for e in range(1, here.count)
            ]
        return [remote(src, dst.at[q] if kind == "stack" else dst, send.at[0], recv.at[0], {"q": 1 - q})]

    def when(kind, sending, do):
        if kind in ("home", "leave"):
            pl.when((q != here.s) if sending == (kind == "home") else (q == here.s))(do)
        else:
            do()

    def start():
        for kind, src, dst, send, recv in riders:
            if kind == "cube":
                pltpu.make_async_copy(src.at[chip], dst.at[chip], recv.at[0]).start()
            if kind == "stack":
                pltpu.make_async_copy(src, dst.at[q], recv.at[1]).start()
            for copy in copies(kind, src, dst, send, recv):
                when(kind, True, copy.start)

    def finish():
        for kind, src, dst, send, recv in riders:
            if kind == "cube":
                for e in range(here.count):
                    arrived(dst.at[here.other(e)], recv.at[e])
            elif kind == "stack":
                arrived(dst.at[1 - q], recv.at[0])
                arrived(dst.at[q], recv.at[1])
            else:
                when(kind, False, lambda: arrived(dst, recv.at[0]))
            for copy in copies(kind, src, dst, send, recv):
                when(kind, True, copy.wait_send)

    return start, finish


def rider_shapes(bits, riders):
    sems = pltpu.SemaphoreType.DMA((2 ** len(bits),))
    shapes = [
        jax.ShapeDtypeStruct(((2,) if kind == "stack" else ()) + array.shape, array.dtype) for kind, array in riders
    ]
    return [array for _, array in riders], shapes, [sems] * (2 * len(riders))


def gather_kernel(bits, total, layer, kinds, shares, *refs):
    here = Place(bits)
    n, s, count = here.n, here.s, here.count
    q, chip = lax.axis_index("q"), here.other(0)
    along, own_count = len(kinds), total + (0 if layer is None else 3)
    inputs, refs = refs[: own_count + along], refs[own_count + along :]
    outputs, sems = refs[: own_count + along], refs[own_count + along :]
    given, made = inputs[:own_count], outputs[:own_count]
    ride_start, ride_end = ride(
        here, kinds, inputs[own_count:] + outputs[own_count:] + sems[len(sems) - 2 * along :]
    )
    local_sem, send, recv, core_send, core_recv = sems[:5]
    spans = spans_of(given[0].shape[1], n, shares)
    parts = [(k, p) for k in range(total) for p in range(n) if spans[p][1]]

    def block(k, e, p, s_of):
        return made[k].at[s_of, here.other(e), :, pl.ds(*spans[p])]

    def source(k, e, p):
        return block(k, e, p, s) if e else given[k].at[:, pl.ds(*spans[p])]

    def deliver(k, p, m):
        t = m.bit_length() - 1
        held = here.dims(p, m - 2**t)
        where = here.toward(2 ** ((p + t) % n))
        return remote(source(k, held, p), block(k, held, p, s), send.at[k, p, m], recv.at[k, p, m], where)

    def core(k, p, m):
        held = here.dims(p, m)
        sems = core_send.at[k, p, m], core_recv.at[k, p, m]
        return remote(source(k, held, p), block(k, held, p, s), *sems, {"section": 1 - s})

    if layer is None:
        here.meet([here.names(2**d) for d in range(n)] + [("section",)] + rider_peers(here, kinds))
    else:
        blocks, small = given[total : total + 2], given[total + 2]
        rows, own_small = made[total : total + 2], made[total + 2]
        lands = [rows[i].at[q, chip] for i in range(2)]
        piece_send, piece_recv, q_send, q_recv, small_send, small_recv = sems[5:]
        peers = [here.names(e) + extra for e in range(count) for extra in ((), ("section",)) if e or extra]
        here.meet(peers + [("q",), ("q", "section")])

        def piece(i, r, e):
            where = dict(here.toward(e), **({"section": 1 - s} if r else {}))
            src = blocks[i].at[1 - s if r else s, here.other(e)]
            return remote(src, lands[i], piece_send.at[i, r, e], piece_recv.at[i, e], where)

        def pass_on(i, e):
            place = rows[i].at[q, here.other(e)]
            return remote(place, place, q_send.at[i, e], q_recv.at[i, e], {"q": 1 - q})

        def hand_small(k, where):
            return remote(small, own_small, small_send.at[k], small_recv, where)

        keep_pieces = [pltpu.make_async_copy(blocks[i].at[s, chip], lands[i], piece_recv.at[i, 0]) for i in range(2)]
        keep_small = pltpu.make_async_copy(small, own_small, small_recv)
        at_layer = s == layer
        stays, leaves = jnp.logical_and(at_layer, q == s), jnp.logical_and(at_layer, q != s)

        @pl.when(at_layer)
        def _():
            for i in range(2):
                keep_pieces[i].start()
                for e in range(count):
                    for r in range(2):
                        if e or r:
                            piece(i, r, e).start()

        @pl.when(stays)
        def _():
            keep_small.start()
            hand_small(0, {"q": 1 - q}).start()

        @pl.when(leaves)
        def _():
            hand_small(0, {"section": 1 - s}).start()
            hand_small(1, {"section": 1 - s, "q": 1 - q}).start()

    own = [pltpu.make_async_copy(given[k], made[k].at[s, chip], local_sem.at[k]) for k in range(total)]
    for k in range(total):
        for t in range(n):
            for p in range(n):
                if spans[p][1]:
                    deliver(k, p, 2**t).start()
        own[k].start()
    ride_start()
    for k, p in parts:
        core(k, p, 0).start()
    for m in range(1, count):
        if layer is not None and m < 3:
            for e in range(count):
                arrived(rows[m - 1].at[q, here.other(e)], piece_recv.at[m - 1, e])
                pass_on(m - 1, e).start()
        for k, p in parts:
            arrived(block(k, here.dims(p, m), p, s), recv.at[k, p, m])
            for t in range(m.bit_length(), n):
                deliver(k, p, m + 2**t).start()
            core(k, p, m).start()
    for copy in own:
        copy.wait()
    for m in range(count):
        for k, p in parts:
            arrived(block(k, here.dims(p, m), p, 1 - s), core_recv.at[k, p, m])
    for m in range(count):
        for k, p in parts:
            core(k, p, m).wait_send()
            if m:
                deliver(k, p, m).wait_send()
    ride_end()
    if layer is not None:
        arrived(own_small, small_recv)
        for i in range(2):
            for e in range(count):
                arrived(rows[i].at[1 - q, here.other(e)], q_recv.at[i, e])
                pass_on(i, e).wait_send()

        @pl.when(at_layer)
        def _():
            for i in range(2):
                for e in range(count):
                    for r in range(2):
                        if e or r:
                            piece(i, r, e).wait_send()

        pl.when(stays)(lambda: hand_small(0, {"q": 1 - q}).wait_send())

        @pl.when(leaves)
        def _():
            hand_small(0, {"section": 1 - s}).wait_send()
            hand_small(1, {"section": 1 - s, "q": 1 - q}).wait_send()


def gather_call(bits, cid, shards, layer=None, extras=(), riders=(), shares=None, us=35):
    rows, width = shards[0].shape
    n = len(bits)
    count = 2**n
    dma = pltpu.SemaphoreType.DMA
    sems = dma((len(shards), n, count))
    shapes = [jax.ShapeDtypeStruct((2, count, rows, width), shard.dtype) for shard in shards]
    scratch = [dma((len(shards),)), sems, sems, sems, sems]
    if layer is not None:
        shapes += [jax.ShapeDtypeStruct(extra.shape, extra.dtype) for extra in extras]
        scratch += [dma((2, 2, count)), dma((2, count)), dma((2, count)), dma((2, count)), dma((2,)), dma]
    arrays, more_shapes, more_scratch = rider_shapes(bits, riders)
    shapes += more_shapes
    out = pl.pallas_call(
        functools.partial(gather_kernel, bits, len(shards), layer, tuple(kind for kind, _ in riders), shares),
        out_shape=shapes,
        in_specs=[pl.BlockSpec(memory_space=pl.ANY)] * len(shapes),
        out_specs=[pl.BlockSpec(memory_space=pl.ANY)] * len(shapes),
        scratch_shapes=scratch + more_scratch,
        compiler_params=pltpu.CompilerParams(collective_id=cid, has_side_effects=True),
        cost_estimate=lasting(us),
    )(*shards, *extras, *arrays)
    return [o.reshape((-1, width)) for o in out[: len(shards)]] + list(out[len(shards) :])


def add_rows(place, terms, out=None):
    step = 32
    out = place if out is None else out

    @pl.loop(0, place.shape[0] // step)
    def _(r):
        lines = pl.ds(pl.multiple_of(r * step, step), step)
        total = place[lines, :].astype(F32)
        for term in terms:
            total = total + term[lines, :].astype(F32)
        out[lines, :] = total.astype(out.dtype)


def scatter_kernel(bits, turned, homing, kinds, shares, terms, *refs):
    here = Place(bits)
    along = len(kinds)
    a_refs, b_refs, refs = refs[:terms], refs[terms : 2 * terms], refs[2 * terms :]
    if homing:
        grad, refs = refs[0], refs[1:]
    rider_in, refs = refs[:along], refs[along:]
    out_ref, refs = refs[0], refs[1:]
    if homing:
        home, other_home = refs[:2]
        refs = refs[2:]
    rider_out, refs = refs[:along], refs[along:]
    mine, give, core_in, landed, core_send, core_recv, send, recv = refs[:8]
    if homing:
        q_in, ready, q_send, q_recv, home_send, home_recv, over_send, over_recv = refs[8:16]
    ride_start, ride_end = ride(here, kinds, rider_in + rider_out + refs[len(refs) - 2 * along :])
    n, s, count = here.n, here.s, here.count
    rows, width = out_ref.shape
    tile = min(width, 512)
    spans = spans_of(width, n, shares)
    parts = [p for p in range(n) if spans[p][1]]

    def core(chip):
        return remote(give.at[chip], core_in.at[chip], core_send.at[chip], core_recv.at[chip], {"section": 1 - s})

    def hand(p, m, t):
        e = here.dims(p, m) if isinstance(m, int) else sum(
            2 ** ((p + u) % n) * (m // 2**u % 2) for u in range(n)
        )
        cols = pl.ds(*spans[p])
        return remote(
            mine.at[here.other(e), :, cols], landed.at[m, :, cols], send.at[p, m], recv.at[p, m],
            here.toward(2 ** ((p + t) % n)),
        )

    def to_q(e):
        q, chip = lax.axis_index("q"), here.other(e)
        return remote(grad.at[1 - q, chip], q_in.at[chip], q_send.at[e], q_recv.at[e], {"q": 1 - q})

    def to_chip(e):
        return remote(ready.at[here.other(e)], home.at[here.other(0)], home_send.at[e], home_recv.at[e], here.toward(e))

    def to_core(e):
        chip = here.other(e)
        return remote(home.at[chip], other_home.at[chip], over_send.at[e], over_recv.at[e], {"section": 1 - s})

    def home_step(e):
        chip = here.other(e)
        arrived(q_in.at[chip], q_recv.at[e])
        place = ready.at[chip] if e else home.at[chip]
        add_rows(q_in.at[chip], [grad.at[lax.axis_index("q"), chip]], place)
        (to_chip(e) if e else to_core(0)).start()

    def home_end(e):
        if e:
            arrived(home.at[here.other(e)], home_recv.at[e])
            to_core(e).start()

    peers = [here.names(2**d) for d in range(n)] + [("section",)]
    if homing:
        peers = [here.names(e) for e in range(1, count)] + [("section",), ("q",)]
    here.meet(peers + rider_peers(here, kinds))
    if homing:
        for e in range(count):
            to_q(e).start()
    ride_start()

    @pl.loop(0, count + 1)
    def _(i):
        @pl.when(i < count)
        def _():
            chip = here.other(count - 1 - i)

            def lines(s_of):
                return pl.ds(pl.multiple_of((s_of * count + chip) * rows, rows), rows)

            lefts = [jnp.concatenate([a_ref[lines(1 - s), :], a_ref[lines(s), :]], axis=0) for a_ref in a_refs]
            for c in range(0, width, tile):
                if turned:
                    value = sum(back_dot(left, b_ref[c : c + tile, :]) for left, b_ref in zip(lefts, b_refs))
                else:
                    value = sum(forward_dot(left, b_ref[:, c : c + tile]) for left, b_ref in zip(lefts, b_refs))
                value = value.astype(BF)
                give[chip, :, c : c + tile] = value[:rows]
                mine[chip, :, c : c + tile] = value[rows:]
            core(chip).start()

        @pl.when(i > 0)
        def _():
            e = count - i
            chip = here.other(e)
            arrived(core_in.at[chip], core_recv.at[chip])
            add_rows(mine.at[chip], [core_in.at[chip]])
            for p in parts:
                pl.when(e // 2 ** ((p + n - 1) % n) % 2 == 1)(
                    lambda p=p: hand(p, here.positions(p, e), n - 1).start()
                )

    def waiting(p, m):
        cols = pl.ds(*spans[p])
        terms = [m + 2**t for t in range(m.bit_length(), n)]
        for term in terms:
            arrived(landed.at[term, :, cols], recv.at[p, term])
        return mine.at[here.other(here.dims(p, m)), :, cols], [landed.at[term, :, cols] for term in terms]

    steps = count // 2
    for m in range(steps - 1, 0, -1):
        if homing:
            home_step(steps - 1 - m)
        for p in parts:
            add_rows(*waiting(p, m))
            hand(p, m, m.bit_length() - 1).start()
    for p in parts:
        place, terms = waiting(p, 0)
        add_rows(place, terms, out_ref.at[:, pl.ds(*spans[p])])
    if homing:
        for e in range(steps - 1, count):
            home_step(e)
        for e in range(count):
            home_end(e)
        for e in range(count):
            arrived(other_home.at[here.other(e)], over_recv.at[e])
            to_core(e).wait_send()
            to_q(e).wait_send()
            if e:
                to_chip(e).wait_send()
    ride_end()
    for chip in range(count):
        core(chip).wait_send()
    for m in range(1, count):
        for p in parts:
            hand(p, m, m.bit_length() - 1).wait_send()


def scatter_columns(bits, cid, a, b, turned, grad=None, riders=(), shares=None):
    tokens, width = a[0].shape[0], b[0].shape[0 if turned else 1]
    n = len(bits)
    count = 2**n
    block = (tokens // (2 * count), width)
    dma = pltpu.SemaphoreType.DMA
    blocks = pltpu.VMEM((count,) + block, BF)
    operands = list(a) + list(b)
    shapes = [jax.ShapeDtypeStruct(block, F32)]
    scratch = [blocks] * 4 + [dma((count,))] * 2 + [dma((n, count))] * 2
    if grad is not None:
        operands += [grad]
        shapes += [jax.ShapeDtypeStruct(grad.shape[1:], BF)] * 2
        scratch += [pltpu.VMEM(grad.shape[1:], BF)] * 2 + [dma((count,))] * 6
    arrays, more_shapes, more_scratch = rider_shapes(bits, riders)
    inside, outside = pl.BlockSpec(memory_space=pltpu.VMEM), pl.BlockSpec(memory_space=pl.ANY)
    return pl.pallas_call(
        functools.partial(
            scatter_kernel, bits, turned, grad is not None, tuple(kind for kind, _ in riders), shares, len(a)
        ),
        out_shape=shapes + more_shapes,
        in_specs=[inside] * len(operands) + [outside] * len(arrays),
        out_specs=[inside] * len(shapes) + [outside] * len(arrays),
        scratch_shapes=scratch + more_scratch,
        compiler_params=pltpu.CompilerParams(
            collective_id=cid, has_side_effects=True, vmem_limit_bytes=56 * 2**20
        ),
        cost_estimate=lasting(40 if grad is None else 60),
    )(*operands, *arrays)


def scatter_dot(bits, cid, a, b, turned, grad=None, riders=(), shares=None):
    tokens, width = a[0].shape[0], b[0].shape[0 if turned else 1]
    pieces = max(1, tokens * width // 2**22)
    size = width // pieces
    cuts = [
        [f[i * size : (i + 1) * size] if turned else f[:, i * size : (i + 1) * size] for f in b] for i in range(pieces)
    ]
    first = scatter_columns(bits, cid, a, cuts[0], turned, grad, riders, shares)
    rest = [scatter_columns(bits, 14 + turned, a, cut, turned)[0] for cut in cuts[1:]]
    return [jnp.concatenate([first[0]] + rest, axis=1)] + list(first[1:])


def total_kernel(bits, kinds, x_ref, *refs):
    here = Place(bits)
    s, count = here.s, here.count
    along = len(kinds)
    rider_in, out_ref, rider_out, refs = refs[:along], refs[along], refs[along + 1 : 2 * along + 1], refs[2 * along + 1 :]
    part, core_in, ready, landed, done, pair_send, pair_recv, send, recv, back_send, back_recv = refs[:11]
    ride_start, ride_end = ride(here, kinds, rider_in + rider_out + refs[11:])
    lanes = part.shape[3]

    def span(s_of, chip):
        at = (s_of * count + chip) * lanes
        return slice(at, at + lanes)

    for s_of in range(2):
        for chip in range(count):
            part[s_of, chip] = x_ref[:, span(s_of, chip)]
    here.meet([here.names(e) for e in range(1, count)] + [("section",)] + rider_peers(here, kinds))
    first = remote(part.at[1 - s], core_in, pair_send.at[0], pair_recv.at[0], {"section": 1 - s})
    first.start()
    first.wait_recv()
    for chip in range(count):
        total = part[s, chip] + core_in[chip]
        part[s, chip] = total
        ready[chip] = total.astype(BF)

    def out(e):
        return remote(ready.at[here.other(e)], landed.at[e], send.at[e], recv.at[e], here.toward(e))

    def back(e):
        place = done.at[s, here.other(0)]
        return remote(place, place, back_send.at[e], back_recv.at[e], here.toward(e))

    others = range(1, count)
    for e in others:
        out(e).start()
    ride_start()
    total = part[s, here.other(0)]
    for e in others:
        out(e).wait_recv()
        total = total + landed[e].astype(F32)
    done[s, here.other(0)] = total.astype(BF)
    for e in others:
        back(e).start()
    for e in others:
        place = done.at[s, here.other(e)]
        arrived(place, back_recv.at[e])
    last = remote(done.at[s], done.at[s], pair_send.at[1], pair_recv.at[1], {"section": 1 - s})
    last.start()
    last.wait_recv()
    for s_of in range(2):
        for chip in range(count):
            out_ref[:, span(s_of, chip)] = done[s_of, chip]
    ride_end()
    first.wait_send()
    last.wait_send()
    for e in others:
        out(e).wait_send()
        back(e).wait_send()


def sum_columns(bits, cid, x, riders=()):
    rows, tokens = x.shape
    count = 2 ** len(bits)
    block = (rows, tokens // (2 * count))
    dma, vmem = pltpu.SemaphoreType.DMA, pltpu.VMEM
    arrays, more_shapes, more_scratch = rider_shapes(bits, riders)
    inside, outside = pl.BlockSpec(memory_space=pltpu.VMEM), pl.BlockSpec(memory_space=pl.ANY)
    return pl.pallas_call(
        functools.partial(total_kernel, bits, tuple(kind for kind, _ in riders)),
        out_shape=[jax.ShapeDtypeStruct((rows, tokens), BF)] + more_shapes,
        in_specs=[inside] + [outside] * len(arrays),
        out_specs=[inside] + [outside] * len(arrays),
        scratch_shapes=[
            vmem((2, count) + block, F32),
            vmem((count,) + block, F32),
            vmem((count,) + block, BF),
            vmem((count,) + block, BF),
            vmem((2, count) + block, BF),
        ]
        + [dma((2,))] * 2
        + [dma((count,))] * 4
        + more_scratch,
        compiler_params=pltpu.CompilerParams(
            collective_id=cid, has_side_effects=True, vmem_limit_bytes=56 * 2**20
        ),
        cost_estimate=lasting(22),
    )(x, *arrays)


def spread_kernel(bits, shard_ref, out_ref, send, recv, pair_send, pair_recv):
    here = Place(bits)
    s, q, chip = here.s, lax.axis_index("q"), here.other(0)
    others = range(1, here.count)
    here.meet([here.names(e) for e in others] + [("section",), ("q",)])
    out_ref[s, q, chip] = shard_ref[...]
    own = out_ref.at[s, q, chip]
    copies = [remote(own, own, send.at[e], recv.at[e], here.toward(e)) for e in others]
    for copy in copies:
        copy.start()
    for e in others:
        arrived(out_ref.at[s, q, here.other(e)], recv.at[e])
    place = out_ref.at[s, q]
    first = remote(place, place, pair_send.at[0], pair_recv.at[0], {"q": 1 - q})
    first.start()
    first.wait_recv()
    place = out_ref.at[s]
    second = remote(place, place, pair_send.at[1], pair_recv.at[1], {"section": 1 - s})
    second.start()
    second.wait_recv()
    for copy in copies + [first, second]:
        copy.wait_send()


def spread(bits, shard):
    width, count = shard.shape[0], 2 ** len(bits)
    block = (16, max(width, 128))
    padded = jnp.pad(shard[None, :], ((0, block[0] - 1), (0, block[1] - width)))
    dma = pltpu.SemaphoreType.DMA
    out = pl.pallas_call(
        functools.partial(spread_kernel, bits),
        out_shape=jax.ShapeDtypeStruct((2, 2, count) + block, shard.dtype),
        in_specs=[pl.BlockSpec(memory_space=pltpu.VMEM)],
        out_specs=pl.BlockSpec(memory_space=pltpu.VMEM),
        scratch_shapes=[dma((count,)), dma((count,)), dma((2,)), dma((2,))],
        compiler_params=pltpu.CompilerParams(collective_id=0, has_side_effects=True),
        cost_estimate=lasting(12),
    )(padded)
    return out[:, :, :, 0, :width].reshape((2, -1))


def chips(bits):
    return tuple(reversed(bits))


def at_home():
    return lax.axis_index("q") == lax.axis_index("section")


def low_first(mine, other):
    low = lax.axis_index("q") == 0
    return jnp.stack([jnp.where(low, mine, other), jnp.where(low, other, mine)])


def by_q(pair):
    low = lax.axis_index("q") == 0
    return jnp.where(low, pair[0], pair[1]), jnp.where(low, pair[1], pair[0])


def leave(value):
    return lax.ppermute(value, ("section", "q"), [(0, 1), (3, 2)])


def home(value):
    return lax.ppermute(value, ("section", "q"), [(1, 0), (2, 3)])


def swap(value):
    return lax.ppermute(value, "q", [(0, 1), (1, 0)])


def after(value, *earlier):
    return lax.optimization_barrier((value,) + earlier)[0]


def over_core(piece, layer):
    other = 1 - layer
    sent = lax.ppermute(piece, ("section", "q"), [(layer * 2 + other, other * 2 + other)])
    return jnp.where(lax.axis_index("section") == layer, piece, sent)


def back_over_core(piece, layer):
    other = 1 - layer
    return lax.ppermute(piece, ("section", "q"), [(other * 2 + other, layer * 2 + other)])


def column_blocks(bits, rows):
    parts = rows.reshape((rows.shape[0], 2, 2, 2 ** len(bits), -1))
    return [jnp.transpose(parts[:, i], (1, 2, 0, 3)) for i in range(2)]


def silu_slope(v):
    gate = jax.nn.sigmoid(v)
    return gate, gate * (1.0 + v * (1.0 - gate))


def normalize(stream, gain):
    inverse = lax.rsqrt(jnp.mean(stream * stream, axis=-1, keepdims=True) + norm_eps)
    return inverse, (stream * inverse * gain[None, :]).astype(BF)


class Small:
    def __init__(self, packed):
        self.taps = packed[:KC].astype(F32)
        self.conv_bias = packed[KC].astype(F32)
        self.dt_bias = packed[KC + 1].astype(F32)
        self.skip = packed[KC + 2].astype(F32)
        self.dt = packed[KC + 3 : KC + 3 + R]
        self.xproj = packed[KC + 3 + R : KC + 3 + 2 * R + 2 * N]


def mixer_inputs(normed, in_inner, small):
    inner = forward_dot(normed, in_inner).astype(BF).astype(F32)
    tokens, channels = inner.shape
    extended = jnp.concatenate([jnp.zeros((KC - 1, channels), F32), inner], axis=0)
    conv = jnp.broadcast_to(small.conv_bias[None, :], (tokens, channels))
    for tap in range(KC):
        conv = conv + small.taps[tap][None, :] * extended[tap : tap + tokens]
    act = jax.nn.silu(conv)
    return extended, conv, act, back_dot(small.xproj, act.astype(BF))


def mixer(xproj, act, normed, in_gate, small):
    gate_in = forward_dot(normed, in_gate).astype(BF).astype(F32)
    key_t, query_t = xproj[R : R + N].astype(F32), xproj[R + N :].astype(F32)
    key_norm = jnp.sum(key_t * key_t, axis=0)[:, None]
    write = jax.nn.sigmoid(cross_dot(xproj[:R], small.dt) + small.dt_bias[None, :])
    rate = write / (1.0 + write * key_norm)
    recur, before, last = recur_forward(rate, act, key_t, query_t)
    recur = recur + small.skip[None, :] * act
    gated = (recur * jax.nn.silu(gate_in)).astype(BF)
    return gate_in, key_t, query_t, key_norm, write, rate, recur, gated, before, last


def gate_back(grad_low, out_weight, kept):
    gate_in, recur = kept[0], kept[6]
    d_gated = back_dot(grad_low, out_weight).astype(BF).astype(F32)
    gate, slope = silu_slope(gate_in)
    return d_gated * (gate_in * gate), (d_gated * recur * slope).astype(BF)


def mixer_back(bits, cid, d_recur, act, xproj, kept, small, riders):
    key_t, query_t, key_norm, write, rate, recur, gated, before, last = kept[1:]
    d_skip = jnp.sum(d_recur * act, axis=0)
    d_rate, d_act_rec, d_key_t, d_query_t, *gots = recur_backward(
        bits, cid, rate, act, d_recur, key_t, query_t, before, last, riders
    )
    share = 1.0 / (1.0 + write * key_norm)
    pulled = d_rate * share * share
    d_pre = pulled * write * (1.0 - write)
    d_key_rate = -2.0 * key_t * jnp.sum(pulled * write * write, axis=1)[None, :]
    d_dt_bias = jnp.sum(d_pre, axis=0)
    d_delta = d_pre.astype(BF)
    d_dt = forward_dot(xproj[:R], d_delta)
    d_xproj = jnp.concatenate([back_dot(small.dt, d_delta), d_key_t + d_key_rate, d_query_t], axis=0)
    return d_act_rec, d_xproj, (d_dt_bias[None], d_skip[None], d_dt), gots


def inputs_back(d_xproj, d_recur, d_act_rec, extended, conv, act, small):
    tokens = act.shape[0]
    d_act = cross_dot(d_xproj, small.xproj) + small.skip[None, :] * d_recur + d_act_rec
    d_conv = d_act * silu_slope(conv)[1]
    d_taps = jnp.stack([jnp.sum(d_conv * extended[tap : tap + tokens], axis=0) for tap in range(KC)])
    d_bias = jnp.sum(d_conv, axis=0)
    later = jnp.concatenate([d_conv, jnp.zeros((KC - 1, d_conv.shape[1]), F32)], axis=0)
    d_inner = sum(small.taps[tap][None, :] * later[KC - 1 - tap : KC - 1 - tap + tokens] for tap in range(KC))
    return d_inner.astype(BF), (d_taps, d_bias[None]), forward_dot(d_xproj, act.astype(BF))


def norm_back(grad_out, d_normed, stream, inverse, gain):
    scaled = gain[None, :] * d_normed
    mean = jnp.mean(stream * scaled, axis=-1, keepdims=True)
    return grad_out + inverse * scaled - stream * inverse**3 * mean


def pack(first, second, third):
    packed = jnp.concatenate(first + second + (third,), axis=0)
    return jnp.pad(packed, ((0, -packed.shape[0] % 16), (0, 0)))


def on_device(
    bits, hidden_in, cotangent, norm_gain, in_weight, conv_weight, conv_bias, xproj_weight, dt_weight, dt_bias, skip_gain, out_weight
):
    packed = pack(
        (conv_weight[0], conv_bias),
        (dt_bias, skip_gain, dt_weight[0]),
        jnp.swapaxes(xproj_weight[0], 0, 1),
    )
    blocks = column_blocks(bits, in_weight[0])
    tight = (2, 5, 9)

    def weight(pair):
        return pair.reshape((-1, pair.shape[-1]))

    def weight_grad(normed, d_out):
        return cross_dot(normed, d_out).astype(BF).reshape((2,) + blocks[0].shape[1:])

    gains = spread(bits, norm_gain[0]).astype(F32)
    mine, others = by_q(hidden_in)
    stream0 = jnp.where(at_home(), mine, leave(others)).astype(F32)

    inverse0, normed = normalize(stream0, gains[0])
    normed0, inner, gate, packed0 = gather_call(bits, 1, [normed], 0, (*blocks, packed), shares=tight, us=60)
    out_weight, packed, blocks, cotangent = lax.optimization_barrier((out_weight, packed, blocks, cotangent, packed0))[:4]
    inner0, small0 = weight(inner), Small(packed0)
    extended0, conv0, act0, part = mixer_inputs(normed0, inner0, small0)
    out_held = over_core(out_weight[0], 0)
    part = after(part, out_held)
    upper = lax.axis_index("section") == 1
    columns = [jnp.where(upper, b[1], lax.ppermute(b[0], "section", [(1, 0)])) for b in blocks]
    xproj0, inner, late_gate = sum_columns(bits, 4, part, [("cube", columns[0]), ("cube", columns[1])])
    gate0 = weight(gate)
    out0 = jnp.where(at_home(), out_held, leave(after(out_held, xproj0)))
    kept0 = mixer(xproj0, act0, normed0, gate0, small0)
    packed_held = over_core(packed, 1)
    grad_mine, grad_others = by_q(cotangent)
    added, got, grad_got = scatter_dot(
        bits, 8, [kept0[7]], [out0], False, riders=[("leave", packed_held), ("leave", grad_others.astype(BF))]
    )
    grad1 = jnp.where(at_home(), grad_mine, grad_got.astype(F32))
    small1 = Small(jnp.where(at_home(), packed_held, got))
    output0 = (stream0 + added).astype(BF)

    stream1 = output0.astype(F32)
    inverse1, normed = normalize(stream1, gains[1])
    normed1, grad_low1, inner, output0_home = gather_call(
        bits, 2, [normed, grad1.astype(BF)], riders=[("stack", inner), ("home", output0)], shares=(3, 5, 8), us=65
    )
    inner1 = weight(inner)
    extended1, conv1, act1, part = mixer_inputs(normed1, inner1, small1)
    out_held = over_core(out_weight[0], 1)
    xproj1, gate = sum_columns(bits, 5, after(part, out_held), [("stack", late_gate)])
    gate1 = weight(gate)
    out1 = jnp.where(at_home(), out_held, leave(after(out_held, xproj1)))
    kept1 = mixer(xproj1, act1, normed1, gate1, small1)

    d_out1 = cross_dot(kept1[7], grad_low1)
    d_recur, d_gate1 = gate_back(grad_low1, out1, kept1)
    keep, give = by_q(weight_grad(normed1, d_gate1))
    d_act_rec, part, d_small, (got,) = mixer_back(bits, 16, d_recur, act1, xproj1, kept1, small1, [("swap", give)])
    (d_xproj,) = sum_columns(bits, 6, part)
    d_gate_in1 = (keep.astype(F32) + got.astype(F32)).astype(BF)
    d_inner, d_conv, d_xproj_weight = inputs_back(d_xproj, d_recur, d_act_rec, extended1, conv1, act1, small1)
    d_packed1 = pack(d_conv, d_small, d_xproj_weight)
    d_normed, d_gate_in1, d_packed1_home, d_out1_home = scatter_dot(
        bits, 11, [d_inner, d_gate1], [inner1, gate1], True,
        riders=[("cube", d_gate_in1), ("home", d_packed1.astype(BF)), ("home", d_out1.astype(BF))], shares=(4, 5, 7),
    )
    keep, give = by_q(weight_grad(normed1, d_inner))
    input_grad1 = norm_back(grad1, d_normed, stream1, inverse1, gains[1])
    grad0 = input_grad1.astype(BF)
    grad_low0, got, grad1_home = gather_call(
        bits, 3, [grad0], riders=[("swap", give), ("home", grad0)], shares=(3, 5, 8), us=45
    )
    d_inner1 = (keep.astype(F32) + got.astype(F32)).astype(BF)

    d_out0 = cross_dot(kept0[7], grad_low0)
    d_recur, d_gate0 = gate_back(grad_low0, out0, kept0)
    added, d_inner1, d_out0_home = scatter_dot(
        bits, 10, [kept1[7]], [out1], False, riders=[("cube", d_inner1), ("home", d_out0.astype(BF))], shares=(4, 5, 7)
    )
    output1 = (stream1 + added).astype(BF)
    keep, give = by_q(weight_grad(normed0, d_gate0))
    d_act_rec, part, d_small, (got, output1_home) = mixer_back(
        bits, 17, d_recur, act0, xproj0, kept0, small0, [("swap", give), ("home", output1)]
    )
    d_gate_in0 = (keep.astype(F32) + got.astype(F32)).astype(BF)
    d_xproj, d_gate_in0 = sum_columns(bits, 7, part, [("cube", d_gate_in0)])
    d_inner, d_conv, d_xproj_weight = inputs_back(d_xproj, d_recur, d_act_rec, extended0, conv0, act0, small0)
    d_packed0 = pack(d_conv, d_small, d_xproj_weight)
    d_normed, d_inner0, d_inner0_other, d_packed0_home = scatter_dot(
        bits, 13, [d_inner, d_gate0], [inner0, gate0], True,
        weight_grad(normed0, d_inner), [("home", d_packed0.astype(BF))], shares=(3, 5, 8),
    )
    input_grad0 = norm_back(grad0.astype(F32), d_normed, stream0, inverse0, gains[0]).astype(BF)

    def settled(pairs):
        sent = [back_over_core(pair, layer) for layer, pair in enumerate(pairs)]
        return jnp.where(at_home(), jnp.where(upper, pairs[1], pairs[0]), jnp.where(upper, sent[1], sent[0]))

    layer_outputs = settled((low_first(output0, output0_home), low_first(output1, output1_home))).astype(F32)
    grads1 = low_first(grad0, grad1_home)
    grads1 = jnp.where(at_home(), grads1, back_over_core(grads1, 1))
    of_first = lax.ppermute(input_grad0, ("section", "q"), [(2, 1)])
    of_second = lax.ppermute(input_grad0, ("section", "q"), [(1, 0), (3, 1)])
    grads0 = jnp.stack([jnp.where(lax.axis_index("q") == 0, input_grad0, of_first), of_second])
    input_grads = jnp.where(upper, grads1, grads0).astype(F32)
    d_packed = settled(
        tuple(
            (mine + other.astype(F32)).astype(BF)
            for mine, other in ((d_packed0, d_packed0_home), (d_packed1, d_packed1_home))
        )
    ).astype(F32)
    d_out = settled(
        tuple(
            (mine + other.astype(F32)).astype(BF) for mine, other in ((d_out0, d_out0_home), (d_out1, d_out1_home))
        )
    ).astype(F32)
    own, others = [], []
    for lower_part, upper_part in ((d_inner0, d_inner1), (d_gate_in0, d_gate_in1)):
        own.append(jnp.where(upper, upper_part, lower_part))
        others.append(jnp.where(upper, lower_part, upper_part))
    others = [d_inner0_other, lax.ppermute(others[1], "section", [(0, 1), (1, 0)])]
    others[0] = jnp.where(upper, lax.ppermute(d_inner1, "section", [(0, 1)]), others[0])
    parts = [part for m, o in zip(own, others) for part in (jnp.where(upper, o, m), jnp.where(upper, m, o))]
    d_in = jnp.concatenate([jnp.swapaxes(part, 0, 1).reshape((part.shape[1], -1)) for part in parts], axis=1).astype(F32)
    d_gain = jnp.sum(d_in * in_weight[0].astype(F32), axis=1) / norm_gain[0].astype(F32)
    return (
        layer_outputs[None],
        input_grads[None],
        d_gain[None],
        d_in[None],
        d_packed[None, :KC],
        d_packed[None, KC],
        jnp.swapaxes(d_packed[KC + 3 + R : KC + 3 + 2 * R + 2 * N], 0, 1)[None],
        d_packed[None, KC + 3 : KC + 3 + R],
        d_packed[None, KC + 1],
        d_packed[None, KC + 2],
        d_out[None],
    )


def solution(mesh):
    sections, chip_count = mesh.devices.shape
    n = chip_count.bit_length() - 2
    bits = tuple("c%d" % d for d in range(n))
    split = Mesh(mesh.devices.reshape((sections,) + (2,) * (n + 1)), ("section", "q") + chips(bits))
    seq = ("q",) + chips(bits)
    placed = (
        P(None, seq, None),
        P(None, seq, None),
        P("section", seq),
        P("section", seq, None),
        P("section", None, seq),
        P("section", seq),
        P("section", seq, None),
        P("section", None, seq),
        P("section", seq),
        P("section", seq),
        P("section", seq, None),
    )
    return jax.shard_map(
        functools.partial(on_device, bits),
        mesh=split,
        in_specs=placed,
        out_specs=(P("section", None, seq, None), P("section", None, seq, None)) + placed[2:],
        check_vma=False,
    )
```

```python
import functools

import jax
import jax.numpy as jnp
from jax import lax
from jax.experimental import pallas as pl
from jax.experimental.pallas import tpu as pltpu
from jax.sharding import Mesh, PartitionSpec as P


N = 16
R = 128
KC = 4
BLOCK = 128
norm_eps = 1e-05
BF = jnp.bfloat16
F32 = jnp.float32
MESH = pl.DeviceIdType.MESH


def forward_dot(operand, factor):
    return jnp.dot(operand, factor, preferred_element_type=F32)


def cross_dot(operand, factor):
    return lax.dot_general(operand, factor, (((0,), (0,)), ((), ())), preferred_element_type=F32)


def back_dot(operand, factor):
    return lax.dot_general(operand, factor, (((1,), (1,)), ((), ())), preferred_element_type=F32)


def lasting(us):
    return pl.CostEstimate(flops=0, bytes_accessed=int(us * 3.4e6), transcendentals=0)


def widths(channels):
    wide = min(channels, 128)
    return wide, channels // wide


def sum_rows(pieces):
    row = lax.broadcasted_iota(jnp.int32, pieces[0].shape, 0)
    shift = 1
    while len(pieces) > 1:
        keep = (row & shift) == 0
        pieces = [
            jnp.where(keep, a, b) + pltpu.roll(jnp.where(keep, b, a), shift, 0)
            for a, b in zip(pieces[0::2], pieces[1::2])
        ]
        shift *= 2
    return pieces[0]


def halves(v):
    return v[:8] + v[8:]


def lanes_of(p, wide):
    return slice(p * wide, (p + 1) * wide)


def recur_forward_kernel(rate_ref, act_ref, key_ref, query_ref, out_ref, before_ref, last_ref, memory_ref):
    wide, parts = widths(rate_ref.shape[1])

    @pl.when(pl.program_id(0) == 0)
    def _():
        memory_ref[...] = jnp.zeros_like(memory_ref)

    memory = [memory_ref[:, lanes_of(p, wide)] for p in range(parts)]
    for base in range(0, rate_ref.shape[0], 8):
        rates = rate_ref[base : base + 8, :]
        feeds = rates * act_ref[base : base + 8, :]
        sums = [[] for _ in range(parts)]
        for i in range(8):
            key = jnp.broadcast_to(key_ref[:, base + i : base + i + 1], (N, wide))
            query = jnp.broadcast_to(query_ref[:, base + i : base + i + 1], (N, wide))
            square = key * key
            for p in range(parts):
                lanes = lanes_of(p, wide)
                before_ref[base + i, :, lanes] = memory[p]
                memory[p] = (1.0 - rates[i : i + 1, lanes] * square) * memory[p] + key * feeds[i : i + 1, lanes]
                sums[p].append(halves(memory[p] * query))
        for p in range(parts):
            out_ref[base : base + 8, lanes_of(p, wide)] = sum_rows(sums[p])
    for p in range(parts):
        memory_ref[:, lanes_of(p, wide)] = memory[p]

    @pl.when(pl.program_id(0) == pl.num_programs(0) - 1)
    def _():
        last_ref[...] = memory_ref[...]


def recur_forward(rate, act, key_t, query_t):
    tokens, channels = rate.shape
    rows = pl.BlockSpec((BLOCK, channels), lambda i: (i, 0))
    cols = pl.BlockSpec((N, BLOCK), lambda i: (0, i))
    return pl.pallas_call(
        recur_forward_kernel,
        grid=(tokens // BLOCK,),
        in_specs=[rows, rows, cols, cols],
        out_specs=[
            rows,
            pl.BlockSpec((BLOCK, N, channels), lambda i: (i, 0, 0)),
            pl.BlockSpec((N, channels), lambda i: (0, 0)),
        ],
        out_shape=[
            jax.ShapeDtypeStruct((tokens, channels), F32),
            jax.ShapeDtypeStruct((tokens, N, channels), F32),
            jax.ShapeDtypeStruct((N, channels), F32),
        ],
        scratch_shapes=[pltpu.VMEM((N, channels), F32)],
        compiler_params=pltpu.CompilerParams(
            dimension_semantics=("arbitrary",), vmem_limit_bytes=40 * 2**20
        ),
        cost_estimate=lasting(1),
    )(rate, act, key_t, query_t)


def recur_backward_kernel(bits, kinds, shares, steps, rate_ref, act_ref, grad_ref, key_ref, query_ref, before_ref, last_ref, *refs):
    along, beside = len(kinds), 1 if steps else 0
    product, refs = refs[: 2 * beside], refs[2 * beside :]
    rider_in, refs = refs[:along], refs[along:]
    d_rate_ref, d_act_ref, d_key_ref, d_query_ref = refs[:4]
    scattered, refs = refs[4 : 4 + beside], refs[4 + beside :]
    rider_out, refs = refs[:along], refs[along:]
    lam_ref, memory_ref, key_rows, query_rows = refs[:4]
    here = Place(bits)
    ride_start, ride_end = ride(here, kinds, rider_in + rider_out + refs[len(refs) - 2 * along :])
    stages = {}
    peers = rider_peers(here, kinds)
    if beside:
        work = Scatter(here, False, shares, product[:1], product[1:], scattered[0], refs[4:12])
        peers = peers + work.peers
        half = here.count // 2
        for k in range(half + 1):
            stages[k] = functools.partial(work.produce, 2 * k, min(2 * k + 2, here.count + 1))
        for k, m in enumerate(range(half - 1, 0, -1)):
            stages[steps - 1 - 2 * (half - 1 - k)] = functools.partial(work.pass_on, m)
    wide, parts = widths(rate_ref.shape[1])
    block = rate_ref.shape[0]

    @pl.when(pl.program_id(0) == 0)
    def _():
        here.meet(peers)
        ride_start()
        lam_ref[...] = jnp.zeros_like(lam_ref)
        memory_ref[...] = last_ref[...]

    for at, stage in stages.items():
        pl.when(pl.program_id(0) == at)(stage)
    lam = [lam_ref[:, lanes_of(p, wide)] for p in range(parts)]
    memory = [memory_ref[:, lanes_of(p, wide)] for p in range(parts)]
    for base in reversed(range(0, block, 8)):
        rates = rate_ref[base : base + 8, :]
        acts = act_ref[base : base + 8, :]
        grads = grad_ref[base : base + 8, :]
        d_rates = [[None] * 8 for _ in range(parts)]
        d_acts = [[None] * 8 for _ in range(parts)]
        for i in reversed(range(8)):
            at = base + i
            key = jnp.broadcast_to(key_ref[:, at : at + 1], (N, wide))
            query = jnp.broadcast_to(query_ref[:, at : at + 1], (N, wide))
            square = key * key
            key_sum = query_sum = None
            for p in range(parts):
                lanes = lanes_of(p, wide)
                grad = grads[i : i + 1, lanes]
                before = before_ref[at, :, lanes]
                pulled = query * grad + lam[p]
                kept = key * before
                missing = acts[i : i + 1, lanes] - kept
                keyed = pulled * key
                scaled = pulled * rates[i : i + 1, lanes]
                d_acts[p][i] = halves(keyed)
                d_rates[p][i] = halves(keyed * missing)
                to_key = scaled * (missing - kept)
                to_query = memory[p] * grad
                key_sum = to_key if key_sum is None else key_sum + to_key
                query_sum = to_query if query_sum is None else query_sum + to_query
                lam[p] = pulled - scaled * square
                memory[p] = before
            key_rows[at * N : (at + 1) * N, :] = key_sum.astype(BF)
            query_rows[at * N : (at + 1) * N, :] = query_sum.astype(BF)
        for p in range(parts):
            lanes = lanes_of(p, wide)
            d_rate_ref[base : base + 8, lanes] = sum_rows(d_rates[p])
            d_act_ref[base : base + 8, lanes] = rates[:, lanes] * sum_rows(d_acts[p])
    for p in range(parts):
        lam_ref[:, lanes_of(p, wide)] = lam[p]
        memory_ref[:, lanes_of(p, wide)] = memory[p]

    ones = jnp.ones((wide, block), BF)
    token = lax.broadcasted_iota(jnp.int32, (block, N, block), 0)
    own = token == lax.broadcasted_iota(jnp.int32, (block, N, block), 2)
    for rows, result in ((key_rows, d_key_ref), (query_rows, d_query_ref)):
        sums = forward_dot(rows[...], ones).reshape(block, N, block)
        result[...] = jnp.sum(jnp.where(own, sums, 0.0), axis=0)

    @pl.when(pl.program_id(0) == pl.num_programs(0) - 1)
    def _():
        if beside:
            work.settle()
            work.drain()
        ride_end()


def recur_backward(bits, cid, rate, act, grad, key_t, query_t, before, last, riders, product=(), shares=None):
    tokens, channels = rate.shape
    count = tokens // BLOCK
    rows = pl.BlockSpec((BLOCK, channels), lambda i: (count - 1 - i, 0))
    cols = pl.BlockSpec((N, BLOCK), lambda i: (0, count - 1 - i))
    products = pltpu.VMEM((BLOCK * N, widths(channels)[0]), BF)
    arrays, more_shapes, more_scratch = rider_shapes(bits, riders)
    outside = [pl.BlockSpec(memory_space=pl.ANY)] * len(arrays)
    inside = [pl.BlockSpec(memory_space=pltpu.VMEM)] * len(product)
    if product:
        block = (tokens // 2 ** (len(bits) + 1), product[1].shape[1])
        more_shapes = [jax.ShapeDtypeStruct(block, F32)] + more_shapes
        more_scratch = scatter_scratch(bits, block) + more_scratch
    return pl.pallas_call(
        functools.partial(
            recur_backward_kernel, bits, tuple(kind for kind, _ in riders), shares, count if product else 0
        ),
        grid=(count,),
        in_specs=[
            rows, rows, rows, cols, cols,
            pl.BlockSpec((BLOCK, N, channels), lambda i: (count - 1 - i, 0, 0)),
            pl.BlockSpec((N, channels), lambda i: (0, 0)),
        ] + inside + outside,
        out_specs=[rows, rows, cols, cols] + inside[:1] + outside,
        out_shape=[
            jax.ShapeDtypeStruct((tokens, channels), F32),
            jax.ShapeDtypeStruct((tokens, channels), F32),
            jax.ShapeDtypeStruct((N, tokens), F32),
            jax.ShapeDtypeStruct((N, tokens), F32),
        ] + more_shapes,
        scratch_shapes=[pltpu.VMEM((N, channels), F32), pltpu.VMEM((N, channels), F32), products, products]
        + more_scratch,
        compiler_params=pltpu.CompilerParams(
            dimension_semantics=("arbitrary",), vmem_limit_bytes=56 * 2**20, collective_id=cid, has_side_effects=True
        ),
        cost_estimate=lasting(1),
    )(rate, act, grad, key_t, query_t, before, last, *product, *arrays)


class Place:
    def __init__(self, bits):
        self.bits = bits
        self.n = len(bits)
        self.count = 2**self.n
        self.at = [lax.axis_index(name) for name in bits]
        self.s = lax.axis_index("section")

    def other(self, e):
        return sum(2**d * (c + e // 2**d % 2 * (1 - 2 * c)) for d, c in enumerate(self.at))

    def toward(self, e):
        return {self.bits[d]: 1 - self.at[d] for d in range(self.n) if e // 2**d % 2}

    def dims(self, p, m):
        return sum(2 ** ((p + t) % self.n) for t in range(self.n) if m // 2**t % 2)

    def positions(self, p, e):
        return sum(2**t * (e // 2 ** ((p + t) % self.n) % 2) for t in range(self.n))

    def names(self, e):
        return tuple(self.bits[d] for d in range(self.n) if e // 2**d % 2)

    def meet(self, peers):
        barrier = pltpu.get_barrier_semaphore()
        peers = list(dict.fromkeys(peers))
        for axes in peers:
            where = {name: 1 - lax.axis_index(name) for name in axes}
            pl.semaphore_signal(barrier, inc=1, device_id=where, device_id_type=MESH)
        pl.semaphore_wait(barrier, len(peers))


def spans_of(width, n, shares=None):
    tiles = width // 128
    sizes = [(tiles // n + (p < tiles % n)) * 128 for p in range(n)]
    if shares is not None and len(shares) == n and sum(shares) == tiles:
        sizes = [share * 128 for share in shares]
    return [(sum(sizes[:p]), size) for p, size in enumerate(sizes)]


def remote(src, dst, send, recv, where):
    return pltpu.make_async_remote_copy(
        src_ref=src, dst_ref=dst, send_sem=send, recv_sem=recv, device_id=where, device_id_type=MESH
    )


def arrived(place, sem):
    pltpu.make_async_copy(place, place, sem).wait()


def rider_peers(here, kinds):
    peers = [here.names(e) for e in range(1, here.count)] if "cube" in kinds else []
    if set(kinds) & {"swap", "stack", "home", "leave"}:
        peers.append(("q",))
    if set(kinds) & {"over", "over_at", "out0", "out1", "back0", "back1"}:
        peers.append(("section",))
    return peers


def ride(here, kinds, refs):
    k = len(kinds)
    riders = list(zip(kinds, refs[:k], refs[k : 2 * k], refs[2 * k : 3 * k], refs[3 * k :]))
    q, chip = lax.axis_index("q"), here.other(0)

    def copies(kind, src, dst, send, recv):
        if kind == "cube":
            return [
                remote(src.at[here.other(e)], dst.at[chip], send.at[e], recv.at[e], here.toward(e))
                for e in range(1, here.count)
            ]
        if kind in ("over", "over_at") or kind[:-1] in ("out", "back"):
            src = src.at[1 - here.s] if kind == "over_at" else src
            return [remote(src, dst, send.at[0], recv.at[0], {"section": 1 - here.s})]
        return [remote(src, dst.at[q] if kind == "stack" else dst, send.at[0], recv.at[0], {"q": 1 - q})]

    def when(kind, sending, do):
        if kind in ("home", "leave"):
            pl.when((q != here.s) if sending == (kind == "home") else (q == here.s))(do)
        elif kind[:-1] in ("out", "back"):
            at_layer = (here.s == int(kind[-1])) if sending == (kind[:-1] == "out") else (here.s != int(kind[-1]))
            away = (q != here.s) if sending == (kind[:-1] == "out") else (q == here.s)
            pl.when(jnp.logical_and(at_layer, away))(do)
        else:
            do()

    def start():
        for kind, src, dst, send, recv in riders:
            if kind == "cube":
                pltpu.make_async_copy(src.at[chip], dst.at[chip], recv.at[0]).start()
            if kind == "stack":
                pltpu.make_async_copy(src, dst.at[q], recv.at[1]).start()
            for copy in copies(kind, src, dst, send, recv):
                when(kind, True, copy.start)

    def finish():
        for kind, src, dst, send, recv in riders:
            if kind == "cube":
                for e in range(here.count):
                    arrived(dst.at[here.other(e)], recv.at[e])
            elif kind == "stack":
                arrived(dst.at[1 - q], recv.at[0])
                arrived(dst.at[q], recv.at[1])
            else:
                when(kind, False, lambda: arrived(dst, recv.at[0]))
            for copy in copies(kind, src, dst, send, recv):
                when(kind, True, copy.wait_send)

    return start, finish


def rider_shapes(bits, riders):
    sems = pltpu.SemaphoreType.DMA((2 ** len(bits),))
    shapes = [
        jax.ShapeDtypeStruct(
            array.shape[1:] if kind == "over_at" else ((2,) if kind == "stack" else ()) + array.shape, array.dtype
        )
        for kind, array in riders
    ]
    return [array for _, array in riders], shapes, [sems] * (2 * len(riders))


def gather_kernel(bits, total, layer, kinds, shares, *refs):
    here = Place(bits)
    n, s, count = here.n, here.s, here.count
    q, chip = lax.axis_index("q"), here.other(0)
    along, own_count = len(kinds), total + (0 if layer is None else 3)
    inputs, refs = refs[: own_count + along], refs[own_count + along :]
    outputs, sems = refs[: own_count + along], refs[own_count + along :]
    given, made = inputs[:own_count], outputs[:own_count]
    ride_start, ride_end = ride(
        here, kinds, inputs[own_count:] + outputs[own_count:] + sems[len(sems) - 2 * along :]
    )
    local_sem, send, recv, core_send, core_recv = sems[:5]
    spans = spans_of(given[0].shape[1], n, shares)
    parts = [(k, p) for k in range(total) for p in range(n) if spans[p][1]]

    def block(k, e, p, s_of):
        return made[k].at[s_of, here.other(e), :, pl.ds(*spans[p])]

    def source(k, e, p):
        return block(k, e, p, s) if e else given[k].at[:, pl.ds(*spans[p])]

    def deliver(k, p, m):
        t = m.bit_length() - 1
        held = here.dims(p, m - 2**t)
        where = here.toward(2 ** ((p + t) % n))
        return remote(source(k, held, p), block(k, held, p, s), send.at[k, p, m], recv.at[k, p, m], where)

    def core(k, p, m):
        held = here.dims(p, m)
        sems = core_send.at[k, p, m], core_recv.at[k, p, m]
        return remote(source(k, held, p), block(k, held, p, s), *sems, {"section": 1 - s})

    if layer is None:
        here.meet([here.names(2**d) for d in range(n)] + [("section",)] + rider_peers(here, kinds))
    else:
        blocks, small = given[total : total + 2], given[total + 2]
        rows, own_small = made[total : total + 2], made[total + 2]
        lands = [rows[i].at[q, chip] for i in range(2)]
        piece_send, piece_recv, q_send, q_recv, small_send, small_recv = sems[5:11]
        peers = [here.names(e) + extra for e in range(count) for extra in ((), ("section",)) if e or extra]
        here.meet(peers + [("q",), ("q", "section")])

        def piece(i, r, e):
            where = dict(here.toward(e), **({"section": 1 - s} if r else {}))
            src = blocks[i].at[1 - s if r else s, here.other(e)]
            return remote(src, lands[i], piece_send.at[i, r, e], piece_recv.at[i, e], where)

        def pass_on(i, e):
            place = rows[i].at[q, here.other(e)]
            return remote(place, place, q_send.at[i, e], q_recv.at[i, e], {"q": 1 - q})

        def hand_small(k, where):
            return remote(small, own_small, small_send.at[k], small_recv, where)

        keep_pieces = [pltpu.make_async_copy(blocks[i].at[s, chip], lands[i], piece_recv.at[i, 0]) for i in range(2)]
        keep_small = pltpu.make_async_copy(small, own_small, small_recv)
        at_layer = s == layer
        stays, leaves = jnp.logical_and(at_layer, q == s), jnp.logical_and(at_layer, q != s)

        @pl.when(at_layer)
        def _():
            for i in range(2):
                keep_pieces[i].start()
                for e in range(count):
                    for r in range(2):
                        if e or r:
                            piece(i, r, e).start()

        @pl.when(stays)
        def _():
            keep_small.start()
            hand_small(0, {"q": 1 - q}).start()

        @pl.when(leaves)
        def _():
            hand_small(0, {"section": 1 - s}).start()
            hand_small(1, {"section": 1 - s, "q": 1 - q}).start()

    own = [pltpu.make_async_copy(given[k], made[k].at[s, chip], local_sem.at[k]) for k in range(total)]
    for k in range(total):
        for t in range(n):
            for p in range(n):
                if spans[p][1]:
                    deliver(k, p, 2**t).start()
        own[k].start()
    ride_start()
    for k, p in parts:
        core(k, p, 0).start()
    for m in range(1, count):
        if layer is not None and m < 3:
            for e in range(count):
                arrived(rows[m - 1].at[q, here.other(e)], piece_recv.at[m - 1, e])
                pass_on(m - 1, e).start()
        for k, p in parts:
            arrived(block(k, here.dims(p, m), p, s), recv.at[k, p, m])
            for t in range(m.bit_length(), n):
                deliver(k, p, m + 2**t).start()
            core(k, p, m).start()
    for copy in own:
        copy.wait()
    for m in range(count):
        for k, p in parts:
            arrived(block(k, here.dims(p, m), p, 1 - s), core_recv.at[k, p, m])
    for m in range(count):
        for k, p in parts:
            core(k, p, m).wait_send()
            if m:
                deliver(k, p, m).wait_send()
    ride_end()
    if layer is not None:
        arrived(own_small, small_recv)
        for i in range(2):
            for e in range(count):
                arrived(rows[i].at[1 - q, here.other(e)], q_recv.at[i, e])
                pass_on(i, e).wait_send()

        @pl.when(at_layer)
        def _():
            for i in range(2):
                for e in range(count):
                    for r in range(2):
                        if e or r:
                            piece(i, r, e).wait_send()

        pl.when(stays)(lambda: hand_small(0, {"q": 1 - q}).wait_send())

        @pl.when(leaves)
        def _():
            hand_small(0, {"section": 1 - s}).wait_send()
            hand_small(1, {"section": 1 - s, "q": 1 - q}).wait_send()


def gather_call(bits, cid, shards, layer=None, extras=(), riders=(), shares=None, us=35):
    rows, width = shards[0].shape
    n = len(bits)
    count = 2**n
    dma = pltpu.SemaphoreType.DMA
    sems = dma((len(shards), n, count))
    shapes = [jax.ShapeDtypeStruct((2, count, rows, width), shard.dtype) for shard in shards]
    scratch = [dma((len(shards),)), sems, sems, sems, sems]
    if layer is not None:
        shapes += [jax.ShapeDtypeStruct(extra.shape, extra.dtype) for extra in extras]
        scratch += [dma((2, 2, count)), dma((2, count)), dma((2, count)), dma((2, count)), dma((2,)), dma]
    arrays, more_shapes, more_scratch = rider_shapes(bits, riders)
    shapes += more_shapes
    out = pl.pallas_call(
        functools.partial(gather_kernel, bits, len(shards), layer, tuple(kind for kind, _ in riders), shares),
        out_shape=shapes,
        in_specs=[pl.BlockSpec(memory_space=pl.ANY)] * len(shapes),
        out_specs=[pl.BlockSpec(memory_space=pl.ANY)] * len(shapes),
        scratch_shapes=scratch + more_scratch,
        compiler_params=pltpu.CompilerParams(collective_id=cid, has_side_effects=True),
        cost_estimate=lasting(us),
    )(*shards, *extras, *arrays)
    return [o.reshape((-1, width)) for o in out[: len(shards)]] + list(out[len(shards) :])


def add_rows(place, terms, out=None):
    step = 32
    out = place if out is None else out

    @pl.loop(0, place.shape[0] // step)
    def _(r):
        lines = pl.ds(pl.multiple_of(r * step, step), step)
        total = place[lines, :].astype(F32)
        for term in terms:
            total = total + term[lines, :].astype(F32)
        out[lines, :] = total.astype(out.dtype)


class Scatter:
    def __init__(self, here, turned, shares, a_refs, b_refs, out_ref, scratch):
        self.here, self.turned, self.a_refs, self.b_refs, self.out_ref = here, turned, a_refs, b_refs, out_ref
        self.mine, self.give, self.core_in, self.landed, self.core_send, self.core_recv, self.send, self.recv = scratch
        self.rows, self.width = out_ref.shape
        self.spans = spans_of(self.width, here.n, shares)
        self.parts = [p for p in range(here.n) if self.spans[p][1]]
        self.peers = [here.names(2**d) for d in range(here.n)] + [("section",)]

    def core(self, chip):
        sems = self.core_send.at[chip], self.core_recv.at[chip]
        return remote(self.give.at[chip], self.core_in.at[chip], *sems, {"section": 1 - self.here.s})

    def hand(self, p, m, t):
        n = self.here.n
        e = sum(2 ** ((p + u) % n) * (m // 2**u % 2) for u in range(n))
        cols = pl.ds(*self.spans[p])
        return remote(
            self.mine.at[self.here.other(e), :, cols], self.landed.at[m, :, cols], self.send.at[p, m], self.recv.at[p, m],
            self.here.toward(2 ** ((p + t) % n)),
        )

    def produce(self, low, high):
        here, rows, width = self.here, self.rows, self.width
        s, n, count = here.s, here.n, here.count
        tile = min(width, 512)

        @pl.loop(low, high)
        def _(i):
            @pl.when(i < count)
            def _():
                chip = here.other(count - 1 - i)

                def lines(s_of):
                    return pl.ds(pl.multiple_of((s_of * count + chip) * rows, rows), rows)

                lefts = [jnp.concatenate([a[lines(1 - s), :], a[lines(s), :]], axis=0) for a in self.a_refs]
                for c in range(0, width, tile):
                    if self.turned:
                        values = [back_dot(left, b[c : c + tile, :]) for left, b in zip(lefts, self.b_refs)]
                    else:
                        values = [forward_dot(left, b[:, c : c + tile]) for left, b in zip(lefts, self.b_refs)]
                    value = functools.reduce(jnp.add, values).astype(BF)
                    self.give[chip, :, c : c + tile] = value[:rows]
                    self.mine[chip, :, c : c + tile] = value[rows:]
                self.core(chip).start()

            @pl.when(i > 0)
            def _():
                e = count - i
                chip = here.other(e)
                arrived(self.core_in.at[chip], self.core_recv.at[chip])
                add_rows(self.mine.at[chip], [self.core_in.at[chip]])
                for p in self.parts:
                    pl.when(e // 2 ** ((p + n - 1) % n) % 2 == 1)(
                        lambda p=p: self.hand(p, here.positions(p, e), n - 1).start()
                    )

    def waiting(self, p, m):
        cols = pl.ds(*self.spans[p])
        terms = [m + 2**t for t in range(m.bit_length(), self.here.n)]
        for term in terms:
            arrived(self.landed.at[term, :, cols], self.recv.at[p, term])
        place = self.mine.at[self.here.other(self.here.dims(p, m)), :, cols]
        return place, [self.landed.at[term, :, cols] for term in terms]

    def pass_on(self, m):
        for p in self.parts:
            add_rows(*self.waiting(p, m))
            self.hand(p, m, m.bit_length() - 1).start()

    def settle(self):
        for p in self.parts:
            place, terms = self.waiting(p, 0)
            add_rows(place, terms, self.out_ref.at[:, pl.ds(*self.spans[p])])

    def drain(self):
        for chip in range(self.here.count):
            self.core(chip).wait_send()
        for m in range(1, self.here.count):
            for p in self.parts:
                self.hand(p, m, m.bit_length() - 1).wait_send()


def scatter_scratch(bits, block):
    n, count = len(bits), 2 ** len(bits)
    dma = pltpu.SemaphoreType.DMA
    return [pltpu.VMEM((count,) + block, BF)] * 4 + [dma((count,))] * 2 + [dma((n, count))] * 2


def scatter_kernel(bits, turned, homing, kinds, shares, terms, *refs):
    here = Place(bits)
    s, count = here.s, here.count
    along = len(kinds)
    a_refs, b_refs, refs = refs[:terms], refs[terms : 2 * terms], refs[2 * terms :]
    if homing:
        grad, refs = refs[0], refs[1:]
    rider_in, refs = refs[:along], refs[along:]
    out_ref, refs = refs[0], refs[1:]
    if homing:
        home, other_home = refs[:2]
        refs = refs[2:]
    rider_out, refs = refs[:along], refs[along:]
    work = Scatter(here, turned, shares, a_refs, b_refs, out_ref, refs[:8])
    if homing:
        q_in, ready, q_send, q_recv, home_send, home_recv, over_send, over_recv = refs[8:16]
    ride_start, ride_end = ride(here, kinds, rider_in + rider_out + refs[len(refs) - 2 * along :])

    def to_q(e):
        q, chip = lax.axis_index("q"), here.other(e)
        return remote(grad.at[1 - q, chip], q_in.at[chip], q_send.at[e], q_recv.at[e], {"q": 1 - q})

    def to_chip(e):
        return remote(ready.at[here.other(e)], home.at[here.other(0)], home_send.at[e], home_recv.at[e], here.toward(e))

    def to_core(e):
        chip = here.other(e)
        return remote(home.at[chip], other_home.at[chip], over_send.at[e], over_recv.at[e], {"section": 1 - s})

    def home_step(e):
        chip = here.other(e)
        arrived(q_in.at[chip], q_recv.at[e])
        place = ready.at[chip] if e else home.at[chip]
        add_rows(q_in.at[chip], [grad.at[lax.axis_index("q"), chip]], place)
        (to_chip(e) if e else to_core(0)).start()

    def home_end(e):
        if e:
            arrived(home.at[here.other(e)], home_recv.at[e])
            to_core(e).start()

    peers = work.peers
    if homing:
        peers = [here.names(e) for e in range(1, count)] + [("section",), ("q",)]
    here.meet(peers + rider_peers(here, kinds))
    if homing:
        for e in range(count):
            to_q(e).start()
    ride_start()
    work.produce(0, count + 1)
    steps = count // 2
    for m in range(steps - 1, 0, -1):
        if homing:
            home_step(steps - 1 - m)
        work.pass_on(m)
    work.settle()
    if homing:
        for e in range(steps - 1, count):
            home_step(e)
        for e in range(count):
            home_end(e)
        for e in range(count):
            arrived(other_home.at[here.other(e)], over_recv.at[e])
            to_core(e).wait_send()
            to_q(e).wait_send()
            if e:
                to_chip(e).wait_send()
    ride_end()
    work.drain()


def scatter_columns(bits, cid, a, b, turned, grad=None, riders=(), shares=None):
    tokens, width = a[0].shape[0], b[0].shape[0 if turned else 1]
    count = 2 ** len(bits)
    block = (tokens // (2 * count), width)
    dma = pltpu.SemaphoreType.DMA
    operands = list(a) + list(b)
    shapes = [jax.ShapeDtypeStruct(block, F32)]
    scratch = scatter_scratch(bits, block)
    if grad is not None:
        operands += [grad]
        shapes += [jax.ShapeDtypeStruct(grad.shape[1:], BF)] * 2
        scratch += [pltpu.VMEM(grad.shape[1:], BF)] * 2 + [dma((count,))] * 6
    arrays, more_shapes, more_scratch = rider_shapes(bits, riders)
    inside, outside = pl.BlockSpec(memory_space=pltpu.VMEM), pl.BlockSpec(memory_space=pl.ANY)
    return pl.pallas_call(
        functools.partial(
            scatter_kernel, bits, turned, grad is not None, tuple(kind for kind, _ in riders), shares, len(a)
        ),
        out_shape=shapes + more_shapes,
        in_specs=[inside] * len(operands) + [outside] * len(arrays),
        out_specs=[inside] * len(shapes) + [outside] * len(arrays),
        scratch_shapes=scratch + more_scratch,
        compiler_params=pltpu.CompilerParams(
            collective_id=cid, has_side_effects=True, vmem_limit_bytes=56 * 2**20
        ),
        cost_estimate=lasting(40 if grad is None else 60),
    )(*operands, *arrays)


def scatter_dot(bits, cid, a, b, turned, grad=None, riders=(), shares=None):
    tokens, width = a[0].shape[0], b[0].shape[0 if turned else 1]
    pieces = max(1, tokens * width // 2**22)
    size = width // pieces
    cuts = [
        [f[i * size : (i + 1) * size] if turned else f[:, i * size : (i + 1) * size] for f in b] for i in range(pieces)
    ]
    first = scatter_columns(bits, cid, a, cuts[0], turned, grad, riders, shares)
    rest = [scatter_columns(bits, 14 + turned, a, cut, turned)[0] for cut in cuts[1:]]
    return [jnp.concatenate([first[0]] + rest, axis=1)] + list(first[1:])


def total_kernel(bits, kinds, x_ref, *refs):
    here = Place(bits)
    s, count = here.s, here.count
    along = len(kinds)
    rider_in, out_ref, rider_out, refs = refs[:along], refs[along], refs[along + 1 : 2 * along + 1], refs[2 * along + 1 :]
    part, core_in, ready, landed, done, pair_send, pair_recv, send, recv, back_send, back_recv = refs[:11]
    ride_start, ride_end = ride(here, kinds, rider_in + rider_out + refs[11:])
    lanes = part.shape[3]

    def span(s_of, chip):
        at = (s_of * count + chip) * lanes
        return slice(at, at + lanes)

    for s_of in range(2):
        for chip in range(count):
            part[s_of, chip] = x_ref[:, span(s_of, chip)]
    here.meet([here.names(e) for e in range(1, count)] + [("section",)] + rider_peers(here, kinds))
    first = remote(part.at[1 - s], core_in, pair_send.at[0], pair_recv.at[0], {"section": 1 - s})
    first.start()
    first.wait_recv()
    for chip in range(count):
        total = part[s, chip] + core_in[chip]
        part[s, chip] = total
        ready[chip] = total.astype(BF)

    def out(e):
        return remote(ready.at[here.other(e)], landed.at[e], send.at[e], recv.at[e], here.toward(e))

    def back(e):
        place = done.at[s, here.other(0)]
        return remote(place, place, back_send.at[e], back_recv.at[e], here.toward(e))

    others = range(1, count)
    for e in others:
        out(e).start()
    ride_start()
    total = part[s, here.other(0)]
    for e in others:
        out(e).wait_recv()
        total = total + landed[e].astype(F32)
    done[s, here.other(0)] = total.astype(BF)
    for e in others:
        back(e).start()
    for e in others:
        place = done.at[s, here.other(e)]
        arrived(place, back_recv.at[e])
    last = remote(done.at[s], done.at[s], pair_send.at[1], pair_recv.at[1], {"section": 1 - s})
    last.start()
    last.wait_recv()
    for s_of in range(2):
        for chip in range(count):
            out_ref[:, span(s_of, chip)] = done[s_of, chip]
    ride_end()
    first.wait_send()
    last.wait_send()
    for e in others:
        out(e).wait_send()
        back(e).wait_send()


def sum_columns(bits, cid, x, riders=()):
    rows, tokens = x.shape
    count = 2 ** len(bits)
    block = (rows, tokens // (2 * count))
    dma, vmem = pltpu.SemaphoreType.DMA, pltpu.VMEM
    arrays, more_shapes, more_scratch = rider_shapes(bits, riders)
    inside, outside = pl.BlockSpec(memory_space=pltpu.VMEM), pl.BlockSpec(memory_space=pl.ANY)
    return pl.pallas_call(
        functools.partial(total_kernel, bits, tuple(kind for kind, _ in riders)),
        out_shape=[jax.ShapeDtypeStruct((rows, tokens), BF)] + more_shapes,
        in_specs=[inside] + [outside] * len(arrays),
        out_specs=[inside] + [outside] * len(arrays),
        scratch_shapes=[
            vmem((2, count) + block, F32),
            vmem((count,) + block, F32),
            vmem((count,) + block, BF),
            vmem((count,) + block, BF),
            vmem((2, count) + block, BF),
        ]
        + [dma((2,))] * 2
        + [dma((count,))] * 4
        + more_scratch,
        compiler_params=pltpu.CompilerParams(
            collective_id=cid, has_side_effects=True, vmem_limit_bytes=56 * 2**20
        ),
        cost_estimate=lasting(22),
    )(x, *arrays)


def spread_kernel(bits, kinds, shard_ref, *refs):
    here = Place(bits)
    along = len(kinds)
    rider_in, out_ref, rider_out, refs = refs[:along], refs[along], refs[along + 1 : 2 * along + 1], refs[2 * along + 1 :]
    send, recv, pair_send, pair_recv = refs[:4]
    ride_start, ride_end = ride(here, kinds, rider_in + rider_out + refs[4:])
    s, q, chip = here.s, lax.axis_index("q"), here.other(0)
    others = range(1, here.count)
    here.meet([here.names(e) for e in others] + [("section",), ("q",)])
    out_ref[s, q, chip] = shard_ref[...]
    own = out_ref.at[s, q, chip]
    copies = [remote(own, own, send.at[e], recv.at[e], here.toward(e)) for e in others]
    for copy in copies:
        copy.start()
    ride_start()
    for e in others:
        arrived(out_ref.at[s, q, here.other(e)], recv.at[e])
    place = out_ref.at[s, q]
    first = remote(place, place, pair_send.at[0], pair_recv.at[0], {"q": 1 - q})
    first.start()
    first.wait_recv()
    place = out_ref.at[s]
    second = remote(place, place, pair_send.at[1], pair_recv.at[1], {"section": 1 - s})
    second.start()
    second.wait_recv()
    ride_end()
    for copy in copies + [first, second]:
        copy.wait_send()


def spread(bits, shard, riders):
    arrays, more_shapes, more_scratch = rider_shapes(bits, riders)
    outside = [pl.BlockSpec(memory_space=pl.ANY)] * len(arrays)
    width, count = shard.shape[0], 2 ** len(bits)
    block = (16, max(width, 128))
    padded = jnp.pad(shard[None, :], ((0, block[0] - 1), (0, block[1] - width)))
    dma = pltpu.SemaphoreType.DMA
    out, *gots = pl.pallas_call(
        functools.partial(spread_kernel, bits, tuple(kind for kind, _ in riders)),
        out_shape=[jax.ShapeDtypeStruct((2, 2, count) + block, shard.dtype)] + more_shapes,
        in_specs=[pl.BlockSpec(memory_space=pltpu.VMEM)] + outside,
        out_specs=[pl.BlockSpec(memory_space=pltpu.VMEM)] + outside,
        scratch_shapes=[dma((count,)), dma((count,)), dma((2,)), dma((2,))] + more_scratch,
        compiler_params=pltpu.CompilerParams(collective_id=0, has_side_effects=True),
        cost_estimate=lasting(12),
    )(padded, *arrays)
    return [out[:, :, :, 0, :width].reshape((2, -1))] + gots


def chips(bits):
    return tuple(reversed(bits))


def at_home():
    return lax.axis_index("q") == lax.axis_index("section")


def low_first(mine, other):
    low = lax.axis_index("q") == 0
    return jnp.stack([jnp.where(low, mine, other), jnp.where(low, other, mine)])


def by_q(pair):
    low = lax.axis_index("q") == 0
    return jnp.where(low, pair[0], pair[1]), jnp.where(low, pair[1], pair[0])


def leave(value):
    return lax.ppermute(value, ("section", "q"), [(0, 1), (3, 2)])


def home(value):
    return lax.ppermute(value, ("section", "q"), [(1, 0), (2, 3)])


def swap(value):
    return lax.ppermute(value, "q", [(0, 1), (1, 0)])


def after(value, *earlier):
    return lax.optimization_barrier((value,) + earlier)[0]


def column_blocks(bits, rows):
    parts = rows.reshape((rows.shape[0], 2, 2, 2 ** len(bits), -1))
    return [jnp.transpose(parts[:, i], (1, 2, 0, 3)) for i in range(2)]


def assemble_kernel(lower_refs, upper_refs, weight_ref, out_ref, gain_ref):
    depth = weight_ref.shape[0]
    step = min(depth, 32)

    def fill(parts):
        chips, _, wide = parts[0].shape

        @pl.loop(0, depth // step)
        def _(r):
            lines = pl.ds(pl.multiple_of(r * step, step), step)
            total = jnp.zeros((step, wide), F32)
            for i, part in enumerate(parts):
                for chip in range(chips):
                    at = (i * chips + chip) * wide
                    value = part[chip, lines, :].astype(F32)
                    out_ref[lines, at : at + wide] = value
                    total = total + value * weight_ref[lines, at : at + wide].astype(F32)
            gain_ref[lines, :] = jnp.sum(total, axis=1, keepdims=True)

    upper = lax.axis_index("section") == 1
    pl.when(jnp.logical_not(upper))(lambda: fill(lower_refs))
    pl.when(upper)(lambda: fill(upper_refs))


def assemble(lower, upper, weight):
    inside = pl.BlockSpec(memory_space=pltpu.VMEM)
    return pl.pallas_call(
        assemble_kernel,
        out_shape=[jax.ShapeDtypeStruct(weight.shape, F32), jax.ShapeDtypeStruct((weight.shape[0], 1), F32)],
        in_specs=[[inside] * 4, [inside] * 4, inside],
        out_specs=[inside, inside],
        compiler_params=pltpu.CompilerParams(vmem_limit_bytes=40 * 2**20),
    )(lower, upper, weight)


def silu_slope(v):
    gate = jax.nn.sigmoid(v)
    return gate, gate * (1.0 + v * (1.0 - gate))


def normalize(stream, gain):
    inverse = lax.rsqrt(jnp.mean(stream * stream, axis=-1, keepdims=True) + norm_eps)
    return inverse, (stream * inverse * gain[None, :]).astype(BF)


class Small:
    def __init__(self, packed):
        self.taps = packed[:KC].astype(F32)
        self.conv_bias = packed[KC].astype(F32)
        self.dt_bias = packed[KC + 1].astype(F32)
        self.skip = packed[KC + 2].astype(F32)
        self.dt = packed[KC + 3 : KC + 3 + R]
        self.xproj = packed[KC + 3 + R : KC + 3 + 2 * R + 2 * N]


def mixer_inputs(normed, in_inner, small):
    inner = forward_dot(normed, in_inner).astype(BF).astype(F32)
    tokens, channels = inner.shape
    extended = jnp.concatenate([jnp.zeros((KC - 1, channels), F32), inner], axis=0)
    conv = jnp.broadcast_to(small.conv_bias[None, :], (tokens, channels))
    for tap in range(KC):
        conv = conv + small.taps[tap][None, :] * extended[tap : tap + tokens]
    act = jax.nn.silu(conv)
    return extended, conv, act, back_dot(small.xproj, act.astype(BF))


def mixer(xproj, act, normed, in_gate, small):
    gate_in = forward_dot(normed, in_gate).astype(BF).astype(F32)
    key_t, query_t = xproj[R : R + N].astype(F32), xproj[R + N :].astype(F32)
    key_norm = jnp.sum(key_t * key_t, axis=0)[:, None]
    write = jax.nn.sigmoid(cross_dot(xproj[:R], small.dt) + small.dt_bias[None, :])
    rate = write / (1.0 + write * key_norm)
    recur, before, last = recur_forward(rate, act, key_t, query_t)
    recur = recur + small.skip[None, :] * act
    gated = (recur * jax.nn.silu(gate_in)).astype(BF)
    return gate_in, key_t, query_t, key_norm, write, rate, recur, gated, before, last


def gate_back(grad_low, out_weight, kept):
    gate_in, recur = kept[0], kept[6]
    d_gated = back_dot(grad_low, out_weight).astype(BF).astype(F32)
    gate, slope = silu_slope(gate_in)
    return d_gated * (gate_in * gate), (d_gated * recur * slope).astype(BF)


def mixer_back(bits, cid, d_recur, act, xproj, kept, small, riders, product=(), shares=None):
    key_t, query_t, key_norm, write, rate, recur, gated, before, last = kept[1:]
    d_skip = jnp.sum(d_recur * act, axis=0)
    d_rate, d_act_rec, d_key_t, d_query_t, *gots = recur_backward(
        bits, cid, rate, act, d_recur, key_t, query_t, before, last, riders, product, shares
    )
    share = 1.0 / (1.0 + write * key_norm)
    pulled = d_rate * share * share
    d_pre = pulled * write * (1.0 - write)
    d_key_rate = -2.0 * key_t * jnp.sum(pulled * write * write, axis=1)[None, :]
    d_dt_bias = jnp.sum(d_pre, axis=0)
    d_delta = d_pre.astype(BF)
    d_dt = forward_dot(xproj[:R], d_delta)
    d_xproj = jnp.concatenate([back_dot(small.dt, d_delta), d_key_t + d_key_rate, d_query_t], axis=0)
    return d_act_rec, d_xproj, (d_dt_bias[None], d_skip[None], d_dt), gots


def inputs_back(d_xproj, d_recur, d_act_rec, extended, conv, act, small):
    tokens = act.shape[0]
    d_act = cross_dot(d_xproj, small.xproj) + small.skip[None, :] * d_recur + d_act_rec
    d_conv = d_act * silu_slope(conv)[1]
    d_taps = jnp.stack([jnp.sum(d_conv * extended[tap : tap + tokens], axis=0) for tap in range(KC)])
    d_bias = jnp.sum(d_conv, axis=0)
    later = jnp.concatenate([d_conv, jnp.zeros((KC - 1, d_conv.shape[1]), F32)], axis=0)
    d_inner = sum(small.taps[tap][None, :] * later[KC - 1 - tap : KC - 1 - tap + tokens] for tap in range(KC))
    return d_inner.astype(BF), (d_taps, d_bias[None]), forward_dot(d_xproj, act.astype(BF))


def norm_back(grad_out, d_normed, stream, inverse, gain):
    scaled = gain[None, :] * d_normed
    mean = jnp.mean(stream * scaled, axis=-1, keepdims=True)
    return grad_out + inverse * scaled - stream * inverse**3 * mean


def pack(first, second, third):
    packed = jnp.concatenate(first + second + (third,), axis=0)
    return jnp.pad(packed, ((0, -packed.shape[0] % 16), (0, 0)))


def on_device(
    bits, hidden_in, cotangent, norm_gain, in_weight, conv_weight, conv_bias, xproj_weight, dt_weight, dt_bias, skip_gain, out_weight
):
    packed = pack(
        (conv_weight[0], conv_bias),
        (dt_bias, skip_gain, dt_weight[0]),
        jnp.swapaxes(xproj_weight[0], 0, 1),
    )
    blocks = column_blocks(bits, in_weight[0])
    tight = (2, 5, 9)

    def weight(pair):
        return pair.reshape((-1, pair.shape[-1]))

    def weight_grad(normed, d_out):
        return cross_dot(normed, d_out).astype(BF).reshape((2,) + blocks[0].shape[1:])

    mine, others = by_q(hidden_in)
    gains, got = spread(bits, norm_gain[0], [("leave", others)])
    gains = gains.astype(F32)
    stream0 = jnp.where(at_home(), mine, got).astype(F32)

    inverse0, normed = normalize(stream0, gains[0])
    normed0, inner, gate, packed0, *sent = gather_call(
        bits, 1, [normed], 0, (*blocks, packed), shares=tight, us=60,
        riders=[("over_at", b) for b in blocks] + [("out1", packed)] + [("out%d" % l, out_weight[0]) for l in range(2)],
    )
    upper = lax.axis_index("section") == 1
    columns = [jnp.where(upper, b[1], got) for b, got in zip(blocks, sent)]
    packed_held = jnp.where(upper, packed, sent[2])
    out_held = jnp.where(upper, sent[3], out_weight[0]), jnp.where(upper, out_weight[0], sent[4])
    inner0, small0 = weight(inner), Small(packed0)
    extended0, conv0, act0, part = mixer_inputs(normed0, inner0, small0)
    part = after(part, out_held[0])
    xproj0, inner, late_gate = sum_columns(bits, 4, part, [("cube", columns[0]), ("cube", columns[1])])
    gate0 = weight(gate)
    out0 = jnp.where(at_home(), out_held[0], leave(after(out_held[0], xproj0)))
    kept0 = mixer(xproj0, act0, normed0, gate0, small0)
    grad_mine, grad_others = by_q(cotangent)
    added, got, grad_got = scatter_dot(
        bits, 8, [kept0[7]], [out0], False, riders=[("leave", packed_held), ("leave", grad_others.astype(BF))]
    )
    grad1 = jnp.where(at_home(), grad_mine, grad_got.astype(F32))
    small1 = Small(jnp.where(at_home(), packed_held, got))
    output0 = (stream0 + added).astype(BF)

    stream1 = output0.astype(F32)
    inverse1, normed = normalize(stream1, gains[1])
    normed1, grad_low1, inner, output0_home = gather_call(
        bits, 2, [normed, grad1.astype(BF)], riders=[("stack", inner), ("home", output0)], shares=(3, 5, 8), us=65
    )
    inner1 = weight(inner)
    extended1, conv1, act1, part = mixer_inputs(normed1, inner1, small1)
    xproj1, gate = sum_columns(bits, 5, after(part, out_held[1]), [("stack", late_gate)])
    gate1 = weight(gate)
    out1 = jnp.where(at_home(), out_held[1], leave(after(out_held[1], xproj1)))
    kept1 = mixer(xproj1, act1, normed1, gate1, small1)

    d_out1 = cross_dot(kept1[7], grad_low1)
    d_recur, d_gate1 = gate_back(grad_low1, out1, kept1)
    keep, give = by_q(weight_grad(normed1, d_gate1))
    beside = kept1[7].shape[0] * out1.shape[1] <= 2**22 and kept1[7].shape[0] >= 16 * BLOCK
    if beside:
        d_act_rec, part, d_small, (added, got) = mixer_back(
            bits, 16, d_recur, act1, xproj1, kept1, small1, [("swap", give)], (kept1[7], out1), (4, 5, 7)
        )
    else:
        (added,) = scatter_dot(bits, 10, [kept1[7]], [out1], False)
        d_act_rec, part, d_small, (got,) = mixer_back(bits, 16, d_recur, act1, xproj1, kept1, small1, [("swap", give)])
    output1 = (stream1 + added).astype(BF)
    d_xproj, output1_home = sum_columns(bits, 6, part, [("home", output1)])
    d_gate_in1 = (keep.astype(F32) + got.astype(F32)).astype(BF)
    d_inner, d_conv, d_xproj_weight = inputs_back(d_xproj, d_recur, d_act_rec, extended1, conv1, act1, small1)
    d_packed1 = pack(d_conv, d_small, d_xproj_weight)
    d_normed, d_gate_in1, d_packed1_home, d_out1_home = scatter_dot(
        bits, 11, [d_inner, d_gate1], [inner1, gate1], True,
        riders=[("cube", d_gate_in1), ("home", d_packed1.astype(BF)), ("home", d_out1.astype(BF))], shares=(4, 5, 7),
    )
    keep, give = by_q(weight_grad(normed1, d_inner))
    input_grad1 = norm_back(grad1, d_normed, stream1, inverse1, gains[1])
    grad0 = input_grad1.astype(BF)
    grad_low0, got, grad1_home = gather_call(
        bits, 3, [grad0], riders=[("swap", give), ("home", grad0)], shares=(3, 5, 8), us=45
    )
    d_inner1 = (keep.astype(F32) + got.astype(F32)).astype(BF)

    d_out0 = cross_dot(kept0[7], grad_low0)
    d_recur, d_gate0 = gate_back(grad_low0, out0, kept0)
    keep, give = by_q(weight_grad(normed0, d_gate0))
    d_act_rec, part, d_small, (got,) = mixer_back(bits, 17, d_recur, act0, xproj0, kept0, small0, [("swap", give)])
    d_gate_in0 = (keep.astype(F32) + got.astype(F32)).astype(BF)
    d_xproj, d_gate_in0, d_inner1, d_out0_home = sum_columns(
        bits, 7, part, [("cube", d_gate_in0), ("cube", d_inner1), ("home", d_out0.astype(BF))]
    )
    d_inner, d_conv, d_xproj_weight = inputs_back(d_xproj, d_recur, d_act_rec, extended0, conv0, act0, small0)
    d_packed0 = pack(d_conv, d_small, d_xproj_weight)
    d_out = [
        (mine + other.astype(F32)).astype(BF) for mine, other in ((d_out0, d_out0_home), (d_out1, d_out1_home))
    ]
    d_packed1 = (d_packed1 + d_packed1_home.astype(F32)).astype(BF)
    gate_over = jnp.where(upper, d_gate_in0, d_gate_in1)
    d_normed, d_inner0, d_inner0_other, d_packed0_home, inner_other, gate_other, *backs = scatter_dot(
        bits, 13, [d_inner, d_gate0], [inner0, gate0], True, weight_grad(normed0, d_inner), shares=(3, 5, 8),
        riders=[
            ("home", d_packed0.astype(BF)), ("over", d_inner1), ("over", gate_over), ("back0", d_out[0]), ("back1", d_out[1]),
            ("back1", d_packed1), ("back0", output0), ("back0", output0_home), ("back1", output1), ("back1", output1_home),
            ("back1", grad0), ("back1", grad1_home),
        ],
    )
    input_grad0 = norm_back(grad0.astype(F32), d_normed, stream0, inverse0, gains[0]).astype(BF)

    def settled(lower, upper_one, lower_back, upper_back):
        return jnp.where(at_home(), jnp.where(upper, upper_one, lower), jnp.where(upper, upper_back, lower_back))

    d_out = settled(*d_out, *backs[:2]).astype(F32)
    d_packed0 = (d_packed0 + d_packed0_home.astype(F32)).astype(BF)
    d_packed = settled(d_packed0, d_packed1, lax.ppermute(d_packed0, ("section", "q"), [(3, 1)]), backs[2]).astype(F32)
    low = lax.axis_index("q") == 0
    mine, other = settled(output0, output1, backs[3], backs[5]), settled(output0_home, output1_home, backs[4], backs[6])
    layer_outputs = low_first(mine, other).astype(F32)
    mine, other = jnp.where(at_home(), grad0, backs[7]), jnp.where(at_home(), grad1_home, backs[8])
    grads1 = low_first(mine, other)
    of_first = lax.ppermute(input_grad0, ("section", "q"), [(2, 1)])
    of_second = lax.ppermute(input_grad0, ("section", "q"), [(1, 0), (3, 1)])
    grads0 = jnp.stack([jnp.where(low, input_grad0, of_first), of_second])
    input_grads = jnp.where(upper, grads1, grads0).astype(F32)
    d_in, d_gain = assemble(
        [d_inner0, d_inner0_other, d_gate_in0, gate_other], [inner_other, d_inner1, gate_other, d_gate_in1], in_weight[0]
    )
    d_gain = d_gain[:, 0] / norm_gain[0].astype(F32)
    return (
        layer_outputs[None],
        input_grads[None],
        d_gain[None],
        d_in[None],
        d_packed[None, :KC],
        d_packed[None, KC],
        jnp.swapaxes(d_packed[KC + 3 + R : KC + 3 + 2 * R + 2 * N], 0, 1)[None],
        d_packed[None, KC + 3 : KC + 3 + R],
        d_packed[None, KC + 1],
        d_packed[None, KC + 2],
        d_out[None],
    )


def solution(mesh):
    sections, chip_count = mesh.devices.shape
    n = chip_count.bit_length() - 2
    bits = tuple("c%d" % d for d in range(n))
    split = Mesh(mesh.devices.reshape((sections,) + (2,) * (n + 1)), ("section", "q") + chips(bits))
    seq = ("q",) + chips(bits)
    placed = (
        P(None, seq, None),
        P(None, seq, None),
        P("section", seq),
        P("section", seq, None),
        P("section", None, seq),
        P("section", seq),
        P("section", seq, None),
        P("section", None, seq),
        P("section", seq),
        P("section", seq),
        P("section", seq, None),
    )
    return jax.shard_map(
        functools.partial(on_device, bits),
        mesh=split,
        in_specs=placed,
        out_specs=(P("section", None, seq, None), P("section", None, seq, None)) + placed[2:],
        check_vma=False,
    )
```

```python
import functools

import jax
import jax.numpy as jnp
from jax import lax
from jax.experimental import pallas as pl
from jax.experimental.pallas import tpu as pltpu
from jax.sharding import Mesh, PartitionSpec as P


N = 16
R = 128
KC = 4
BLOCK = 128
norm_eps = 1e-05
BF = jnp.bfloat16
F32 = jnp.float32
MESH = pl.DeviceIdType.MESH


def forward_dot(operand, factor):
    return jnp.dot(operand, factor, preferred_element_type=F32)


def cross_dot(operand, factor):
    return lax.dot_general(operand, factor, (((0,), (0,)), ((), ())), preferred_element_type=F32)


def back_dot(operand, factor):
    return lax.dot_general(operand, factor, (((1,), (1,)), ((), ())), preferred_element_type=F32)


def lasting(us):
    return pl.CostEstimate(flops=0, bytes_accessed=int(us * 3.4e6), transcendentals=0)


def widths(channels):
    wide = min(channels, 128)
    return wide, channels // wide


def sum_rows(pieces):
    row = lax.broadcasted_iota(jnp.int32, pieces[0].shape, 0)
    shift = 1
    while len(pieces) > 1:
        keep = (row & shift) == 0
        pieces = [
            jnp.where(keep, a, b) + pltpu.roll(jnp.where(keep, b, a), shift, 0)
            for a, b in zip(pieces[0::2], pieces[1::2])
        ]
        shift *= 2
    return pieces[0]


def halves(v):
    return v[:8] + v[8:]


def lanes_of(p, wide):
    return slice(p * wide, (p + 1) * wide)


def recur_forward_kernel(rate_ref, act_ref, key_ref, query_ref, out_ref, before_ref, last_ref, memory_ref):
    wide, parts = widths(rate_ref.shape[1])

    @pl.when(pl.program_id(0) == 0)
    def _():
        memory_ref[...] = jnp.zeros_like(memory_ref)

    memory = [memory_ref[:, lanes_of(p, wide)] for p in range(parts)]
    for base in range(0, rate_ref.shape[0], 8):
        rates = rate_ref[base : base + 8, :]
        feeds = rates * act_ref[base : base + 8, :]
        sums = [[] for _ in range(parts)]
        for i in range(8):
            key = jnp.broadcast_to(key_ref[:, base + i : base + i + 1], (N, wide))
            query = jnp.broadcast_to(query_ref[:, base + i : base + i + 1], (N, wide))
            square = key * key
            for p in range(parts):
                lanes = lanes_of(p, wide)
                before_ref[base + i, :, lanes] = memory[p]
                memory[p] = (1.0 - rates[i : i + 1, lanes] * square) * memory[p] + key * feeds[i : i + 1, lanes]
                sums[p].append(halves(memory[p] * query))
        for p in range(parts):
            out_ref[base : base + 8, lanes_of(p, wide)] = sum_rows(sums[p])
    for p in range(parts):
        memory_ref[:, lanes_of(p, wide)] = memory[p]

    @pl.when(pl.program_id(0) == pl.num_programs(0) - 1)
    def _():
        last_ref[...] = memory_ref[...]


def recur_forward(rate, act, key_t, query_t):
    tokens, channels = rate.shape
    rows = pl.BlockSpec((BLOCK, channels), lambda i: (i, 0))
    cols = pl.BlockSpec((N, BLOCK), lambda i: (0, i))
    return pl.pallas_call(
        recur_forward_kernel,
        grid=(tokens // BLOCK,),
        in_specs=[rows, rows, cols, cols],
        out_specs=[
            rows,
            pl.BlockSpec((BLOCK, N, channels), lambda i: (i, 0, 0)),
            pl.BlockSpec((N, channels), lambda i: (0, 0)),
        ],
        out_shape=[
            jax.ShapeDtypeStruct((tokens, channels), F32),
            jax.ShapeDtypeStruct((tokens, N, channels), F32),
            jax.ShapeDtypeStruct((N, channels), F32),
        ],
        scratch_shapes=[pltpu.VMEM((N, channels), F32)],
        compiler_params=pltpu.CompilerParams(
            dimension_semantics=("arbitrary",), vmem_limit_bytes=40 * 2**20
        ),
        cost_estimate=lasting(1),
    )(rate, act, key_t, query_t)


def recur_backward_kernel(bits, kinds, shares, steps, rate_ref, act_ref, grad_ref, key_ref, query_ref, before_ref, last_ref, *refs):
    along, beside = len(kinds), 1 if steps else 0
    product, refs = refs[: 2 * beside], refs[2 * beside :]
    rider_in, refs = refs[:along], refs[along:]
    d_rate_ref, d_act_ref, d_key_ref, d_query_ref = refs[:4]
    scattered, refs = refs[4 : 4 + beside], refs[4 + beside :]
    rider_out, refs = refs[:along], refs[along:]
    lam_ref, memory_ref, key_rows, query_rows = refs[:4]
    here = Place(bits)
    ride_start, ride_end = ride(here, kinds, rider_in + rider_out + refs[len(refs) - 2 * along :])
    stages = {}
    peers = rider_peers(here, kinds)
    if beside:
        work = Scatter(here, False, shares, product[:1], product[1:], scattered[0], refs[4:12])
        peers = peers + work.peers
        half = here.count // 2
        for k in range(half + 1):
            stages[k] = functools.partial(work.produce, 2 * k, min(2 * k + 2, here.count + 1))
        for k, m in enumerate(range(half - 1, 0, -1)):
            stages[steps - 1 - 2 * (half - 1 - k)] = functools.partial(work.pass_on, m)
    wide, parts = widths(rate_ref.shape[1])
    block = rate_ref.shape[0]

    @pl.when(pl.program_id(0) == 0)
    def _():
        here.meet(peers)
        ride_start()
        lam_ref[...] = jnp.zeros_like(lam_ref)
        memory_ref[...] = last_ref[...]

    for at, stage in stages.items():
        pl.when(pl.program_id(0) == at)(stage)
    lam = [lam_ref[:, lanes_of(p, wide)] for p in range(parts)]
    memory = [memory_ref[:, lanes_of(p, wide)] for p in range(parts)]
    for base in reversed(range(0, block, 8)):
        rates = rate_ref[base : base + 8, :]
        acts = act_ref[base : base + 8, :]
        grads = grad_ref[base : base + 8, :]
        d_rates = [[None] * 8 for _ in range(parts)]
        d_acts = [[None] * 8 for _ in range(parts)]
        for i in reversed(range(8)):
            at = base + i
            key = jnp.broadcast_to(key_ref[:, at : at + 1], (N, wide))
            query = jnp.broadcast_to(query_ref[:, at : at + 1], (N, wide))
            square = key * key
            key_sum = query_sum = None
            for p in range(parts):
                lanes = lanes_of(p, wide)
                grad = grads[i : i + 1, lanes]
                before = before_ref[at, :, lanes]
                pulled = query * grad + lam[p]
                kept = key * before
                missing = acts[i : i + 1, lanes] - kept
                keyed = pulled * key
                scaled = pulled * rates[i : i + 1, lanes]
                d_acts[p][i] = halves(keyed)
                d_rates[p][i] = halves(keyed * missing)
                to_key = scaled * (missing - kept)
                to_query = memory[p] * grad
                key_sum = to_key if key_sum is None else key_sum + to_key
                query_sum = to_query if query_sum is None else query_sum + to_query
                lam[p] = pulled - scaled * square
                memory[p] = before
            key_rows[at * N : (at + 1) * N, :] = key_sum.astype(BF)
            query_rows[at * N : (at + 1) * N, :] = query_sum.astype(BF)
        for p in range(parts):
            lanes = lanes_of(p, wide)
            d_rate_ref[base : base + 8, lanes] = sum_rows(d_rates[p])
            d_act_ref[base : base + 8, lanes] = rates[:, lanes] * sum_rows(d_acts[p])
    for p in range(parts):
        lam_ref[:, lanes_of(p, wide)] = lam[p]
        memory_ref[:, lanes_of(p, wide)] = memory[p]

    ones = jnp.ones((wide, block), BF)
    token = lax.broadcasted_iota(jnp.int32, (block, N, block), 0)
    own = token == lax.broadcasted_iota(jnp.int32, (block, N, block), 2)
    for rows, result in ((key_rows, d_key_ref), (query_rows, d_query_ref)):
        sums = forward_dot(rows[...], ones).reshape(block, N, block)
        result[...] = jnp.sum(jnp.where(own, sums, 0.0), axis=0)

    @pl.when(pl.program_id(0) == pl.num_programs(0) - 1)
    def _():
        if beside:
            work.settle()
            work.drain()
        ride_end()


def recur_backward(bits, cid, rate, act, grad, key_t, query_t, before, last, riders, product=(), shares=None):
    tokens, channels = rate.shape
    count = tokens // BLOCK
    rows = pl.BlockSpec((BLOCK, channels), lambda i: (count - 1 - i, 0))
    cols = pl.BlockSpec((N, BLOCK), lambda i: (0, count - 1 - i))
    products = pltpu.VMEM((BLOCK * N, widths(channels)[0]), BF)
    arrays, more_shapes, more_scratch = rider_shapes(bits, riders)
    outside = [pl.BlockSpec(memory_space=pl.ANY)] * len(arrays)
    inside = [pl.BlockSpec(memory_space=pltpu.VMEM)] * len(product)
    if product:
        block = (tokens // 2 ** (len(bits) + 1), product[1].shape[1])
        more_shapes = [jax.ShapeDtypeStruct(block, F32)] + more_shapes
        more_scratch = scatter_scratch(bits, block) + more_scratch
    return pl.pallas_call(
        functools.partial(
            recur_backward_kernel, bits, tuple(kind for kind, _ in riders), shares, count if product else 0
        ),
        grid=(count,),
        in_specs=[
            rows, rows, rows, cols, cols,
            pl.BlockSpec((BLOCK, N, channels), lambda i: (count - 1 - i, 0, 0)),
            pl.BlockSpec((N, channels), lambda i: (0, 0)),
        ] + inside + outside,
        out_specs=[rows, rows, cols, cols] + inside[:1] + outside,
        out_shape=[
            jax.ShapeDtypeStruct((tokens, channels), F32),
            jax.ShapeDtypeStruct((tokens, channels), F32),
            jax.ShapeDtypeStruct((N, tokens), F32),
            jax.ShapeDtypeStruct((N, tokens), F32),
        ] + more_shapes,
        scratch_shapes=[pltpu.VMEM((N, channels), F32), pltpu.VMEM((N, channels), F32), products, products]
        + more_scratch,
        compiler_params=pltpu.CompilerParams(
            dimension_semantics=("arbitrary",), vmem_limit_bytes=56 * 2**20, collective_id=cid, has_side_effects=True
        ),
        cost_estimate=lasting(1),
    )(rate, act, grad, key_t, query_t, before, last, *product, *arrays)


class Place:
    def __init__(self, bits):
        self.bits = bits
        self.n = len(bits)
        self.count = 2**self.n
        self.at = [lax.axis_index(name) for name in bits]
        self.s = lax.axis_index("section")

    def other(self, e):
        return sum(2**d * (c + e // 2**d % 2 * (1 - 2 * c)) for d, c in enumerate(self.at))

    def toward(self, e):
        return {self.bits[d]: 1 - self.at[d] for d in range(self.n) if e // 2**d % 2}

    def dims(self, p, m):
        return sum(2 ** ((p + t) % self.n) for t in range(self.n) if m // 2**t % 2)

    def positions(self, p, e):
        return sum(2**t * (e // 2 ** ((p + t) % self.n) % 2) for t in range(self.n))

    def names(self, e):
        return tuple(self.bits[d] for d in range(self.n) if e // 2**d % 2)

    def meet(self, peers):
        barrier = pltpu.get_barrier_semaphore()
        peers = list(dict.fromkeys(peers))
        for axes in peers:
            where = {name: 1 - lax.axis_index(name) for name in axes}
            pl.semaphore_signal(barrier, inc=1, device_id=where, device_id_type=MESH)
        pl.semaphore_wait(barrier, len(peers))


def spans_of(width, n, shares=None):
    tiles = width // 128
    sizes = [(tiles // n + (p < tiles % n)) * 128 for p in range(n)]
    if shares is not None and len(shares) == n and sum(shares) == tiles:
        sizes = [share * 128 for share in shares]
    return [(sum(sizes[:p]), size) for p, size in enumerate(sizes)]


def remote(src, dst, send, recv, where):
    return pltpu.make_async_remote_copy(
        src_ref=src, dst_ref=dst, send_sem=send, recv_sem=recv, device_id=where, device_id_type=MESH
    )


def arrived(place, sem):
    pltpu.make_async_copy(place, place, sem).wait()


def rider_peers(here, kinds):
    peers = [here.names(e) for e in range(1, here.count)] if "cube" in kinds else []
    if set(kinds) & {"swap", "stack", "home", "leave"}:
        peers.append(("q",))
    if set(kinds) & {"over", "over_at", "out0", "out1", "back0", "back1"}:
        peers.append(("section",))
    return peers


def ride(here, kinds, refs):
    k = len(kinds)
    riders = list(zip(kinds, refs[:k], refs[k : 2 * k], refs[2 * k : 3 * k], refs[3 * k :]))
    q, chip = lax.axis_index("q"), here.other(0)

    def copies(kind, src, dst, send, recv):
        if kind == "cube":
            return [
                remote(src.at[here.other(e)], dst.at[chip], send.at[e], recv.at[e], here.toward(e))
                for e in range(1, here.count)
            ]
        if kind in ("over", "over_at") or kind[:-1] in ("out", "back"):
            src = src.at[1 - here.s] if kind == "over_at" else src
            return [remote(src, dst, send.at[0], recv.at[0], {"section": 1 - here.s})]
        return [remote(src, dst.at[q] if kind == "stack" else dst, send.at[0], recv.at[0], {"q": 1 - q})]

    def when(kind, sending, do):
        if kind in ("home", "leave"):
            pl.when((q != here.s) if sending == (kind == "home") else (q == here.s))(do)
        elif kind[:-1] in ("out", "back"):
            at_layer = (here.s == int(kind[-1])) if sending == (kind[:-1] == "out") else (here.s != int(kind[-1]))
            away = (q != here.s) if sending == (kind[:-1] == "out") else (q == here.s)
            pl.when(jnp.logical_and(at_layer, away))(do)
        else:
            do()

    def start():
        for kind, src, dst, send, recv in riders:
            if kind == "cube":
                pltpu.make_async_copy(src.at[chip], dst.at[chip], recv.at[0]).start()
            if kind == "stack":
                pltpu.make_async_copy(src, dst.at[q], recv.at[1]).start()
            for copy in copies(kind, src, dst, send, recv):
                when(kind, True, copy.start)

    def finish():
        for kind, src, dst, send, recv in riders:
            if kind == "cube":
                for e in range(here.count):
                    arrived(dst.at[here.other(e)], recv.at[e])
            elif kind == "stack":
                arrived(dst.at[1 - q], recv.at[0])
                arrived(dst.at[q], recv.at[1])
            else:
                when(kind, False, lambda: arrived(dst, recv.at[0]))
            for copy in copies(kind, src, dst, send, recv):
                when(kind, True, copy.wait_send)

    return start, finish


def rider_shapes(bits, riders):
    sems = pltpu.SemaphoreType.DMA((2 ** len(bits),))
    shapes = [
        jax.ShapeDtypeStruct(
            array.shape[1:] if kind == "over_at" else ((2,) if kind == "stack" else ()) + array.shape, array.dtype
        )
        for kind, array in riders
    ]
    return [array for _, array in riders], shapes, [sems] * (2 * len(riders))


def gather_kernel(bits, total, kinds, shares, *refs):
    here = Place(bits)
    n, s, count = here.n, here.s, here.count
    chip, along = here.other(0), len(kinds)
    inputs, refs = refs[: total + along], refs[total + along :]
    outputs, sems = refs[: total + along], refs[total + along :]
    given, made = inputs[:total], outputs[:total]
    ride_start, ride_end = ride(here, kinds, inputs[total:] + outputs[total:] + sems[len(sems) - 2 * along :])
    local_sem, send, recv, core_send, core_recv = sems[:5]
    spans = spans_of(given[0].shape[1], n, shares)
    parts = [(k, p) for k in range(total) for p in range(n) if spans[p][1]]

    def block(k, e, p, s_of):
        return made[k].at[s_of, here.other(e), :, pl.ds(*spans[p])]

    def source(k, e, p):
        return block(k, e, p, s) if e else given[k].at[:, pl.ds(*spans[p])]

    def deliver(k, p, m):
        t = m.bit_length() - 1
        held = here.dims(p, m - 2**t)
        where = here.toward(2 ** ((p + t) % n))
        return remote(source(k, held, p), block(k, held, p, s), send.at[k, p, m], recv.at[k, p, m], where)

    def core(k, p, m):
        held = here.dims(p, m)
        sems = core_send.at[k, p, m], core_recv.at[k, p, m]
        return remote(source(k, held, p), block(k, held, p, s), *sems, {"section": 1 - s})

    here.meet([here.names(2**d) for d in range(n)] + [("section",)] + rider_peers(here, kinds))
    own = [pltpu.make_async_copy(given[k], made[k].at[s, chip], local_sem.at[k]) for k in range(total)]
    for k in range(total):
        for t in range(n):
            for p in range(n):
                if spans[p][1]:
                    deliver(k, p, 2**t).start()
        own[k].start()
    ride_start()
    for k, p in parts:
        core(k, p, 0).start()
    for m in range(1, count):
        for k, p in parts:
            arrived(block(k, here.dims(p, m), p, s), recv.at[k, p, m])
            for t in range(m.bit_length(), n):
                deliver(k, p, m + 2**t).start()
            core(k, p, m).start()
    for copy in own:
        copy.wait()
    for m in range(count):
        for k, p in parts:
            arrived(block(k, here.dims(p, m), p, 1 - s), core_recv.at[k, p, m])
    for m in range(count):
        for k, p in parts:
            core(k, p, m).wait_send()
            if m:
                deliver(k, p, m).wait_send()
    ride_end()


def gather_call(bits, cid, shards, riders=(), shares=None, us=35):
    rows, width = shards[0].shape
    n = len(bits)
    count = 2**n
    dma = pltpu.SemaphoreType.DMA
    sems = dma((len(shards), n, count))
    shapes = [jax.ShapeDtypeStruct((2, count, rows, width), shard.dtype) for shard in shards]
    scratch = [dma((len(shards),)), sems, sems, sems, sems]
    arrays, more_shapes, more_scratch = rider_shapes(bits, riders)
    shapes += more_shapes
    out = pl.pallas_call(
        functools.partial(gather_kernel, bits, len(shards), tuple(kind for kind, _ in riders), shares),
        out_shape=shapes,
        in_specs=[pl.BlockSpec(memory_space=pl.ANY)] * len(shapes),
        out_specs=[pl.BlockSpec(memory_space=pl.ANY)] * len(shapes),
        scratch_shapes=scratch + more_scratch,
        compiler_params=pltpu.CompilerParams(collective_id=cid, has_side_effects=True),
        cost_estimate=lasting(us),
    )(*shards, *arrays)
    return [o.reshape((-1, width)) for o in out[: len(shards)]] + list(out[len(shards) :])


def add_rows(place, terms, out=None):
    step = 32
    out = place if out is None else out

    @pl.loop(0, place.shape[0] // step)
    def _(r):
        lines = pl.ds(pl.multiple_of(r * step, step), step)
        total = place[lines, :].astype(F32)
        for term in terms:
            total = total + term[lines, :].astype(F32)
        out[lines, :] = total.astype(out.dtype)


class Scatter:
    def __init__(self, here, turned, shares, a_refs, b_refs, out_ref, scratch):
        self.here, self.turned, self.a_refs, self.b_refs, self.out_ref = here, turned, a_refs, b_refs, out_ref
        self.mine, self.give, self.core_in, self.landed, self.core_send, self.core_recv, self.send, self.recv = scratch
        self.rows, self.width = out_ref.shape
        self.spans = spans_of(self.width, here.n, shares)
        self.parts = [p for p in range(here.n) if self.spans[p][1]]
        self.peers = [here.names(2**d) for d in range(here.n)] + [("section",)]

    def core(self, chip):
        sems = self.core_send.at[chip], self.core_recv.at[chip]
        return remote(self.give.at[chip], self.core_in.at[chip], *sems, {"section": 1 - self.here.s})

    def hand(self, p, m, t):
        n = self.here.n
        e = sum(2 ** ((p + u) % n) * (m // 2**u % 2) for u in range(n))
        cols = pl.ds(*self.spans[p])
        return remote(
            self.mine.at[self.here.other(e), :, cols], self.landed.at[m, :, cols], self.send.at[p, m], self.recv.at[p, m],
            self.here.toward(2 ** ((p + t) % n)),
        )

    def produce(self, low, high):
        here, rows, width = self.here, self.rows, self.width
        s, n, count = here.s, here.n, here.count
        tile = min(width, 512)

        @pl.loop(low, high)
        def _(i):
            @pl.when(i < count)
            def _():
                chip = here.other(count - 1 - i)

                def lines(s_of):
                    return pl.ds(pl.multiple_of((s_of * count + chip) * rows, rows), rows)

                lefts = [jnp.concatenate([a[lines(1 - s), :], a[lines(s), :]], axis=0) for a in self.a_refs]
                for c in range(0, width, tile):
                    if self.turned:
                        values = [back_dot(left, b[c : c + tile, :]) for left, b in zip(lefts, self.b_refs)]
                    else:
                        values = [forward_dot(left, b[:, c : c + tile]) for left, b in zip(lefts, self.b_refs)]
                    value = functools.reduce(jnp.add, values).astype(BF)
                    self.give[chip, :, c : c + tile] = value[:rows]
                    self.mine[chip, :, c : c + tile] = value[rows:]
                self.core(chip).start()

            @pl.when(i > 0)
            def _():
                e = count - i
                chip = here.other(e)
                arrived(self.core_in.at[chip], self.core_recv.at[chip])
                add_rows(self.mine.at[chip], [self.core_in.at[chip]])
                for p in self.parts:
                    pl.when(e // 2 ** ((p + n - 1) % n) % 2 == 1)(
                        lambda p=p: self.hand(p, here.positions(p, e), n - 1).start()
                    )

    def waiting(self, p, m):
        cols = pl.ds(*self.spans[p])
        terms = [m + 2**t for t in range(m.bit_length(), self.here.n)]
        for term in terms:
            arrived(self.landed.at[term, :, cols], self.recv.at[p, term])
        place = self.mine.at[self.here.other(self.here.dims(p, m)), :, cols]
        return place, [self.landed.at[term, :, cols] for term in terms]

    def pass_on(self, m):
        for p in self.parts:
            add_rows(*self.waiting(p, m))
            self.hand(p, m, m.bit_length() - 1).start()

    def settle(self):
        for p in self.parts:
            place, terms = self.waiting(p, 0)
            add_rows(place, terms, self.out_ref.at[:, pl.ds(*self.spans[p])])

    def drain(self):
        for chip in range(self.here.count):
            self.core(chip).wait_send()
        for m in range(1, self.here.count):
            for p in self.parts:
                self.hand(p, m, m.bit_length() - 1).wait_send()


def scatter_scratch(bits, block):
    n, count = len(bits), 2 ** len(bits)
    dma = pltpu.SemaphoreType.DMA
    return [pltpu.VMEM((count,) + block, BF)] * 4 + [dma((count,))] * 2 + [dma((n, count))] * 2


def scatter_kernel(bits, turned, homing, kinds, shares, terms, *refs):
    here = Place(bits)
    s, count = here.s, here.count
    along = len(kinds)
    a_refs, b_refs, refs = refs[:terms], refs[terms : 2 * terms], refs[2 * terms :]
    if homing:
        grad, refs = refs[0], refs[1:]
    rider_in, refs = refs[:along], refs[along:]
    out_ref, refs = refs[0], refs[1:]
    if homing:
        home, other_home = refs[:2]
        refs = refs[2:]
    rider_out, refs = refs[:along], refs[along:]
    work = Scatter(here, turned, shares, a_refs, b_refs, out_ref, refs[:8])
    if homing:
        q_in, ready, kept, kept_sem, q_send, q_recv, home_send, home_recv, over_send, over_recv = refs[8:18]
        keep = pltpu.make_async_copy(grad.at[lax.axis_index("q")], kept, kept_sem)
    ride_start, ride_end = ride(here, kinds, rider_in + rider_out + refs[len(refs) - 2 * along :])

    def to_q(e):
        q, chip = lax.axis_index("q"), here.other(e)
        return remote(grad.at[1 - q, chip], q_in.at[chip], q_send.at[e], q_recv.at[e], {"q": 1 - q})

    def to_chip(e):
        return remote(ready.at[here.other(e)], home.at[here.other(0)], home_send.at[e], home_recv.at[e], here.toward(e))

    def to_core(e):
        chip = here.other(e)
        return remote(home.at[chip], other_home.at[chip], over_send.at[e], over_recv.at[e], {"section": 1 - s})

    def home_step(e):
        chip = here.other(e)
        arrived(q_in.at[chip], q_recv.at[e])
        place = ready.at[chip] if e else home.at[chip]
        add_rows(q_in.at[chip], [kept.at[chip]], place)
        (to_chip(e) if e else to_core(0)).start()

    def home_end(e):
        if e:
            arrived(home.at[here.other(e)], home_recv.at[e])
            to_core(e).start()

    peers = work.peers
    if homing:
        peers = [here.names(e) for e in range(1, count)] + [("section",), ("q",)]
    here.meet(peers + rider_peers(here, kinds))
    if homing:
        for e in range(count):
            to_q(e).start()
        keep.start()
    ride_start()
    work.produce(0, count + 1)
    if homing:
        keep.wait()
    steps = count // 2
    for m in range(steps - 1, 0, -1):
        if homing:
            home_step(steps - 1 - m)
        work.pass_on(m)
    work.settle()
    if homing:
        for e in range(steps - 1, count):
            home_step(e)
        for e in range(count):
            home_end(e)
        for e in range(count):
            arrived(other_home.at[here.other(e)], over_recv.at[e])
            to_core(e).wait_send()
            to_q(e).wait_send()
            if e:
                to_chip(e).wait_send()
    ride_end()
    work.drain()


def scatter_columns(bits, cid, a, b, turned, grad=None, riders=(), shares=None):
    tokens, width = a[0].shape[0], b[0].shape[0 if turned else 1]
    count = 2 ** len(bits)
    block = (tokens // (2 * count), width)
    dma = pltpu.SemaphoreType.DMA
    operands = list(a) + list(b)
    shapes = [jax.ShapeDtypeStruct(block, F32)]
    scratch = scatter_scratch(bits, block)
    if grad is not None:
        operands += [grad]
        shapes += [jax.ShapeDtypeStruct(grad.shape[1:], BF)] * 2
        scratch += [pltpu.VMEM(grad.shape[1:], BF)] * 3 + [dma] + [dma((count,))] * 6
    arrays, more_shapes, more_scratch = rider_shapes(bits, riders)
    inside, outside = pl.BlockSpec(memory_space=pltpu.VMEM), pl.BlockSpec(memory_space=pl.ANY)
    return pl.pallas_call(
        functools.partial(
            scatter_kernel, bits, turned, grad is not None, tuple(kind for kind, _ in riders), shares, len(a)
        ),
        out_shape=shapes + more_shapes,
        in_specs=[inside] * (2 * len(a)) + [outside] * (len(operands) - 2 * len(a) + len(arrays)),
        out_specs=[inside] * len(shapes) + [outside] * len(arrays),
        scratch_shapes=scratch + more_scratch,
        compiler_params=pltpu.CompilerParams(
            collective_id=cid, has_side_effects=True, vmem_limit_bytes=56 * 2**20
        ),
        cost_estimate=lasting(40 if grad is None else 60),
    )(*operands, *arrays)


def scatter_dot(bits, cid, a, b, turned, grad=None, riders=(), shares=None):
    tokens, width = a[0].shape[0], b[0].shape[0 if turned else 1]
    pieces = max(1, tokens * width // 2**22)
    size = width // pieces
    cuts = [
        [f[i * size : (i + 1) * size] if turned else f[:, i * size : (i + 1) * size] for f in b] for i in range(pieces)
    ]
    first = scatter_columns(bits, cid, a, cuts[0], turned, grad, riders, shares)
    rest = [scatter_columns(bits, 14 + turned, a, cut, turned)[0] for cut in cuts[1:]]
    return [jnp.concatenate([first[0]] + rest, axis=1)] + list(first[1:])


def total_kernel(bits, kinds, x_ref, *refs):
    here = Place(bits)
    s, count = here.s, here.count
    along = len(kinds)
    rider_in, out_ref, rider_out, refs = refs[:along], refs[along], refs[along + 1 : 2 * along + 1], refs[2 * along + 1 :]
    part, core_in, ready, landed, done, pair_send, pair_recv, send, recv, back_send, back_recv = refs[:11]
    ride_start, ride_end = ride(here, kinds, rider_in + rider_out + refs[11:])
    lanes = part.shape[3]

    def span(s_of, chip):
        at = (s_of * count + chip) * lanes
        return slice(at, at + lanes)

    for s_of in range(2):
        for chip in range(count):
            part[s_of, chip] = x_ref[:, span(s_of, chip)]
    here.meet([here.names(e) for e in range(1, count)] + [("section",)] + rider_peers(here, kinds))
    first = remote(part.at[1 - s], core_in, pair_send.at[0], pair_recv.at[0], {"section": 1 - s})
    first.start()
    first.wait_recv()
    for chip in range(count):
        total = part[s, chip] + core_in[chip]
        part[s, chip] = total
        ready[chip] = total.astype(BF)

    def out(e):
        return remote(ready.at[here.other(e)], landed.at[e], send.at[e], recv.at[e], here.toward(e))

    def back(e):
        place = done.at[s, here.other(0)]
        return remote(place, place, back_send.at[e], back_recv.at[e], here.toward(e))

    others = range(1, count)
    for e in others:
        out(e).start()
    ride_start()
    total = part[s, here.other(0)]
    for e in others:
        out(e).wait_recv()
        total = total + landed[e].astype(F32)
    done[s, here.other(0)] = total.astype(BF)
    for e in others:
        back(e).start()
    for e in others:
        place = done.at[s, here.other(e)]
        arrived(place, back_recv.at[e])
    last = remote(done.at[s], done.at[s], pair_send.at[1], pair_recv.at[1], {"section": 1 - s})
    last.start()
    last.wait_recv()
    for s_of in range(2):
        for chip in range(count):
            out_ref[:, span(s_of, chip)] = done[s_of, chip]
    ride_end()
    first.wait_send()
    last.wait_send()
    for e in others:
        out(e).wait_send()
        back(e).wait_send()


def sum_columns(bits, cid, x, riders=()):
    rows, tokens = x.shape
    count = 2 ** len(bits)
    block = (rows, tokens // (2 * count))
    dma, vmem = pltpu.SemaphoreType.DMA, pltpu.VMEM
    arrays, more_shapes, more_scratch = rider_shapes(bits, riders)
    inside, outside = pl.BlockSpec(memory_space=pltpu.VMEM), pl.BlockSpec(memory_space=pl.ANY)
    return pl.pallas_call(
        functools.partial(total_kernel, bits, tuple(kind for kind, _ in riders)),
        out_shape=[jax.ShapeDtypeStruct((rows, tokens), BF)] + more_shapes,
        in_specs=[inside] + [outside] * len(arrays),
        out_specs=[inside] + [outside] * len(arrays),
        scratch_shapes=[
            vmem((2, count) + block, F32),
            vmem((count,) + block, F32),
            vmem((count,) + block, BF),
            vmem((count,) + block, BF),
            vmem((2, count) + block, BF),
        ]
        + [dma((2,))] * 2
        + [dma((count,))] * 4
        + more_scratch,
        compiler_params=pltpu.CompilerParams(
            collective_id=cid, has_side_effects=True, vmem_limit_bytes=56 * 2**20
        ),
        cost_estimate=lasting(22),
    )(x, *arrays)


def spread_kernel(bits, kinds, shard_ref, inner_ref, gate_ref, small, *refs):
    here = Place(bits)
    along = len(kinds)
    blocks = inner_ref, gate_ref
    rider_in, refs = refs[:along], refs[along:]
    out_ref, rows, own_small, refs = refs[0], refs[1:3], refs[3], refs[4:]
    rider_out, refs = refs[:along], refs[along:]
    send, recv, pair_send, pair_recv, piece_send, piece_recv, small_send, small_recv = refs[:8]
    ride_start, ride_end = ride(here, kinds, rider_in + rider_out + refs[8:])
    s, q, chip, count = here.s, lax.axis_index("q"), here.other(0), here.count
    others = range(1, count)
    peers = [here.names(e) + extra for e in range(count) for extra in ((), ("section",)) if e or extra]
    here.meet(peers + [("q",), ("q", "section")])

    def piece(i, r, e):
        where = dict(here.toward(e), **({"section": 1 - s} if r else {}))
        src = blocks[i].at[1 - s if r else s, here.other(e)]
        return remote(src, rows[i].at[chip], piece_send.at[i, r, e], piece_recv.at[i, e], where)

    def hand_small(k, where):
        return remote(small, own_small, small_send.at[k], small_recv, where)

    keep_pieces = [pltpu.make_async_copy(blocks[i].at[s, chip], rows[i].at[chip], piece_recv.at[i, 0]) for i in range(2)]
    keep_small = pltpu.make_async_copy(small, own_small, small_recv)
    at_layer = s == 0
    stays, leaves = jnp.logical_and(at_layer, q == s), jnp.logical_and(at_layer, q != s)

    out_ref[s, q, chip] = shard_ref[...]
    own = out_ref.at[s, q, chip]
    copies = [remote(own, own, send.at[e], recv.at[e], here.toward(e)) for e in others]
    for copy in copies:
        copy.start()
    ride_start()

    @pl.when(at_layer)
    def _():
        for i in range(2):
            keep_pieces[i].start()
            for e in range(count):
                for r in range(2):
                    if e or r:
                        piece(i, r, e).start()

    @pl.when(stays)
    def _():
        keep_small.start()
        hand_small(0, {"q": 1 - q}).start()

    @pl.when(leaves)
    def _():
        hand_small(0, {"section": 1 - s}).start()
        hand_small(1, {"section": 1 - s, "q": 1 - q}).start()

    for e in others:
        arrived(out_ref.at[s, q, here.other(e)], recv.at[e])
    place = out_ref.at[s, q]
    first = remote(place, place, pair_send.at[0], pair_recv.at[0], {"q": 1 - q})
    first.start()
    first.wait_recv()
    place = out_ref.at[s]
    second = remote(place, place, pair_send.at[1], pair_recv.at[1], {"section": 1 - s})
    second.start()
    second.wait_recv()
    ride_end()
    arrived(own_small, small_recv)
    for i in range(2):
        for e in range(count):
            arrived(rows[i].at[here.other(e)], piece_recv.at[i, e])
    for copy in copies + [first, second]:
        copy.wait_send()

    @pl.when(at_layer)
    def _():
        for i in range(2):
            for e in range(count):
                for r in range(2):
                    if e or r:
                        piece(i, r, e).wait_send()

    pl.when(stays)(lambda: hand_small(0, {"q": 1 - q}).wait_send())

    @pl.when(leaves)
    def _():
        hand_small(0, {"section": 1 - s}).wait_send()
        hand_small(1, {"section": 1 - s, "q": 1 - q}).wait_send()


def spread(bits, shard, blocks, small, riders):
    arrays, more_shapes, more_scratch = rider_shapes(bits, riders)
    width, count = shard.shape[0], 2 ** len(bits)
    block = (16, max(width, 128))
    padded = jnp.pad(shard[None, :], ((0, block[0] - 1), (0, block[1] - width)))
    dma = pltpu.SemaphoreType.DMA
    shapes = [jax.ShapeDtypeStruct((2, 2, count) + block, shard.dtype)]
    shapes += [jax.ShapeDtypeStruct(b.shape[1:], b.dtype) for b in blocks] + [jax.ShapeDtypeStruct(small.shape, small.dtype)]
    inside, outside = pl.BlockSpec(memory_space=pltpu.VMEM), pl.BlockSpec(memory_space=pl.ANY)
    out, *gots = pl.pallas_call(
        functools.partial(spread_kernel, bits, tuple(kind for kind, _ in riders)),
        out_shape=shapes + more_shapes,
        in_specs=[inside] + [outside] * (3 + len(arrays)),
        out_specs=[inside] + [outside] * (3 + len(arrays)),
        scratch_shapes=[dma((count,)), dma((count,)), dma((2,)), dma((2,))]
        + [dma((2, 2, count)), dma((2, count)), dma((2,)), dma]
        + more_scratch,
        compiler_params=pltpu.CompilerParams(collective_id=0, has_side_effects=True),
        cost_estimate=lasting(12),
    )(padded, *blocks, small, *arrays)
    return [out[:, :, :, 0, :width].reshape((2, -1))] + gots


def chips(bits):
    return tuple(reversed(bits))


def at_home():
    return lax.axis_index("q") == lax.axis_index("section")


def low_first(mine, other):
    low = lax.axis_index("q") == 0
    return jnp.stack([jnp.where(low, mine, other), jnp.where(low, other, mine)])


def by_q(pair):
    low = lax.axis_index("q") == 0
    return jnp.where(low, pair[0], pair[1]), jnp.where(low, pair[1], pair[0])


def leave(value):
    return lax.ppermute(value, ("section", "q"), [(0, 1), (3, 2)])


def home(value):
    return lax.ppermute(value, ("section", "q"), [(1, 0), (2, 3)])


def swap(value):
    return lax.ppermute(value, "q", [(0, 1), (1, 0)])


def after(value, *earlier):
    return lax.optimization_barrier((value,) + earlier)[0]


def column_blocks(bits, rows):
    parts = rows.reshape((rows.shape[0], 2, 2, 2 ** len(bits), -1))
    return [jnp.transpose(parts[:, i], (1, 2, 0, 3)) for i in range(2)]


def assemble_kernel(lower_refs, upper_refs, weight_ref, out_ref, gain_ref):
    depth = weight_ref.shape[0]
    step = min(depth, 32)

    def fill(parts):
        chips, _, wide = parts[0].shape

        @pl.loop(0, depth // step)
        def _(r):
            lines = pl.ds(pl.multiple_of(r * step, step), step)
            total = jnp.zeros((step, wide), F32)
            for i, part in enumerate(parts):
                for chip in range(chips):
                    at = (i * chips + chip) * wide
                    value = part[chip, lines, :].astype(F32)
                    out_ref[lines, at : at + wide] = value
                    total = total + value * weight_ref[lines, at : at + wide].astype(F32)
            gain_ref[lines, :] = jnp.sum(total, axis=1, keepdims=True)

    upper = lax.axis_index("section") == 1
    pl.when(jnp.logical_not(upper))(lambda: fill(lower_refs))
    pl.when(upper)(lambda: fill(upper_refs))


def assemble(lower, upper, weight):
    inside = pl.BlockSpec(memory_space=pltpu.VMEM)
    return pl.pallas_call(
        assemble_kernel,
        out_shape=[jax.ShapeDtypeStruct(weight.shape, F32), jax.ShapeDtypeStruct((weight.shape[0], 1), F32)],
        in_specs=[[inside] * 4, [inside] * 4, inside],
        out_specs=[inside, inside],
        compiler_params=pltpu.CompilerParams(vmem_limit_bytes=40 * 2**20),
    )(lower, upper, weight)


def silu_slope(v):
    gate = jax.nn.sigmoid(v)
    return gate, gate * (1.0 + v * (1.0 - gate))


def normalize(stream, gain):
    inverse = lax.rsqrt(jnp.mean(stream * stream, axis=-1, keepdims=True) + norm_eps)
    return inverse, (stream * inverse * gain[None, :]).astype(BF)


class Small:
    def __init__(self, packed):
        self.taps = packed[:KC].astype(F32)
        self.conv_bias = packed[KC].astype(F32)
        self.dt_bias = packed[KC + 1].astype(F32)
        self.skip = packed[KC + 2].astype(F32)
        self.dt = packed[KC + 3 : KC + 3 + R]
        self.xproj = packed[KC + 3 + R : KC + 3 + 2 * R + 2 * N]


def mixer_inputs(normed, in_inner, small):
    inner = forward_dot(normed, in_inner).astype(BF).astype(F32)
    tokens, channels = inner.shape
    extended = jnp.concatenate([jnp.zeros((KC - 1, channels), F32), inner], axis=0)
    conv = jnp.broadcast_to(small.conv_bias[None, :], (tokens, channels))
    for tap in range(KC):
        conv = conv + small.taps[tap][None, :] * extended[tap : tap + tokens]
    act = jax.nn.silu(conv)
    return extended, conv, act, back_dot(small.xproj, act.astype(BF))


def mixer(xproj, act, normed, in_gate, small):
    gate_in = forward_dot(normed, in_gate).astype(BF).astype(F32)
    key_t, query_t = xproj[R : R + N].astype(F32), xproj[R + N :].astype(F32)
    key_norm = jnp.sum(key_t * key_t, axis=0)[:, None]
    write = jax.nn.sigmoid(cross_dot(xproj[:R], small.dt) + small.dt_bias[None, :])
    rate = write / (1.0 + write * key_norm)
    recur, before, last = recur_forward(rate, act, key_t, query_t)
    recur = recur + small.skip[None, :] * act
    gated = (recur * jax.nn.silu(gate_in)).astype(BF)
    return gate_in, key_t, query_t, key_norm, write, rate, recur, gated, before, last


def gate_back(grad_low, out_weight, kept):
    gate_in, recur = kept[0], kept[6]
    d_gated = back_dot(grad_low, out_weight).astype(BF).astype(F32)
    gate, slope = silu_slope(gate_in)
    return d_gated * (gate_in * gate), (d_gated * recur * slope).astype(BF)


def mixer_back(bits, cid, d_recur, act, xproj, kept, small, riders, product=(), shares=None):
    key_t, query_t, key_norm, write, rate, recur, gated, before, last = kept[1:]
    d_skip = jnp.sum(d_recur * act, axis=0)
    d_rate, d_act_rec, d_key_t, d_query_t, *gots = recur_backward(
        bits, cid, rate, act, d_recur, key_t, query_t, before, last, riders, product, shares
    )
    share = 1.0 / (1.0 + write * key_norm)
    pulled = d_rate * share * share
    d_pre = pulled * write * (1.0 - write)
    d_key_rate = -2.0 * key_t * jnp.sum(pulled * write * write, axis=1)[None, :]
    d_dt_bias = jnp.sum(d_pre, axis=0)
    d_delta = d_pre.astype(BF)
    d_dt = forward_dot(xproj[:R], d_delta)
    d_xproj = jnp.concatenate([back_dot(small.dt, d_delta), d_key_t + d_key_rate, d_query_t], axis=0)
    return d_act_rec, d_xproj, (d_dt_bias[None], d_skip[None], d_dt), gots


def inputs_back(d_xproj, d_recur, d_act_rec, extended, conv, act, small):
    tokens = act.shape[0]
    d_act = cross_dot(d_xproj, small.xproj) + small.skip[None, :] * d_recur + d_act_rec
    d_conv = d_act * silu_slope(conv)[1]
    d_taps = jnp.stack([jnp.sum(d_conv * extended[tap : tap + tokens], axis=0) for tap in range(KC)])
    d_bias = jnp.sum(d_conv, axis=0)
    later = jnp.concatenate([d_conv, jnp.zeros((KC - 1, d_conv.shape[1]), F32)], axis=0)
    d_inner = sum(small.taps[tap][None, :] * later[KC - 1 - tap : KC - 1 - tap + tokens] for tap in range(KC))
    return d_inner.astype(BF), (d_taps, d_bias[None]), forward_dot(d_xproj, act.astype(BF))


def norm_back(grad_out, d_normed, stream, inverse, gain):
    scaled = gain[None, :] * d_normed
    mean = jnp.mean(stream * scaled, axis=-1, keepdims=True)
    return grad_out + inverse * scaled - stream * inverse**3 * mean


def pack(first, second, third):
    packed = jnp.concatenate(first + second + (third,), axis=0)
    return jnp.pad(packed, ((0, -packed.shape[0] % 16), (0, 0)))


def on_device(
    bits, hidden_in, cotangent, norm_gain, in_weight, conv_weight, conv_bias, xproj_weight, dt_weight, dt_bias, skip_gain, out_weight
):
    packed = pack(
        (conv_weight[0], conv_bias),
        (dt_bias, skip_gain, dt_weight[0]),
        jnp.swapaxes(xproj_weight[0], 0, 1),
    )
    blocks = column_blocks(bits, in_weight[0])
    tight = (2, 5, 9)

    def weight(pair):
        return pair.reshape((-1, pair.shape[-1]))

    def weight_grad(normed, d_out):
        return cross_dot(normed, d_out).astype(BF).reshape((2,) + blocks[0].shape[1:])

    mine, others = by_q(hidden_in)
    gains, inner, gate, packed0, got = spread(bits, norm_gain[0], blocks, packed, [("leave", others)])
    gains = gains.astype(F32)
    stream0 = jnp.where(at_home(), mine, got).astype(F32)

    inverse0, normed = normalize(stream0, gains[0])
    normed0, inner, gate, *sent = gather_call(
        bits, 1, [normed], shares=tight, us=60,
        riders=[("stack", inner), ("stack", gate)] + [("over_at", b) for b in blocks] + [("out1", packed)] + [("out%d" % l, out_weight[0]) for l in range(2)],
    )
    upper = lax.axis_index("section") == 1
    columns = [jnp.where(upper, b[1], got) for b, got in zip(blocks, sent)]
    packed_held = jnp.where(upper, packed, sent[2])
    out_held = jnp.where(upper, sent[3], out_weight[0]), jnp.where(upper, out_weight[0], sent[4])
    inner0, small0 = weight(inner), Small(packed0)
    extended0, conv0, act0, part = mixer_inputs(normed0, inner0, small0)
    part = after(part, out_held[0])
    xproj0, inner, late_gate = sum_columns(bits, 4, part, [("cube", columns[0]), ("cube", columns[1])])
    gate0 = weight(gate)
    out0 = jnp.where(at_home(), out_held[0], leave(after(out_held[0], xproj0)))
    kept0 = mixer(xproj0, act0, normed0, gate0, small0)
    grad_mine, grad_others = by_q(cotangent)
    added, got, grad_got, gate = scatter_dot(
        bits, 8, [kept0[7]], [out0], False, shares=(3, 5, 8),
        riders=[("leave", packed_held), ("leave", grad_others.astype(BF)), ("stack", late_gate)],
    )
    gate1 = weight(gate)
    grad1 = jnp.where(at_home(), grad_mine, grad_got.astype(F32))
    small1 = Small(jnp.where(at_home(), packed_held, got))
    output0 = (stream0 + added).astype(BF)

    stream1 = output0.astype(F32)
    inverse1, normed = normalize(stream1, gains[1])
    normed1, grad_low1, inner, output0_home = gather_call(
        bits, 2, [normed, grad1.astype(BF)], riders=[("stack", inner), ("home", output0)], shares=(3, 5, 8), us=65
    )
    inner1 = weight(inner)
    extended1, conv1, act1, part = mixer_inputs(normed1, inner1, small1)
    (xproj1,) = sum_columns(bits, 5, after(part, out_held[1]))
    out1 = jnp.where(at_home(), out_held[1], leave(after(out_held[1], xproj1)))
    kept1 = mixer(xproj1, act1, normed1, gate1, small1)

    d_out1 = cross_dot(kept1[7], grad_low1).astype(BF)
    d_recur, d_gate1 = gate_back(grad_low1, out1, kept1)
    keep, give = by_q(weight_grad(normed1, d_gate1))
    beside = kept1[7].shape[0] * out1.shape[1] <= 2**22 and kept1[7].shape[0] >= 16 * BLOCK
    if beside:
        d_act_rec, part, d_small, (added, got) = mixer_back(
            bits, 16, d_recur, act1, xproj1, kept1, small1, [("swap", give)], (kept1[7], out1), (4, 5, 7)
        )
    else:
        (added,) = scatter_dot(bits, 10, [kept1[7]], [out1], False)
        d_act_rec, part, d_small, (got,) = mixer_back(bits, 16, d_recur, act1, xproj1, kept1, small1, [("swap", give)])
    output1 = (stream1 + added).astype(BF)
    d_xproj, output1_home = sum_columns(bits, 6, part, [("home", output1)])
    d_gate_in1 = (keep.astype(F32) + got.astype(F32)).astype(BF)
    d_inner, d_conv, d_xproj_weight = inputs_back(d_xproj, d_recur, d_act_rec, extended1, conv1, act1, small1)
    d_packed1 = pack(d_conv, d_small, d_xproj_weight)
    d_normed, d_gate_in1, d_packed1_home, d_out1_home = scatter_dot(
        bits, 11, [d_inner, d_gate1], [inner1, gate1], True,
        riders=[("cube", d_gate_in1), ("home", d_packed1.astype(BF)), ("home", d_out1)], shares=(4, 5, 7),
    )
    keep, give = by_q(weight_grad(normed1, d_inner))
    input_grad1 = norm_back(grad1, d_normed, stream1, inverse1, gains[1])
    grad0 = input_grad1.astype(BF)
    grad_low0, got, grad1_home = gather_call(
        bits, 3, [grad0], riders=[("swap", give), ("home", grad0)], shares=(3, 5, 8), us=45
    )
    d_inner1 = (keep.astype(F32) + got.astype(F32)).astype(BF)

    d_out0 = cross_dot(kept0[7], grad_low0).astype(BF)
    d_recur, d_gate0 = gate_back(grad_low0, out0, kept0)
    keep, give = by_q(weight_grad(normed0, d_gate0))
    d_act_rec, part, d_small, (got, d_inner1) = mixer_back(
        bits, 17, d_recur, act0, xproj0, kept0, small0, [("swap", give), ("cube", d_inner1)]
    )
    d_gate_in0 = (keep.astype(F32) + got.astype(F32)).astype(BF)
    d_xproj, d_gate_in0, d_out0_home = sum_columns(
        bits, 7, part, [("cube", d_gate_in0), ("home", d_out0)]
    )
    d_inner, d_conv, d_xproj_weight = inputs_back(d_xproj, d_recur, d_act_rec, extended0, conv0, act0, small0)
    d_packed0 = pack(d_conv, d_small, d_xproj_weight)
    d_out = [
        (mine.astype(F32) + other.astype(F32)).astype(BF) for mine, other in ((d_out0, d_out0_home), (d_out1, d_out1_home))
    ]
    d_packed1 = (d_packed1 + d_packed1_home.astype(F32)).astype(BF)
    gate_over = jnp.where(upper, d_gate_in0, d_gate_in1)
    d_normed, d_inner0, d_inner0_other, d_packed0_home, inner_other, gate_other, *backs = scatter_dot(
        bits, 13, [d_inner, d_gate0], [inner0, gate0], True, weight_grad(normed0, d_inner), shares=(3, 5, 8),
        riders=[
            ("home", d_packed0.astype(BF)), ("over", d_inner1), ("over", gate_over), ("back0", d_out[0]), ("back1", d_out[1]),
            ("back1", d_packed1), ("back0", output0), ("back0", output0_home), ("back1", output1), ("back1", output1_home),
            ("back1", grad0), ("back1", grad1_home),
        ],
    )
    input_grad0 = norm_back(grad0.astype(F32), d_normed, stream0, inverse0, gains[0]).astype(BF)

    def settled(lower, upper_one, lower_back, upper_back):
        return jnp.where(at_home(), jnp.where(upper, upper_one, lower), jnp.where(upper, upper_back, lower_back))

    d_out = settled(*d_out, *backs[:2]).astype(F32)
    d_packed0 = (d_packed0 + d_packed0_home.astype(F32)).astype(BF)
    d_packed = settled(d_packed0, d_packed1, lax.ppermute(d_packed0, ("section", "q"), [(3, 1)]), backs[2]).astype(F32)
    low = lax.axis_index("q") == 0
    mine, other = settled(output0, output1, backs[3], backs[5]), settled(output0_home, output1_home, backs[4], backs[6])
    layer_outputs = low_first(mine, other).astype(F32)
    mine, other = jnp.where(at_home(), grad0, backs[7]), jnp.where(at_home(), grad1_home, backs[8])
    grads1 = low_first(mine, other)
    of_first = lax.ppermute(input_grad0, ("section", "q"), [(2, 1)])
    of_second = lax.ppermute(input_grad0, ("section", "q"), [(1, 0), (3, 1)])
    grads0 = jnp.stack([jnp.where(low, input_grad0, of_first), of_second])
    input_grads = jnp.where(upper, grads1, grads0).astype(F32)
    d_in, d_gain = assemble(
        [d_inner0, d_inner0_other, d_gate_in0, gate_other], [inner_other, d_inner1, gate_other, d_gate_in1], in_weight[0]
    )
    d_gain = d_gain[:, 0] / norm_gain[0].astype(F32)
    return (
        layer_outputs[None],
        input_grads[None],
        d_gain[None],
        d_in[None],
        d_packed[None, :KC],
        d_packed[None, KC],
        jnp.swapaxes(d_packed[KC + 3 + R : KC + 3 + 2 * R + 2 * N], 0, 1)[None],
        d_packed[None, KC + 3 : KC + 3 + R],
        d_packed[None, KC + 1],
        d_packed[None, KC + 2],
        d_out[None],
    )


def solution(mesh):
    sections, chip_count = mesh.devices.shape
    n = chip_count.bit_length() - 2
    bits = tuple("c%d" % d for d in range(n))
    split = Mesh(mesh.devices.reshape((sections,) + (2,) * (n + 1)), ("section", "q") + chips(bits))
    seq = ("q",) + chips(bits)
    placed = (
        P(None, seq, None),
        P(None, seq, None),
        P("section", seq),
        P("section", seq, None),
        P("section", None, seq),
        P("section", seq),
        P("section", seq, None),
        P("section", None, seq),
        P("section", seq),
        P("section", seq),
        P("section", seq, None),
    )
    return jax.shard_map(
        functools.partial(on_device, bits),
        mesh=split,
        in_specs=placed,
        out_specs=(P("section", None, seq, None), P("section", None, seq, None)) + placed[2:],
        check_vma=False,
    )
```

```python
import functools

import jax
import jax.numpy as jnp
from jax import lax
from jax.experimental import pallas as pl
from jax.experimental.pallas import tpu as pltpu
from jax.sharding import Mesh, PartitionSpec as P


N = 16
R = 128
KC = 4
BLOCK = 128
norm_eps = 1e-05
BF = jnp.bfloat16
F32 = jnp.float32
MESH = pl.DeviceIdType.MESH


def forward_dot(operand, factor):
    return jnp.dot(operand, factor, preferred_element_type=F32)


def cross_dot(operand, factor):
    return lax.dot_general(operand, factor, (((0,), (0,)), ((), ())), preferred_element_type=F32)


def back_dot(operand, factor):
    return lax.dot_general(operand, factor, (((1,), (1,)), ((), ())), preferred_element_type=F32)


def lasting(us):
    return pl.CostEstimate(flops=0, bytes_accessed=int(us * 3.4e6), transcendentals=0)


def widths(channels):
    wide = min(channels, 128)
    return wide, channels // wide


def sum_rows(pieces):
    row = lax.broadcasted_iota(jnp.int32, pieces[0].shape, 0)
    shift = 1
    while len(pieces) > 1:
        keep = (row & shift) == 0
        pieces = [
            jnp.where(keep, a, b) + pltpu.roll(jnp.where(keep, b, a), shift, 0)
            for a, b in zip(pieces[0::2], pieces[1::2])
        ]
        shift *= 2
    return pieces[0]


def halves(v):
    return v[:8] + v[8:]


def lanes_of(p, wide):
    return slice(p * wide, (p + 1) * wide)


def recur_forward_kernel(rate_ref, act_ref, key_ref, query_ref, out_ref, before_ref, last_ref, memory_ref):
    wide, parts = widths(rate_ref.shape[1])

    @pl.when(pl.program_id(0) == 0)
    def _():
        memory_ref[...] = jnp.zeros_like(memory_ref)

    memory = [memory_ref[:, lanes_of(p, wide)] for p in range(parts)]
    for base in range(0, rate_ref.shape[0], 8):
        rates = rate_ref[base : base + 8, :]
        feeds = rates * act_ref[base : base + 8, :]
        sums = [[] for _ in range(parts)]
        for i in range(8):
            key = jnp.broadcast_to(key_ref[:, base + i : base + i + 1], (N, wide))
            query = jnp.broadcast_to(query_ref[:, base + i : base + i + 1], (N, wide))
            square = key * key
            for p in range(parts):
                lanes = lanes_of(p, wide)
                before_ref[base + i, :, lanes] = memory[p]
                memory[p] = (1.0 - rates[i : i + 1, lanes] * square) * memory[p] + key * feeds[i : i + 1, lanes]
                sums[p].append(halves(memory[p] * query))
        for p in range(parts):
            out_ref[base : base + 8, lanes_of(p, wide)] = sum_rows(sums[p])
    for p in range(parts):
        memory_ref[:, lanes_of(p, wide)] = memory[p]

    @pl.when(pl.program_id(0) == pl.num_programs(0) - 1)
    def _():
        last_ref[...] = memory_ref[...]


def recur_forward(rate, act, key_t, query_t):
    tokens, channels = rate.shape
    rows = pl.BlockSpec((BLOCK, channels), lambda i: (i, 0))
    cols = pl.BlockSpec((N, BLOCK), lambda i: (0, i))
    return pl.pallas_call(
        recur_forward_kernel,
        grid=(tokens // BLOCK,),
        in_specs=[rows, rows, cols, cols],
        out_specs=[
            rows,
            pl.BlockSpec((BLOCK, N, channels), lambda i: (i, 0, 0)),
            pl.BlockSpec((N, channels), lambda i: (0, 0)),
        ],
        out_shape=[
            jax.ShapeDtypeStruct((tokens, channels), F32),
            jax.ShapeDtypeStruct((tokens, N, channels), F32),
            jax.ShapeDtypeStruct((N, channels), F32),
        ],
        scratch_shapes=[pltpu.VMEM((N, channels), F32)],
        compiler_params=pltpu.CompilerParams(
            dimension_semantics=("arbitrary",), vmem_limit_bytes=40 * 2**20
        ),
        cost_estimate=lasting(1),
    )(rate, act, key_t, query_t)


def recur_backward_kernel(bits, kinds, shares, steps, rate_ref, act_ref, grad_ref, key_ref, query_ref, before_ref, last_ref, *refs):
    along, beside = len(kinds), 1 if steps else 0
    product, refs = refs[: 2 * beside], refs[2 * beside :]
    rider_in, refs = refs[:along], refs[along:]
    d_rate_ref, d_act_ref, d_key_ref, d_query_ref = refs[:4]
    scattered, refs = refs[4 : 4 + beside], refs[4 + beside :]
    rider_out, refs = refs[:along], refs[along:]
    lam_ref, memory_ref, key_rows, query_rows = refs[:4]
    here = Place(bits)
    ride_start, ride_end = ride(here, kinds, rider_in + rider_out + refs[len(refs) - 2 * along :])
    stages = {}
    peers = rider_peers(here, kinds)
    if beside:
        work = Scatter(here, False, shares, product[:1], product[1:], scattered[0], refs[4:12])
        peers = peers + work.peers
        half = here.count // 2
        for k in range(half + 1):
            stages[k] = functools.partial(work.produce, 2 * k, min(2 * k + 2, here.count + 1))
        for k, m in enumerate(range(half - 1, 0, -1)):
            stages[steps - 1 - 2 * (half - 1 - k)] = functools.partial(work.pass_on, m)
    wide, parts = widths(rate_ref.shape[1])
    block = rate_ref.shape[0]

    @pl.when(pl.program_id(0) == 0)
    def _():
        here.meet(peers)
        ride_start()
        lam_ref[...] = jnp.zeros_like(lam_ref)
        memory_ref[...] = last_ref[...]

    for at, stage in stages.items():
        pl.when(pl.program_id(0) == at)(stage)
    lam = [lam_ref[:, lanes_of(p, wide)] for p in range(parts)]
    memory = [memory_ref[:, lanes_of(p, wide)] for p in range(parts)]
    for base in reversed(range(0, block, 8)):
        rates = rate_ref[base : base + 8, :]
        acts = act_ref[base : base + 8, :]
        grads = grad_ref[base : base + 8, :]
        d_rates = [[None] * 8 for _ in range(parts)]
        d_acts = [[None] * 8 for _ in range(parts)]
        for i in reversed(range(8)):
            at = base + i
            key = jnp.broadcast_to(key_ref[:, at : at + 1], (N, wide))
            query = jnp.broadcast_to(query_ref[:, at : at + 1], (N, wide))
            square = key * key
            key_sum = query_sum = None
            for p in range(parts):
                lanes = lanes_of(p, wide)
                grad = grads[i : i + 1, lanes]
                before = before_ref[at, :, lanes]
                pulled = query * grad + lam[p]
                kept = key * before
                missing = acts[i : i + 1, lanes] - kept
                keyed = pulled * key
                scaled = pulled * rates[i : i + 1, lanes]
                d_acts[p][i] = halves(keyed)
                d_rates[p][i] = halves(keyed * missing)
                to_key = scaled * (missing - kept)
                to_query = memory[p] * grad
                key_sum = to_key if key_sum is None else key_sum + to_key
                query_sum = to_query if query_sum is None else query_sum + to_query
                lam[p] = pulled - scaled * square
                memory[p] = before
            key_rows[at * N : (at + 1) * N, :] = key_sum.astype(BF)
            query_rows[at * N : (at + 1) * N, :] = query_sum.astype(BF)
        for p in range(parts):
            lanes = lanes_of(p, wide)
            d_rate_ref[base : base + 8, lanes] = sum_rows(d_rates[p])
            d_act_ref[base : base + 8, lanes] = rates[:, lanes] * sum_rows(d_acts[p])
    for p in range(parts):
        lam_ref[:, lanes_of(p, wide)] = lam[p]
        memory_ref[:, lanes_of(p, wide)] = memory[p]

    ones = jnp.ones((wide, block), BF)
    token = lax.broadcasted_iota(jnp.int32, (block, N, block), 0)
    own = token == lax.broadcasted_iota(jnp.int32, (block, N, block), 2)
    for rows, result in ((key_rows, d_key_ref), (query_rows, d_query_ref)):
        sums = forward_dot(rows[...], ones).reshape(block, N, block)
        result[...] = jnp.sum(jnp.where(own, sums, 0.0), axis=0)

    @pl.when(pl.program_id(0) == pl.num_programs(0) - 1)
    def _():
        if beside:
            work.settle()
            work.drain()
        ride_end()


def recur_backward(bits, cid, rate, act, grad, key_t, query_t, before, last, riders, product=(), shares=None):
    tokens, channels = rate.shape
    count = tokens // BLOCK
    rows = pl.BlockSpec((BLOCK, channels), lambda i: (count - 1 - i, 0))
    cols = pl.BlockSpec((N, BLOCK), lambda i: (0, count - 1 - i))
    products = pltpu.VMEM((BLOCK * N, widths(channels)[0]), BF)
    arrays, more_shapes, more_scratch = rider_shapes(bits, riders)
    outside = [pl.BlockSpec(memory_space=pl.ANY)] * len(arrays)
    inside = [pl.BlockSpec(memory_space=pltpu.VMEM)] * len(product)
    if product:
        block = (tokens // 2 ** (len(bits) + 1), product[1].shape[1])
        more_shapes = [jax.ShapeDtypeStruct(block, F32)] + more_shapes
        more_scratch = scatter_scratch(bits, block) + more_scratch
    return pl.pallas_call(
        functools.partial(
            recur_backward_kernel, bits, tuple(kind for kind, _ in riders), shares, count if product else 0
        ),
        grid=(count,),
        in_specs=[
            rows, rows, rows, cols, cols,
            pl.BlockSpec((BLOCK, N, channels), lambda i: (count - 1 - i, 0, 0)),
            pl.BlockSpec((N, channels), lambda i: (0, 0)),
        ] + inside + outside,
        out_specs=[rows, rows, cols, cols] + inside[:1] + outside,
        out_shape=[
            jax.ShapeDtypeStruct((tokens, channels), F32),
            jax.ShapeDtypeStruct((tokens, channels), F32),
            jax.ShapeDtypeStruct((N, tokens), F32),
            jax.ShapeDtypeStruct((N, tokens), F32),
        ] + more_shapes,
        scratch_shapes=[pltpu.VMEM((N, channels), F32), pltpu.VMEM((N, channels), F32), products, products]
        + more_scratch,
        compiler_params=pltpu.CompilerParams(
            dimension_semantics=("arbitrary",), vmem_limit_bytes=56 * 2**20, collective_id=cid, has_side_effects=True
        ),
        cost_estimate=lasting(1),
    )(rate, act, grad, key_t, query_t, before, last, *product, *arrays)


class Place:
    def __init__(self, bits):
        self.bits = bits
        self.n = len(bits)
        self.count = 2**self.n
        self.at = [lax.axis_index(name) for name in bits]
        self.s = lax.axis_index("section")

    def other(self, e):
        return sum(2**d * (c + e // 2**d % 2 * (1 - 2 * c)) for d, c in enumerate(self.at))

    def toward(self, e):
        return {self.bits[d]: 1 - self.at[d] for d in range(self.n) if e // 2**d % 2}

    def dims(self, p, m):
        return sum(2 ** ((p + t) % self.n) for t in range(self.n) if m // 2**t % 2)

    def positions(self, p, e):
        return sum(2**t * (e // 2 ** ((p + t) % self.n) % 2) for t in range(self.n))

    def names(self, e):
        return tuple(self.bits[d] for d in range(self.n) if e // 2**d % 2)

    def meet(self, peers):
        barrier = pltpu.get_barrier_semaphore()
        peers = list(dict.fromkeys(peers))
        for axes in peers:
            where = {name: 1 - lax.axis_index(name) for name in axes}
            pl.semaphore_signal(barrier, inc=1, device_id=where, device_id_type=MESH)
        pl.semaphore_wait(barrier, len(peers))


def spans_of(width, n, shares=None):
    tiles = width // 128
    sizes = [(tiles // n + (p < tiles % n)) * 128 for p in range(n)]
    if shares is not None and len(shares) == n and sum(shares) == tiles:
        sizes = [share * 128 for share in shares]
    return [(sum(sizes[:p]), size) for p, size in enumerate(sizes)]


def remote(src, dst, send, recv, where):
    return pltpu.make_async_remote_copy(
        src_ref=src, dst_ref=dst, send_sem=send, recv_sem=recv, device_id=where, device_id_type=MESH
    )


def arrived(place, sem):
    pltpu.make_async_copy(place, place, sem).wait()


def rider_peers(here, kinds):
    peers = [here.names(e) for e in range(1, here.count)] if set(kinds) & {"cube", "cube_cols"} else []
    if set(kinds) & {"swap", "stack", "home", "leave"}:
        peers.append(("q",))
    if set(kinds) & {"over", "over_at", "over_cols0", "over_cols1", "out0", "out1", "back0", "back1"}:
        peers.append(("section",))
    return peers


def ride(here, kinds, refs):
    k = len(kinds)
    riders = list(zip(kinds, refs[:k], refs[k : 2 * k], refs[2 * k : 3 * k], refs[3 * k :]))
    q, chip = lax.axis_index("q"), here.other(0)

    def row(kind, src, at):
        if kind == "cube":
            return src.at[at]
        wide = src.shape[1] // here.count
        return src.at[:, pl.ds(pl.multiple_of(at * wide, 128), wide)]

    def copies(kind, src, dst, send, recv):
        if kind in ("cube", "cube_cols"):
            return [
                remote(row(kind, src, here.other(e)), dst.at[chip], send.at[e], recv.at[e], here.toward(e))
                for e in range(1, here.count)
            ]
        if kind in ("over", "over_at") or kind[:-1] in ("out", "back", "over_cols"):
            src = src.at[1 - here.s] if kind == "over_at" else src
            if kind[:-1] == "over_cols":
                wide = src.shape[1] // 4
                src = src.at[:, pl.ds(pl.multiple_of((int(kind[-1]) * 2 + 1 - here.s) * wide, 128), wide)]
            return [remote(src, dst, send.at[0], recv.at[0], {"section": 1 - here.s})]
        return [remote(src, dst.at[q] if kind == "stack" else dst, send.at[0], recv.at[0], {"q": 1 - q})]

    def when(kind, sending, do):
        if kind in ("home", "leave"):
            pl.when((q != here.s) if sending == (kind == "home") else (q == here.s))(do)
        elif kind[:-1] in ("out", "back"):
            at_layer = (here.s == int(kind[-1])) if sending == (kind[:-1] == "out") else (here.s != int(kind[-1]))
            away = (q != here.s) if sending == (kind[:-1] == "out") else (q == here.s)
            pl.when(jnp.logical_and(at_layer, away))(do)
        else:
            do()

    def start():
        for kind, src, dst, send, recv in riders:
            if kind in ("cube", "cube_cols"):
                pltpu.make_async_copy(row(kind, src, chip), dst.at[chip], recv.at[0]).start()
            if kind == "stack":
                pltpu.make_async_copy(src, dst.at[q], recv.at[1]).start()
            for copy in copies(kind, src, dst, send, recv):
                when(kind, True, copy.start)

    def finish():
        for kind, src, dst, send, recv in riders:
            if kind in ("cube", "cube_cols"):
                for e in range(here.count):
                    arrived(dst.at[here.other(e)], recv.at[e])
            elif kind == "stack":
                arrived(dst.at[1 - q], recv.at[0])
                arrived(dst.at[q], recv.at[1])
            else:
                when(kind, False, lambda: arrived(dst, recv.at[0]))
            for copy in copies(kind, src, dst, send, recv):
                when(kind, True, copy.wait_send)

    return start, finish


def rider_shapes(bits, riders):
    sems = pltpu.SemaphoreType.DMA((2 ** len(bits),))
    def made(kind, shape):
        if kind == "over_at":
            return shape[1:]
        if kind[:-1] == "over_cols":
            return (shape[0], shape[1] // 4)
        if kind == "cube_cols":
            return (2 ** len(bits), shape[0], shape[1] // 2 ** len(bits))
        return ((2,) if kind == "stack" else ()) + shape

    shapes = [jax.ShapeDtypeStruct(made(kind, array.shape), array.dtype) for kind, array in riders]
    return [array for _, array in riders], shapes, [sems] * (2 * len(riders))


def gather_kernel(bits, total, kinds, shares, *refs):
    here = Place(bits)
    n, s, count = here.n, here.s, here.count
    chip, along = here.other(0), len(kinds)
    inputs, refs = refs[: total + along], refs[total + along :]
    outputs, sems = refs[: total + along], refs[total + along :]
    given, made = inputs[:total], outputs[:total]
    ride_start, ride_end = ride(here, kinds, inputs[total:] + outputs[total:] + sems[len(sems) - 2 * along :])
    local_sem, send, recv, core_send, core_recv = sems[:5]
    spans = spans_of(given[0].shape[1], n, shares)
    parts = [(k, p) for k in range(total) for p in range(n) if spans[p][1]]

    def block(k, e, p, s_of):
        return made[k].at[s_of, here.other(e), :, pl.ds(*spans[p])]

    def source(k, e, p):
        return block(k, e, p, s) if e else given[k].at[:, pl.ds(*spans[p])]

    def deliver(k, p, m):
        t = m.bit_length() - 1
        held = here.dims(p, m - 2**t)
        where = here.toward(2 ** ((p + t) % n))
        return remote(source(k, held, p), block(k, held, p, s), send.at[k, p, m], recv.at[k, p, m], where)

    def core(k, p, m):
        held = here.dims(p, m)
        sems = core_send.at[k, p, m], core_recv.at[k, p, m]
        return remote(source(k, held, p), block(k, held, p, s), *sems, {"section": 1 - s})

    here.meet([here.names(2**d) for d in range(n)] + [("section",)] + rider_peers(here, kinds))
    own = [pltpu.make_async_copy(given[k], made[k].at[s, chip], local_sem.at[k]) for k in range(total)]
    for k in range(total):
        for t in range(n):
            for p in range(n):
                if spans[p][1]:
                    deliver(k, p, 2**t).start()
        own[k].start()
    ride_start()
    for k, p in parts:
        core(k, p, 0).start()
    for m in range(1, count):
        for k, p in parts:
            arrived(block(k, here.dims(p, m), p, s), recv.at[k, p, m])
            for t in range(m.bit_length(), n):
                deliver(k, p, m + 2**t).start()
            core(k, p, m).start()
    for copy in own:
        copy.wait()
    for m in range(count):
        for k, p in parts:
            arrived(block(k, here.dims(p, m), p, 1 - s), core_recv.at[k, p, m])
    for m in range(count):
        for k, p in parts:
            core(k, p, m).wait_send()
            if m:
                deliver(k, p, m).wait_send()
    ride_end()


def gather_call(bits, cid, shards, riders=(), shares=None, us=35):
    rows, width = shards[0].shape
    n = len(bits)
    count = 2**n
    dma = pltpu.SemaphoreType.DMA
    sems = dma((len(shards), n, count))
    shapes = [jax.ShapeDtypeStruct((2, count, rows, width), shard.dtype) for shard in shards]
    scratch = [dma((len(shards),)), sems, sems, sems, sems]
    arrays, more_shapes, more_scratch = rider_shapes(bits, riders)
    shapes += more_shapes
    out = pl.pallas_call(
        functools.partial(gather_kernel, bits, len(shards), tuple(kind for kind, _ in riders), shares),
        out_shape=shapes,
        in_specs=[pl.BlockSpec(memory_space=pl.ANY)] * len(shapes),
        out_specs=[pl.BlockSpec(memory_space=pl.ANY)] * len(shapes),
        scratch_shapes=scratch + more_scratch,
        compiler_params=pltpu.CompilerParams(collective_id=cid, has_side_effects=True),
        cost_estimate=lasting(us),
    )(*shards, *arrays)
    return [o.reshape((-1, width)) for o in out[: len(shards)]] + list(out[len(shards) :])


def add_rows(place, terms, out=None):
    step = 32
    out = place if out is None else out

    @pl.loop(0, place.shape[0] // step)
    def _(r):
        lines = pl.ds(pl.multiple_of(r * step, step), step)
        total = place[lines, :].astype(F32)
        for term in terms:
            total = total + term[lines, :].astype(F32)
        out[lines, :] = total.astype(out.dtype)


class Scatter:
    def __init__(self, here, turned, shares, a_refs, b_refs, out_ref, scratch):
        self.here, self.turned, self.a_refs, self.b_refs, self.out_ref = here, turned, a_refs, b_refs, out_ref
        self.mine, self.give, self.core_in, self.landed, self.core_send, self.core_recv, self.send, self.recv = scratch
        self.rows, self.width = out_ref.shape
        self.spans = spans_of(self.width, here.n, shares)
        self.parts = [p for p in range(here.n) if self.spans[p][1]]
        self.peers = [here.names(2**d) for d in range(here.n)] + [("section",)]

    def core(self, chip):
        sems = self.core_send.at[chip], self.core_recv.at[chip]
        return remote(self.give.at[chip], self.core_in.at[chip], *sems, {"section": 1 - self.here.s})

    def hand(self, p, m, t):
        n = self.here.n
        e = sum(2 ** ((p + u) % n) * (m // 2**u % 2) for u in range(n))
        cols = pl.ds(*self.spans[p])
        return remote(
            self.mine.at[self.here.other(e), :, cols], self.landed.at[m, :, cols], self.send.at[p, m], self.recv.at[p, m],
            self.here.toward(2 ** ((p + t) % n)),
        )

    def produce(self, low, high):
        here, rows, width = self.here, self.rows, self.width
        s, n, count = here.s, here.n, here.count
        tile = min(width, 512)

        @pl.loop(low, high)
        def _(i):
            @pl.when(i < count)
            def _():
                chip = here.other(count - 1 - i)

                def lines(s_of):
                    return pl.ds(pl.multiple_of((s_of * count + chip) * rows, rows), rows)

                lefts = [jnp.concatenate([a[lines(1 - s), :], a[lines(s), :]], axis=0) for a in self.a_refs]
                for c in range(0, width, tile):
                    if self.turned:
                        values = [back_dot(left, b[c : c + tile, :]) for left, b in zip(lefts, self.b_refs)]
                    else:
                        values = [forward_dot(left, b[:, c : c + tile]) for left, b in zip(lefts, self.b_refs)]
                    value = functools.reduce(jnp.add, values).astype(BF)
                    self.give[chip, :, c : c + tile] = value[:rows]
                    self.mine[chip, :, c : c + tile] = value[rows:]
                self.core(chip).start()

            @pl.when(i > 0)
            def _():
                e = count - i
                chip = here.other(e)
                arrived(self.core_in.at[chip], self.core_recv.at[chip])
                add_rows(self.mine.at[chip], [self.core_in.at[chip]])
                for p in self.parts:
                    pl.when(e // 2 ** ((p + n - 1) % n) % 2 == 1)(
                        lambda p=p: self.hand(p, here.positions(p, e), n - 1).start()
                    )

    def waiting(self, p, m):
        cols = pl.ds(*self.spans[p])
        terms = [m + 2**t for t in range(m.bit_length(), self.here.n)]
        for term in terms:
            arrived(self.landed.at[term, :, cols], self.recv.at[p, term])
        place = self.mine.at[self.here.other(self.here.dims(p, m)), :, cols]
        return place, [self.landed.at[term, :, cols] for term in terms]

    def pass_on(self, m):
        for p in self.parts:
            add_rows(*self.waiting(p, m))
            self.hand(p, m, m.bit_length() - 1).start()

    def settle(self):
        for p in self.parts:
            place, terms = self.waiting(p, 0)
            add_rows(place, terms, self.out_ref.at[:, pl.ds(*self.spans[p])])

    def drain(self):
        for chip in range(self.here.count):
            self.core(chip).wait_send()
        for m in range(1, self.here.count):
            for p in self.parts:
                self.hand(p, m, m.bit_length() - 1).wait_send()


def scatter_scratch(bits, block):
    n, count = len(bits), 2 ** len(bits)
    dma = pltpu.SemaphoreType.DMA
    return [pltpu.VMEM((count,) + block, BF)] * 4 + [dma((count,))] * 2 + [dma((n, count))] * 2


def scatter_kernel(bits, turned, homing, kinds, shares, terms, *refs):
    here = Place(bits)
    s, count = here.s, here.count
    along = len(kinds)
    a_refs, b_refs, refs = refs[:terms], refs[terms : 2 * terms], refs[2 * terms :]
    if homing:
        grad, refs = refs[0], refs[1:]
    rider_in, refs = refs[:along], refs[along:]
    out_ref, refs = refs[0], refs[1:]
    if homing:
        home, other_home = refs[:2]
        refs = refs[2:]
    rider_out, refs = refs[:along], refs[along:]
    work = Scatter(here, turned, shares, a_refs, b_refs, out_ref, refs[:8])
    if homing:
        q_in, ready, kept, kept_sem, q_send, q_recv, home_send, home_recv, over_send, over_recv = refs[8:18]
        keep = pltpu.make_async_copy(grad.at[lax.axis_index("q")], kept, kept_sem)
    ride_start, ride_end = ride(here, kinds, rider_in + rider_out + refs[len(refs) - 2 * along :])

    def to_q(e):
        q, chip = lax.axis_index("q"), here.other(e)
        return remote(grad.at[1 - q, chip], q_in.at[chip], q_send.at[e], q_recv.at[e], {"q": 1 - q})

    def to_chip(e):
        return remote(ready.at[here.other(e)], home.at[here.other(0)], home_send.at[e], home_recv.at[e], here.toward(e))

    def to_core(e):
        chip = here.other(e)
        return remote(home.at[chip], other_home.at[chip], over_send.at[e], over_recv.at[e], {"section": 1 - s})

    def home_step(e):
        chip = here.other(e)
        arrived(q_in.at[chip], q_recv.at[e])
        place = ready.at[chip] if e else home.at[chip]
        add_rows(q_in.at[chip], [kept.at[chip]], place)
        (to_chip(e) if e else to_core(0)).start()

    def home_end(e):
        if e:
            arrived(home.at[here.other(e)], home_recv.at[e])
            to_core(e).start()

    peers = work.peers
    if homing:
        peers = [here.names(e) for e in range(1, count)] + [("section",), ("q",)]
    here.meet(peers + rider_peers(here, kinds))
    if homing:
        for e in range(count):
            to_q(e).start()
        keep.start()
    ride_start()
    work.produce(0, count + 1)
    if homing:
        keep.wait()
    steps = count // 2
    for m in range(steps - 1, 0, -1):
        if homing:
            home_step(steps - 1 - m)
        work.pass_on(m)
    work.settle()
    if homing:
        for e in range(steps - 1, count):
            home_step(e)
        for e in range(count):
            home_end(e)
        for e in range(count):
            arrived(other_home.at[here.other(e)], over_recv.at[e])
            to_core(e).wait_send()
            to_q(e).wait_send()
            if e:
                to_chip(e).wait_send()
    ride_end()
    work.drain()


def scatter_columns(bits, cid, a, b, turned, grad=None, riders=(), shares=None):
    tokens, width = a[0].shape[0], b[0].shape[0 if turned else 1]
    count = 2 ** len(bits)
    block = (tokens // (2 * count), width)
    dma = pltpu.SemaphoreType.DMA
    operands = list(a) + list(b)
    shapes = [jax.ShapeDtypeStruct(block, F32)]
    scratch = scatter_scratch(bits, block)
    if grad is not None:
        operands += [grad]
        shapes += [jax.ShapeDtypeStruct(grad.shape[1:], BF)] * 2
        scratch += [pltpu.VMEM(grad.shape[1:], BF)] * 3 + [dma] + [dma((count,))] * 6
    arrays, more_shapes, more_scratch = rider_shapes(bits, riders)
    inside, outside = pl.BlockSpec(memory_space=pltpu.VMEM), pl.BlockSpec(memory_space=pl.ANY)
    return pl.pallas_call(
        functools.partial(
            scatter_kernel, bits, turned, grad is not None, tuple(kind for kind, _ in riders), shares, len(a)
        ),
        out_shape=shapes + more_shapes,
        in_specs=[inside] * (2 * len(a)) + [outside] * (len(operands) - 2 * len(a) + len(arrays)),
        out_specs=[inside] * len(shapes) + [outside] * len(arrays),
        scratch_shapes=scratch + more_scratch,
        compiler_params=pltpu.CompilerParams(
            collective_id=cid, has_side_effects=True, vmem_limit_bytes=56 * 2**20
        ),
        cost_estimate=lasting(40 if grad is None else 60),
    )(*operands, *arrays)


def scatter_dot(bits, cid, a, b, turned, grad=None, riders=(), shares=None):
    tokens, width = a[0].shape[0], b[0].shape[0 if turned else 1]
    pieces = max(1, tokens * width // 2**22)
    size = width // pieces
    cuts = [
        [f[i * size : (i + 1) * size] if turned else f[:, i * size : (i + 1) * size] for f in b] for i in range(pieces)
    ]
    first = scatter_columns(bits, cid, a, cuts[0], turned, grad, riders, shares)
    rest = [scatter_columns(bits, 14 + turned, a, cut, turned)[0] for cut in cuts[1:]]
    return [jnp.concatenate([first[0]] + rest, axis=1)] + list(first[1:])


def total_kernel(bits, kinds, x_ref, *refs):
    here = Place(bits)
    s, count = here.s, here.count
    along = len(kinds)
    rider_in, out_ref, rider_out, refs = refs[:along], refs[along], refs[along + 1 : 2 * along + 1], refs[2 * along + 1 :]
    part, core_in, ready, landed, done, pair_send, pair_recv, send, recv, back_send, back_recv = refs[:11]
    ride_start, ride_end = ride(here, kinds, rider_in + rider_out + refs[11:])
    lanes = part.shape[3]

    def span(s_of, chip):
        at = (s_of * count + chip) * lanes
        return slice(at, at + lanes)

    for s_of in range(2):
        for chip in range(count):
            part[s_of, chip] = x_ref[:, span(s_of, chip)]
    here.meet([here.names(e) for e in range(1, count)] + [("section",)] + rider_peers(here, kinds))
    first = remote(part.at[1 - s], core_in, pair_send.at[0], pair_recv.at[0], {"section": 1 - s})
    first.start()
    first.wait_recv()
    for chip in range(count):
        total = part[s, chip] + core_in[chip]
        part[s, chip] = total
        ready[chip] = total.astype(BF)

    def out(e):
        return remote(ready.at[here.other(e)], landed.at[e], send.at[e], recv.at[e], here.toward(e))

    def back(e):
        place = done.at[s, here.other(0)]
        return remote(place, place, back_send.at[e], back_recv.at[e], here.toward(e))

    others = range(1, count)
    for e in others:
        out(e).start()
    ride_start()
    total = part[s, here.other(0)]
    for e in others:
        out(e).wait_recv()
        total = total + landed[e].astype(F32)
    done[s, here.other(0)] = total.astype(BF)
    for e in others:
        back(e).start()
    for e in others:
        place = done.at[s, here.other(e)]
        arrived(place, back_recv.at[e])
    last = remote(done.at[s], done.at[s], pair_send.at[1], pair_recv.at[1], {"section": 1 - s})
    last.start()
    last.wait_recv()
    for s_of in range(2):
        for chip in range(count):
            out_ref[:, span(s_of, chip)] = done[s_of, chip]
    ride_end()
    first.wait_send()
    last.wait_send()
    for e in others:
        out(e).wait_send()
        back(e).wait_send()


def sum_columns(bits, cid, x, riders=()):
    rows, tokens = x.shape
    count = 2 ** len(bits)
    block = (rows, tokens // (2 * count))
    dma, vmem = pltpu.SemaphoreType.DMA, pltpu.VMEM
    arrays, more_shapes, more_scratch = rider_shapes(bits, riders)
    inside, outside = pl.BlockSpec(memory_space=pltpu.VMEM), pl.BlockSpec(memory_space=pl.ANY)
    return pl.pallas_call(
        functools.partial(total_kernel, bits, tuple(kind for kind, _ in riders)),
        out_shape=[jax.ShapeDtypeStruct((rows, tokens), BF)] + more_shapes,
        in_specs=[inside] + [outside] * len(arrays),
        out_specs=[inside] + [outside] * len(arrays),
        scratch_shapes=[
            vmem((2, count) + block, F32),
            vmem((count,) + block, F32),
            vmem((count,) + block, BF),
            vmem((count,) + block, BF),
            vmem((2, count) + block, BF),
        ]
        + [dma((2,))] * 2
        + [dma((count,))] * 4
        + more_scratch,
        compiler_params=pltpu.CompilerParams(
            collective_id=cid, has_side_effects=True, vmem_limit_bytes=56 * 2**20
        ),
        cost_estimate=lasting(22),
    )(x, *arrays)


def spread_kernel(bits, kinds, count_blocks, shard_ref, *refs):
    here = Place(bits)
    along = len(kinds)
    blocks, small, refs = refs[:count_blocks], refs[count_blocks], refs[count_blocks + 1 :]
    rider_in, refs = refs[:along], refs[along:]
    out_ref, rows, own_small, refs = refs[0], refs[1:3], refs[3], refs[4:]
    rider_out, refs = refs[:along], refs[along:]
    send, recv, pair_send, pair_recv, piece_send, piece_recv, small_send, small_recv = refs[:8]
    ride_start, ride_end = ride(here, kinds, rider_in + rider_out + refs[8:])
    s, q, chip, count = here.s, lax.axis_index("q"), here.other(0), here.count
    others = range(1, count)
    peers = [here.names(e) + extra for e in range(count) for extra in ((), ("section",)) if e or extra]
    here.meet(peers + [("q",), ("q", "section")])

    def block(i, s_of, chip_of):
        if count_blocks == 2:
            return blocks[i].at[s_of, chip_of]
        wide = blocks[0].shape[1] // (4 * count)
        return blocks[0].at[:, pl.ds(pl.multiple_of(((i * 2 + s_of) * count + chip_of) * wide, 128), wide)]

    def piece(i, r, e):
        where = dict(here.toward(e), **({"section": 1 - s} if r else {}))
        src = block(i, 1 - s if r else s, here.other(e))
        return remote(src, rows[i].at[chip], piece_send.at[i, r, e], piece_recv.at[i, e], where)

    def hand_small(k, where):
        return remote(small, own_small, small_send.at[k], small_recv, where)

    keep_pieces = [pltpu.make_async_copy(block(i, s, chip), rows[i].at[chip], piece_recv.at[i, 0]) for i in range(2)]
    keep_small = pltpu.make_async_copy(small, own_small, small_recv)
    at_layer = s == 0
    stays, leaves = jnp.logical_and(at_layer, q == s), jnp.logical_and(at_layer, q != s)

    out_ref[s, q, chip] = shard_ref[...]
    own = out_ref.at[s, q, chip]
    copies = [remote(own, own, send.at[e], recv.at[e], here.toward(e)) for e in others]
    for copy in copies:
        copy.start()
    ride_start()

    @pl.when(at_layer)
    def _():
        for i in range(2):
            keep_pieces[i].start()
            for e in range(count):
                for r in range(2):
                    if e or r:
                        piece(i, r, e).start()

    @pl.when(stays)
    def _():
        keep_small.start()
        hand_small(0, {"q": 1 - q}).start()

    @pl.when(leaves)
    def _():
        hand_small(0, {"section": 1 - s}).start()
        hand_small(1, {"section": 1 - s, "q": 1 - q}).start()

    for e in others:
        arrived(out_ref.at[s, q, here.other(e)], recv.at[e])
    place = out_ref.at[s, q]
    first = remote(place, place, pair_send.at[0], pair_recv.at[0], {"q": 1 - q})
    first.start()
    first.wait_recv()
    place = out_ref.at[s]
    second = remote(place, place, pair_send.at[1], pair_recv.at[1], {"section": 1 - s})
    second.start()
    second.wait_recv()
    ride_end()
    arrived(own_small, small_recv)
    for i in range(2):
        for e in range(count):
            arrived(rows[i].at[here.other(e)], piece_recv.at[i, e])
    for copy in copies + [first, second]:
        copy.wait_send()

    @pl.when(at_layer)
    def _():
        for i in range(2):
            for e in range(count):
                for r in range(2):
                    if e or r:
                        piece(i, r, e).wait_send()

    pl.when(stays)(lambda: hand_small(0, {"q": 1 - q}).wait_send())

    @pl.when(leaves)
    def _():
        hand_small(0, {"section": 1 - s}).wait_send()
        hand_small(1, {"section": 1 - s, "q": 1 - q}).wait_send()


def spread(bits, shard, blocks, small, riders):
    arrays, more_shapes, more_scratch = rider_shapes(bits, riders)
    width, count = shard.shape[0], 2 ** len(bits)
    block = (16, max(width, 128))
    padded = jnp.pad(shard[None, :], ((0, block[0] - 1), (0, block[1] - width)))
    dma = pltpu.SemaphoreType.DMA
    shapes = [jax.ShapeDtypeStruct((2, 2, count) + block, shard.dtype)]
    if len(blocks) == 2:
        piece = blocks[0].shape[1:]
    else:
        piece = (count, blocks[0].shape[0], blocks[0].shape[1] // (4 * count))
    shapes += [jax.ShapeDtypeStruct(piece, b.dtype) for b in (blocks[0], blocks[0])] + [jax.ShapeDtypeStruct(small.shape, small.dtype)]
    inside, outside = pl.BlockSpec(memory_space=pltpu.VMEM), pl.BlockSpec(memory_space=pl.ANY)
    out, *gots = pl.pallas_call(
        functools.partial(spread_kernel, bits, tuple(kind for kind, _ in riders), len(blocks)),
        out_shape=shapes + more_shapes,
        in_specs=[inside] + [outside] * (len(blocks) + 1 + len(arrays)),
        out_specs=[inside] + [outside] * (3 + len(arrays)),
        scratch_shapes=[dma((count,)), dma((count,)), dma((2,)), dma((2,))]
        + [dma((2, 2, count)), dma((2, count)), dma((2,)), dma]
        + more_scratch,
        compiler_params=pltpu.CompilerParams(collective_id=0, has_side_effects=True),
        cost_estimate=lasting(12),
    )(padded, *blocks, small, *arrays)
    return [out[:, :, :, 0, :width].reshape((2, -1))] + gots


def chips(bits):
    return tuple(reversed(bits))


def at_home():
    return lax.axis_index("q") == lax.axis_index("section")


def low_first(mine, other):
    low = lax.axis_index("q") == 0
    return jnp.stack([jnp.where(low, mine, other), jnp.where(low, other, mine)])


def by_q(pair):
    low = lax.axis_index("q") == 0
    return jnp.where(low, pair[0], pair[1]), jnp.where(low, pair[1], pair[0])


def leave(value):
    return lax.ppermute(value, ("section", "q"), [(0, 1), (3, 2)])


def home(value):
    return lax.ppermute(value, ("section", "q"), [(1, 0), (2, 3)])


def swap(value):
    return lax.ppermute(value, "q", [(0, 1), (1, 0)])


def after(value, *earlier):
    return lax.optimization_barrier((value,) + earlier)[0]


def column_blocks(bits, rows):
    parts = rows.reshape((rows.shape[0], 2, 2, 2 ** len(bits), -1))
    return [jnp.transpose(parts[:, i], (1, 2, 0, 3)) for i in range(2)]


def assemble_kernel(lower_refs, upper_refs, weight_ref, out_ref, gain_ref):
    depth = weight_ref.shape[0]
    step = min(depth, 32)

    def fill(parts):
        chips, _, wide = parts[0].shape

        @pl.loop(0, depth // step)
        def _(r):
            lines = pl.ds(pl.multiple_of(r * step, step), step)
            total = jnp.zeros((step, wide), F32)
            for i, part in enumerate(parts):
                for chip in range(chips):
                    at = (i * chips + chip) * wide
                    value = part[chip, lines, :].astype(F32)
                    out_ref[lines, at : at + wide] = value
                    total = total + value * weight_ref[lines, at : at + wide].astype(F32)
            gain_ref[lines, :] = jnp.sum(total, axis=1, keepdims=True)

    upper = lax.axis_index("section") == 1
    pl.when(jnp.logical_not(upper))(lambda: fill(lower_refs))
    pl.when(upper)(lambda: fill(upper_refs))


def assemble(lower, upper, weight):
    inside = pl.BlockSpec(memory_space=pltpu.VMEM)
    return pl.pallas_call(
        assemble_kernel,
        out_shape=[jax.ShapeDtypeStruct(weight.shape, F32), jax.ShapeDtypeStruct((weight.shape[0], 1), F32)],
        in_specs=[[inside] * 4, [inside] * 4, inside],
        out_specs=[inside, inside],
        compiler_params=pltpu.CompilerParams(vmem_limit_bytes=40 * 2**20),
    )(lower, upper, weight)


def silu_slope(v):
    gate = jax.nn.sigmoid(v)
    return gate, gate * (1.0 + v * (1.0 - gate))


def normalize(stream, gain):
    inverse = lax.rsqrt(jnp.mean(stream * stream, axis=-1, keepdims=True) + norm_eps)
    return inverse, (stream * inverse * gain[None, :]).astype(BF)


class Small:
    def __init__(self, packed):
        self.taps = packed[:KC].astype(F32)
        self.conv_bias = packed[KC].astype(F32)
        self.dt_bias = packed[KC + 1].astype(F32)
        self.skip = packed[KC + 2].astype(F32)
        self.dt = packed[KC + 3 : KC + 3 + R]
        self.xproj = packed[KC + 3 + R : KC + 3 + 2 * R + 2 * N]


def mixer_inputs(normed, in_inner, small):
    inner = forward_dot(normed, in_inner).astype(BF).astype(F32)
    tokens, channels = inner.shape
    extended = jnp.concatenate([jnp.zeros((KC - 1, channels), F32), inner], axis=0)
    conv = jnp.broadcast_to(small.conv_bias[None, :], (tokens, channels))
    for tap in range(KC):
        conv = conv + small.taps[tap][None, :] * extended[tap : tap + tokens]
    act = jax.nn.silu(conv)
    return extended, conv, act, back_dot(small.xproj, act.astype(BF))


def mixer(xproj, act, normed, in_gate, small):
    gate_in = forward_dot(normed, in_gate).astype(BF).astype(F32)
    key_t, query_t = xproj[R : R + N].astype(F32), xproj[R + N :].astype(F32)
    key_norm = jnp.sum(key_t * key_t, axis=0)[:, None]
    write = jax.nn.sigmoid(cross_dot(xproj[:R], small.dt) + small.dt_bias[None, :])
    rate = write / (1.0 + write * key_norm)
    recur, before, last = recur_forward(rate, act, key_t, query_t)
    recur = recur + small.skip[None, :] * act
    gated = (recur * jax.nn.silu(gate_in)).astype(BF)
    return gate_in, key_t, query_t, key_norm, write, rate, recur, gated, before, last


def gate_back(grad_low, out_weight, kept):
    gate_in, recur = kept[0], kept[6]
    d_gated = back_dot(grad_low, out_weight).astype(BF).astype(F32)
    gate, slope = silu_slope(gate_in)
    return d_gated * (gate_in * gate), (d_gated * recur * slope).astype(BF)


def mixer_back(bits, cid, d_recur, act, xproj, kept, small, riders, product=(), shares=None):
    key_t, query_t, key_norm, write, rate, recur, gated, before, last = kept[1:]
    d_skip = jnp.sum(d_recur * act, axis=0)
    d_rate, d_act_rec, d_key_t, d_query_t, *gots = recur_backward(
        bits, cid, rate, act, d_recur, key_t, query_t, before, last, riders, product, shares
    )
    share = 1.0 / (1.0 + write * key_norm)
    pulled = d_rate * share * share
    d_pre = pulled * write * (1.0 - write)
    d_key_rate = -2.0 * key_t * jnp.sum(pulled * write * write, axis=1)[None, :]
    d_dt_bias = jnp.sum(d_pre, axis=0)
    d_delta = d_pre.astype(BF)
    d_dt = forward_dot(xproj[:R], d_delta)
    d_xproj = jnp.concatenate([back_dot(small.dt, d_delta), d_key_t + d_key_rate, d_query_t], axis=0)
    return d_act_rec, d_xproj, (d_dt_bias[None], d_skip[None], d_dt), gots


def inputs_back(d_xproj, d_recur, d_act_rec, extended, conv, act, small):
    tokens = act.shape[0]
    d_act = cross_dot(d_xproj, small.xproj) + small.skip[None, :] * d_recur + d_act_rec
    d_conv = d_act * silu_slope(conv)[1]
    d_taps = jnp.stack([jnp.sum(d_conv * extended[tap : tap + tokens], axis=0) for tap in range(KC)])
    d_bias = jnp.sum(d_conv, axis=0)
    later = jnp.concatenate([d_conv, jnp.zeros((KC - 1, d_conv.shape[1]), F32)], axis=0)
    d_inner = sum(small.taps[tap][None, :] * later[KC - 1 - tap : KC - 1 - tap + tokens] for tap in range(KC))
    return d_inner.astype(BF), (d_taps, d_bias[None]), forward_dot(d_xproj, act.astype(BF))


def norm_back(grad_out, d_normed, stream, inverse, gain):
    scaled = gain[None, :] * d_normed
    mean = jnp.mean(stream * scaled, axis=-1, keepdims=True)
    return grad_out + inverse * scaled - stream * inverse**3 * mean


def pack(first, second, third):
    packed = jnp.concatenate(first + second + (third,), axis=0)
    return jnp.pad(packed, ((0, -packed.shape[0] % 16), (0, 0)))


def on_device(
    bits, hidden_in, cotangent, norm_gain, in_weight, conv_weight, conv_bias, xproj_weight, dt_weight, dt_bias, skip_gain, out_weight
):
    packed = pack(
        (conv_weight[0], conv_bias),
        (dt_bias, skip_gain, dt_weight[0]),
        jnp.swapaxes(xproj_weight[0], 0, 1),
    )
    rows = in_weight[0]
    channels = conv_bias.shape[1]
    aligned = channels % 128 == 0
    blocks = [rows] if aligned else column_blocks(bits, rows)
    tight = (2, 5, 9)

    def weight(pair):
        return pair.reshape((-1, pair.shape[-1]))

    def weight_grad(normed, d_out):
        return cross_dot(normed, d_out).astype(BF).reshape((2, 2 ** len(bits), rows.shape[0], channels))

    mine, others = by_q(hidden_in)
    gains, inner, gate, packed0, got = spread(bits, norm_gain[0], blocks, packed, [("leave", others)])
    gains = gains.astype(F32)
    stream0 = jnp.where(at_home(), mine, got).astype(F32)

    inverse0, normed = normalize(stream0, gains[0])
    normed0, inner, gate, *sent = gather_call(
        bits, 1, [normed], shares=tight, us=60,
        riders=[("stack", inner), ("stack", gate)] + ([("over_cols0", rows), ("over_cols1", rows)] if aligned else [("over_at", b) for b in blocks])
        + [("out1", packed)] + [("out%d" % l, out_weight[0]) for l in range(2)],
    )
    upper = lax.axis_index("section") == 1
    if aligned:
        slab = rows.shape[1] // 4
        columns = [("cube_cols", jnp.where(upper, rows[:, slab : 2 * slab], sent[0]))]
        columns += [("cube_cols", jnp.where(upper, rows[:, 3 * slab :], sent[1]))]
    else:
        columns = [("cube", jnp.where(upper, b[1], got)) for b, got in zip(blocks, sent)]
    packed_held = jnp.where(upper, packed, sent[2])
    out_held = jnp.where(upper, sent[3], out_weight[0]), jnp.where(upper, out_weight[0], sent[4])
    inner0, small0 = weight(inner), Small(packed0)
    extended0, conv0, act0, part = mixer_inputs(normed0, inner0, small0)
    part = after(part, out_held[0])
    xproj0, inner, late_gate = sum_columns(bits, 4, part, columns)
    gate0 = weight(gate)
    out0 = jnp.where(at_home(), out_held[0], leave(after(out_held[0], xproj0)))
    kept0 = mixer(xproj0, act0, normed0, gate0, small0)
    grad_mine, grad_others = by_q(cotangent)
    added, got, grad_got, gate = scatter_dot(
        bits, 8, [kept0[7]], [out0], False, shares=(3, 5, 8),
        riders=[("leave", packed_held), ("leave", grad_others.astype(BF)), ("stack", late_gate)],
    )
    gate1 = weight(gate)
    grad1 = jnp.where(at_home(), grad_mine, grad_got.astype(F32))
    small1 = Small(jnp.where(at_home(), packed_held, got))
    output0 = (stream0 + added).astype(BF)

    stream1 = output0.astype(F32)
    inverse1, normed = normalize(stream1, gains[1])
    normed1, grad_low1, inner = gather_call(
        bits, 2, [normed, grad1.astype(BF)], riders=[("stack", inner)], shares=(4, 5, 7), us=65
    )
    inner1 = weight(inner)
    extended1, conv1, act1, part = mixer_inputs(normed1, inner1, small1)
    xproj1, output0_home = sum_columns(bits, 5, after(part, out_held[1]), [("home", output0)])
    out1 = jnp.where(at_home(), out_held[1], leave(after(out_held[1], xproj1)))
    kept1 = mixer(xproj1, act1, normed1, gate1, small1)

    d_out1 = cross_dot(kept1[7], grad_low1).astype(BF)
    d_recur, d_gate1 = gate_back(grad_low1, out1, kept1)
    keep, give = by_q(weight_grad(normed1, d_gate1))
    beside = kept1[7].shape[0] * out1.shape[1] <= 2**22 and kept1[7].shape[0] >= 16 * BLOCK
    if beside:
        d_act_rec, part, d_small, (added, got) = mixer_back(
            bits, 16, d_recur, act1, xproj1, kept1, small1, [("swap", give)], (kept1[7], out1), (4, 5, 7)
        )
    else:
        (added,) = scatter_dot(bits, 10, [kept1[7]], [out1], False)
        d_act_rec, part, d_small, (got,) = mixer_back(bits, 16, d_recur, act1, xproj1, kept1, small1, [("swap", give)])
    output1 = (stream1 + added).astype(BF)
    d_xproj, output1_home = sum_columns(bits, 6, part, [("home", output1)])
    d_gate_in1 = (keep.astype(F32) + got.astype(F32)).astype(BF)
    d_inner, d_conv, d_xproj_weight = inputs_back(d_xproj, d_recur, d_act_rec, extended1, conv1, act1, small1)
    d_packed1 = pack(d_conv, d_small, d_xproj_weight)
    d_normed, d_gate_in1, d_packed1_home, d_out1_home = scatter_dot(
        bits, 11, [d_inner, d_gate1], [inner1, gate1], True,
        riders=[("cube", d_gate_in1), ("home", d_packed1.astype(BF)), ("home", d_out1)], shares=(4, 5, 7),
    )
    keep, give = by_q(weight_grad(normed1, d_inner))
    input_grad1 = norm_back(grad1, d_normed, stream1, inverse1, gains[1])
    grad0 = input_grad1.astype(BF)
    grad_low0, got, grad1_home = gather_call(
        bits, 3, [grad0], riders=[("swap", give), ("home", grad0)], shares=(3, 5, 8), us=45
    )
    d_inner1 = (keep.astype(F32) + got.astype(F32)).astype(BF)

    d_out0 = cross_dot(kept0[7], grad_low0).astype(BF)
    d_recur, d_gate0 = gate_back(grad_low0, out0, kept0)
    keep, give = by_q(weight_grad(normed0, d_gate0))
    d_act_rec, part, d_small, (got, d_inner1) = mixer_back(
        bits, 17, d_recur, act0, xproj0, kept0, small0, [("swap", give), ("cube", d_inner1)]
    )
    d_gate_in0 = (keep.astype(F32) + got.astype(F32)).astype(BF)
    d_xproj, d_gate_in0, d_out0_home = sum_columns(
        bits, 7, part, [("cube", d_gate_in0), ("home", d_out0)]
    )
    d_inner, d_conv, d_xproj_weight = inputs_back(d_xproj, d_recur, d_act_rec, extended0, conv0, act0, small0)
    d_packed0 = pack(d_conv, d_small, d_xproj_weight)
    d_out = [
        (mine.astype(F32) + other.astype(F32)).astype(BF) for mine, other in ((d_out0, d_out0_home), (d_out1, d_out1_home))
    ]
    d_packed1 = (d_packed1 + d_packed1_home.astype(F32)).astype(BF)
    gate_over = jnp.where(upper, d_gate_in0, d_gate_in1)
    d_normed, d_inner0, d_inner0_other, d_packed0_home, inner_other, gate_other, *backs = scatter_dot(
        bits, 13, [d_inner, d_gate0], [inner0, gate0], True, weight_grad(normed0, d_inner), shares=(3, 5, 8),
        riders=[
            ("home", d_packed0.astype(BF)), ("over", d_inner1), ("over", gate_over), ("back0", d_out[0]), ("back1", d_out[1]),
            ("back1", d_packed1), ("back0", output0), ("back0", output0_home), ("back1", output1), ("back1", output1_home),
            ("back1", grad0), ("back1", grad1_home),
        ],
    )
    input_grad0 = norm_back(grad0.astype(F32), d_normed, stream0, inverse0, gains[0]).astype(BF)

    def settled(lower, upper_one, lower_back, upper_back):
        return jnp.where(at_home(), jnp.where(upper, upper_one, lower), jnp.where(upper, upper_back, lower_back))

    d_out = settled(*d_out, *backs[:2]).astype(F32)
    d_packed0 = (d_packed0 + d_packed0_home.astype(F32)).astype(BF)
    d_packed = settled(d_packed0, d_packed1, lax.ppermute(d_packed0, ("section", "q"), [(3, 1)]), backs[2]).astype(F32)
    low = lax.axis_index("q") == 0
    mine, other = settled(output0, output1, backs[3], backs[5]), settled(output0_home, output1_home, backs[4], backs[6])
    layer_outputs = low_first(mine, other).astype(F32)
    mine, other = jnp.where(at_home(), grad0, backs[7]), jnp.where(at_home(), grad1_home, backs[8])
    grads1 = low_first(mine, other)
    of_first = lax.ppermute(input_grad0, ("section", "q"), [(2, 1)])
    of_second = lax.ppermute(input_grad0, ("section", "q"), [(1, 0), (3, 1)])
    grads0 = jnp.stack([jnp.where(low, input_grad0, of_first), of_second])
    input_grads = jnp.where(upper, grads1, grads0).astype(F32)
    d_in, d_gain = assemble(
        [d_inner0, d_inner0_other, d_gate_in0, gate_other], [inner_other, d_inner1, gate_other, d_gate_in1], in_weight[0]
    )
    d_gain = d_gain[:, 0] / norm_gain[0].astype(F32)
    return (
        layer_outputs[None],
        input_grads[None],
        d_gain[None],
        d_in[None],
        d_packed[None, :KC],
        d_packed[None, KC],
        jnp.swapaxes(d_packed[KC + 3 + R : KC + 3 + 2 * R + 2 * N], 0, 1)[None],
        d_packed[None, KC + 3 : KC + 3 + R],
        d_packed[None, KC + 1],
        d_packed[None, KC + 2],
        d_out[None],
    )


def solution(mesh):
    sections, chip_count = mesh.devices.shape
    n = chip_count.bit_length() - 2
    bits = tuple("c%d" % d for d in range(n))
    split = Mesh(mesh.devices.reshape((sections,) + (2,) * (n + 1)), ("section", "q") + chips(bits))
    seq = ("q",) + chips(bits)
    placed = (
        P(None, seq, None),
        P(None, seq, None),
        P("section", seq),
        P("section", seq, None),
        P("section", None, seq),
        P("section", seq),
        P("section", seq, None),
        P("section", None, seq),
        P("section", seq),
        P("section", seq),
        P("section", seq, None),
    )
    return jax.shard_map(
        functools.partial(on_device, bits),
        mesh=split,
        in_specs=placed,
        out_specs=(P("section", None, seq, None), P("section", None, seq, None)) + placed[2:],
        check_vma=False,
    )
```

```python
import functools

import jax
import jax.numpy as jnp
from jax import lax
from jax.experimental import pallas as pl
from jax.experimental.pallas import tpu as pltpu
from jax.sharding import Mesh, PartitionSpec as P


N = 16
R = 128
KC = 4
BLOCK = 128
norm_eps = 1e-05
BF = jnp.bfloat16
F32 = jnp.float32
MESH = pl.DeviceIdType.MESH


def forward_dot(operand, factor):
    return jnp.dot(operand, factor, preferred_element_type=F32)


def cross_dot(operand, factor):
    return lax.dot_general(operand, factor, (((0,), (0,)), ((), ())), preferred_element_type=F32)


def back_dot(operand, factor):
    return lax.dot_general(operand, factor, (((1,), (1,)), ((), ())), preferred_element_type=F32)


def lasting(us):
    return pl.CostEstimate(flops=0, bytes_accessed=int(us * 3.4e6), transcendentals=0)


def widths(channels):
    wide = min(channels, 128)
    return wide, channels // wide


def sum_rows(pieces):
    row = lax.broadcasted_iota(jnp.int32, pieces[0].shape, 0)
    shift = 1
    while len(pieces) > 1:
        keep = (row & shift) == 0
        pieces = [
            jnp.where(keep, a, b) + pltpu.roll(jnp.where(keep, b, a), shift, 0)
            for a, b in zip(pieces[0::2], pieces[1::2])
        ]
        shift *= 2
    return pieces[0]


def halves(v):
    return v[:8] + v[8:]


def lanes_of(p, wide):
    return slice(p * wide, (p + 1) * wide)


def recur_forward_kernel(rate_ref, act_ref, key_ref, query_ref, out_ref, before_ref, last_ref, memory_ref):
    wide, parts = widths(rate_ref.shape[1])

    @pl.when(pl.program_id(0) == 0)
    def _():
        memory_ref[...] = jnp.zeros_like(memory_ref)

    memory = [memory_ref[:, lanes_of(p, wide)] for p in range(parts)]
    for base in range(0, rate_ref.shape[0], 8):
        rates = rate_ref[base : base + 8, :]
        feeds = rates * act_ref[base : base + 8, :]
        sums = [[] for _ in range(parts)]
        for i in range(8):
            key = jnp.broadcast_to(key_ref[:, base + i : base + i + 1], (N, wide))
            query = jnp.broadcast_to(query_ref[:, base + i : base + i + 1], (N, wide))
            square = key * key
            for p in range(parts):
                lanes = lanes_of(p, wide)
                before_ref[base + i, :, lanes] = memory[p]
                memory[p] = (1.0 - rates[i : i + 1, lanes] * square) * memory[p] + key * feeds[i : i + 1, lanes]
                sums[p].append(halves(memory[p] * query))
        for p in range(parts):
            out_ref[base : base + 8, lanes_of(p, wide)] = sum_rows(sums[p])
    for p in range(parts):
        memory_ref[:, lanes_of(p, wide)] = memory[p]

    @pl.when(pl.program_id(0) == pl.num_programs(0) - 1)
    def _():
        last_ref[...] = memory_ref[...]


def recur_forward(rate, act, key_t, query_t):
    tokens, channels = rate.shape
    rows = pl.BlockSpec((BLOCK, channels), lambda i: (i, 0))
    cols = pl.BlockSpec((N, BLOCK), lambda i: (0, i))
    return pl.pallas_call(
        recur_forward_kernel,
        grid=(tokens // BLOCK,),
        in_specs=[rows, rows, cols, cols],
        out_specs=[
            rows,
            pl.BlockSpec((BLOCK, N, channels), lambda i: (i, 0, 0)),
            pl.BlockSpec((N, channels), lambda i: (0, 0)),
        ],
        out_shape=[
            jax.ShapeDtypeStruct((tokens, channels), F32),
            jax.ShapeDtypeStruct((tokens, N, channels), F32),
            jax.ShapeDtypeStruct((N, channels), F32),
        ],
        scratch_shapes=[pltpu.VMEM((N, channels), F32)],
        compiler_params=pltpu.CompilerParams(
            dimension_semantics=("arbitrary",), vmem_limit_bytes=40 * 2**20
        ),
        cost_estimate=lasting(1),
    )(rate, act, key_t, query_t)


def recur_backward_kernel(bits, kinds, shares, steps, rate_ref, act_ref, grad_ref, key_ref, query_ref, before_ref, last_ref, *refs):
    along, beside = len(kinds), 1 if steps else 0
    product, refs = refs[: 2 * beside], refs[2 * beside :]
    rider_in, refs = refs[:along], refs[along:]
    d_rate_ref, d_act_ref, d_key_ref, d_query_ref = refs[:4]
    scattered, refs = refs[4 : 4 + beside], refs[4 + beside :]
    rider_out, refs = refs[:along], refs[along:]
    lam_ref, memory_ref, key_rows, query_rows = refs[:4]
    here = Place(bits)
    ride_start, ride_end = ride(here, kinds, rider_in + rider_out + refs[len(refs) - 2 * along :])
    stages = {}
    peers = rider_peers(here, kinds)
    if beside:
        work = Scatter(here, False, shares, product[:1], product[1:], scattered[0], refs[4:12])
        peers = peers + work.peers
        half = here.count // 2
        for k in range(half + 1):
            stages[k] = functools.partial(work.produce, 2 * k, min(2 * k + 2, here.count + 1))
        for k, m in enumerate(range(half - 1, 0, -1)):
            stages[steps - 1 - 2 * (half - 1 - k)] = functools.partial(work.pass_on, m)
    wide, parts = widths(rate_ref.shape[1])
    block = rate_ref.shape[0]

    @pl.when(pl.program_id(0) == 0)
    def _():
        here.meet(peers)
        ride_start()
        lam_ref[...] = jnp.zeros_like(lam_ref)
        memory_ref[...] = last_ref[...]

    for at, stage in stages.items():
        pl.when(pl.program_id(0) == at)(stage)
    lam = [lam_ref[:, lanes_of(p, wide)] for p in range(parts)]
    memory = [memory_ref[:, lanes_of(p, wide)] for p in range(parts)]
    for base in reversed(range(0, block, 8)):
        rates = rate_ref[base : base + 8, :]
        acts = act_ref[base : base + 8, :]
        grads = grad_ref[base : base + 8, :]
        d_rates = [[None] * 8 for _ in range(parts)]
        d_acts = [[None] * 8 for _ in range(parts)]
        for i in reversed(range(8)):
            at = base + i
            key = jnp.broadcast_to(key_ref[:, at : at + 1], (N, wide))
            query = jnp.broadcast_to(query_ref[:, at : at + 1], (N, wide))
            square = key * key
            key_sum = query_sum = None
            for p in range(parts):
                lanes = lanes_of(p, wide)
                grad = grads[i : i + 1, lanes]
                before = before_ref[at, :, lanes]
                pulled = query * grad + lam[p]
                kept = key * before
                missing = acts[i : i + 1, lanes] - kept
                keyed = pulled * key
                scaled = pulled * rates[i : i + 1, lanes]
                d_acts[p][i] = halves(keyed)
                d_rates[p][i] = halves(keyed * missing)
                to_key = scaled * (missing - kept)
                to_query = memory[p] * grad
                key_sum = to_key if key_sum is None else key_sum + to_key
                query_sum = to_query if query_sum is None else query_sum + to_query
                lam[p] = pulled - scaled * square
                memory[p] = before
            key_rows[at * N : (at + 1) * N, :] = key_sum.astype(BF)
            query_rows[at * N : (at + 1) * N, :] = query_sum.astype(BF)
        for p in range(parts):
            lanes = lanes_of(p, wide)
            d_rate_ref[base : base + 8, lanes] = sum_rows(d_rates[p])
            d_act_ref[base : base + 8, lanes] = rates[:, lanes] * sum_rows(d_acts[p])
    for p in range(parts):
        lam_ref[:, lanes_of(p, wide)] = lam[p]
        memory_ref[:, lanes_of(p, wide)] = memory[p]

    ones = jnp.ones((wide, block), BF)
    token = lax.broadcasted_iota(jnp.int32, (block, N, block), 0)
    own = token == lax.broadcasted_iota(jnp.int32, (block, N, block), 2)
    for rows, result in ((key_rows, d_key_ref), (query_rows, d_query_ref)):
        sums = forward_dot(rows[...], ones).reshape(block, N, block)
        result[...] = jnp.sum(jnp.where(own, sums, 0.0), axis=0)

    @pl.when(pl.program_id(0) == pl.num_programs(0) - 1)
    def _():
        if beside:
            work.settle()
            work.drain()
        ride_end()


def recur_backward(bits, cid, rate, act, grad, key_t, query_t, before, last, riders, product=(), shares=None):
    tokens, channels = rate.shape
    count = tokens // BLOCK
    rows = pl.BlockSpec((BLOCK, channels), lambda i: (count - 1 - i, 0))
    cols = pl.BlockSpec((N, BLOCK), lambda i: (0, count - 1 - i))
    products = pltpu.VMEM((BLOCK * N, widths(channels)[0]), BF)
    arrays, more_shapes, more_scratch = rider_shapes(bits, riders)
    outside = [pl.BlockSpec(memory_space=pl.ANY)] * len(arrays)
    inside = [pl.BlockSpec(memory_space=pltpu.VMEM)] * len(product)
    if product:
        block = (tokens // 2 ** (len(bits) + 1), product[1].shape[1])
        more_shapes = [jax.ShapeDtypeStruct(block, F32)] + more_shapes
        more_scratch = scatter_scratch(bits, block) + more_scratch
    return pl.pallas_call(
        functools.partial(
            recur_backward_kernel, bits, tuple(kind for kind, _ in riders), shares, count if product else 0
        ),
        grid=(count,),
        in_specs=[
            rows, rows, rows, cols, cols,
            pl.BlockSpec((BLOCK, N, channels), lambda i: (count - 1 - i, 0, 0)),
            pl.BlockSpec((N, channels), lambda i: (0, 0)),
        ] + inside + outside,
        out_specs=[rows, rows, cols, cols] + inside[:1] + outside,
        out_shape=[
            jax.ShapeDtypeStruct((tokens, channels), F32),
            jax.ShapeDtypeStruct((tokens, channels), F32),
            jax.ShapeDtypeStruct((N, tokens), F32),
            jax.ShapeDtypeStruct((N, tokens), F32),
        ] + more_shapes,
        scratch_shapes=[pltpu.VMEM((N, channels), F32), pltpu.VMEM((N, channels), F32), products, products]
        + more_scratch,
        compiler_params=pltpu.CompilerParams(
            dimension_semantics=("arbitrary",), vmem_limit_bytes=56 * 2**20, collective_id=cid, has_side_effects=True
        ),
        cost_estimate=lasting(1),
    )(rate, act, grad, key_t, query_t, before, last, *product, *arrays)


class Place:
    def __init__(self, bits):
        self.bits = bits
        self.n = len(bits)
        self.count = 2**self.n
        self.at = [lax.axis_index(name) for name in bits]
        self.s = lax.axis_index("section")

    def other(self, e):
        return sum(2**d * (c + e // 2**d % 2 * (1 - 2 * c)) for d, c in enumerate(self.at))

    def toward(self, e):
        return {self.bits[d]: 1 - self.at[d] for d in range(self.n) if e // 2**d % 2}

    def dims(self, p, m):
        return sum(2 ** ((p + t) % self.n) for t in range(self.n) if m // 2**t % 2)

    def positions(self, p, e):
        return sum(2**t * (e // 2 ** ((p + t) % self.n) % 2) for t in range(self.n))

    def names(self, e):
        return tuple(self.bits[d] for d in range(self.n) if e // 2**d % 2)

    def meet(self, peers):
        barrier = pltpu.get_barrier_semaphore()
        peers = list(dict.fromkeys(peers))
        for axes in peers:
            where = {name: 1 - lax.axis_index(name) for name in axes}
            pl.semaphore_signal(barrier, inc=1, device_id=where, device_id_type=MESH)
        pl.semaphore_wait(barrier, len(peers))


def spans_of(width, n, shares=None):
    tiles = width // 128
    sizes = [(tiles // n + (p < tiles % n)) * 128 for p in range(n)]
    if shares is not None and len(shares) == n and sum(shares) == tiles:
        sizes = [share * 128 for share in shares]
    return [(sum(sizes[:p]), size) for p, size in enumerate(sizes)]


def remote(src, dst, send, recv, where):
    return pltpu.make_async_remote_copy(
        src_ref=src, dst_ref=dst, send_sem=send, recv_sem=recv, device_id=where, device_id_type=MESH
    )


def arrived(place, sem):
    pltpu.make_async_copy(place, place, sem).wait()


def rider_peers(here, kinds):
    peers = [here.names(e) for e in range(1, here.count)] if set(kinds) & {"cube", "cube_cols"} else []
    if set(kinds) & {"swap", "stack", "home", "leave"}:
        peers.append(("q",))
    if set(kinds) & {"over", "over_at", "over_cols0", "over_cols1", "out0", "out1", "back0", "back1"}:
        peers.append(("section",))
    return peers


def ride(here, kinds, refs):
    k = len(kinds)
    riders = list(zip(kinds, refs[:k], refs[k : 2 * k], refs[2 * k : 3 * k], refs[3 * k :]))
    q, chip = lax.axis_index("q"), here.other(0)

    def row(kind, src, at):
        if kind == "cube":
            return src.at[at]
        wide = src.shape[1] // here.count
        return src.at[:, pl.ds(pl.multiple_of(at * wide, 128), wide)]

    def copies(kind, src, dst, send, recv):
        if kind in ("cube", "cube_cols"):
            return [
                remote(row(kind, src, here.other(e)), dst.at[chip], send.at[e], recv.at[e], here.toward(e))
                for e in range(1, here.count)
            ]
        if kind in ("over", "over_at") or kind[:-1] in ("out", "back", "over_cols"):
            src = src.at[1 - here.s] if kind == "over_at" else src
            if kind[:-1] == "over_cols":
                wide = src.shape[1] // 4
                src = src.at[:, pl.ds(pl.multiple_of((int(kind[-1]) * 2 + 1 - here.s) * wide, 128), wide)]
            return [remote(src, dst, send.at[0], recv.at[0], {"section": 1 - here.s})]
        return [remote(src, dst.at[q] if kind == "stack" else dst, send.at[0], recv.at[0], {"q": 1 - q})]

    def when(kind, sending, do):
        if kind in ("home", "leave"):
            pl.when((q != here.s) if sending == (kind == "home") else (q == here.s))(do)
        elif kind[:-1] in ("out", "back"):
            at_layer = (here.s == int(kind[-1])) if sending == (kind[:-1] == "out") else (here.s != int(kind[-1]))
            away = (q != here.s) if sending == (kind[:-1] == "out") else (q == here.s)
            pl.when(jnp.logical_and(at_layer, away))(do)
        else:
            do()

    def start():
        for kind, src, dst, send, recv in riders:
            if kind in ("cube", "cube_cols"):
                pltpu.make_async_copy(row(kind, src, chip), dst.at[chip], recv.at[0]).start()
            if kind == "stack":
                pltpu.make_async_copy(src, dst.at[q], recv.at[1]).start()
            for copy in copies(kind, src, dst, send, recv):
                when(kind, True, copy.start)

    def finish():
        for kind, src, dst, send, recv in riders:
            if kind in ("cube", "cube_cols"):
                for e in range(here.count):
                    arrived(dst.at[here.other(e)], recv.at[e])
            elif kind == "stack":
                arrived(dst.at[1 - q], recv.at[0])
                arrived(dst.at[q], recv.at[1])
            else:
                when(kind, False, lambda: arrived(dst, recv.at[0]))
            for copy in copies(kind, src, dst, send, recv):
                when(kind, True, copy.wait_send)

    return start, finish


def rider_shapes(bits, riders):
    sems = pltpu.SemaphoreType.DMA((2 ** len(bits),))
    def made(kind, shape):
        if kind == "over_at":
            return shape[1:]
        if kind[:-1] == "over_cols":
            return (shape[0], shape[1] // 4)
        if kind == "cube_cols":
            return (2 ** len(bits), shape[0], shape[1] // 2 ** len(bits))
        return ((2,) if kind == "stack" else ()) + shape

    shapes = [jax.ShapeDtypeStruct(made(kind, array.shape), array.dtype) for kind, array in riders]
    return [array for _, array in riders], shapes, [sems] * (2 * len(riders))


def gather_kernel(bits, total, kinds, shares, *refs):
    here = Place(bits)
    n, s, count = here.n, here.s, here.count
    chip, along = here.other(0), len(kinds)
    inputs, refs = refs[: total + along], refs[total + along :]
    outputs, sems = refs[: total + along], refs[total + along :]
    given, made = inputs[:total], outputs[:total]
    ride_start, ride_end = ride(here, kinds, inputs[total:] + outputs[total:] + sems[len(sems) - 2 * along :])
    local_sem, send, recv, core_send, core_recv = sems[:5]
    spans = spans_of(given[0].shape[1], n, shares)
    parts = [(k, p) for k in range(total) for p in range(n) if spans[p][1]]

    def block(k, e, p, s_of):
        return made[k].at[s_of, here.other(e), :, pl.ds(*spans[p])]

    def source(k, e, p):
        return block(k, e, p, s) if e else given[k].at[:, pl.ds(*spans[p])]

    def deliver(k, p, m):
        t = m.bit_length() - 1
        held = here.dims(p, m - 2**t)
        where = here.toward(2 ** ((p + t) % n))
        return remote(source(k, held, p), block(k, held, p, s), send.at[k, p, m], recv.at[k, p, m], where)

    def core(k, p, m):
        held = here.dims(p, m)
        sems = core_send.at[k, p, m], core_recv.at[k, p, m]
        return remote(source(k, held, p), block(k, held, p, s), *sems, {"section": 1 - s})

    here.meet([here.names(2**d) for d in range(n)] + [("section",)] + rider_peers(here, kinds))
    own = [pltpu.make_async_copy(given[k], made[k].at[s, chip], local_sem.at[k]) for k in range(total)]
    for k in range(total):
        for t in range(n):
            for p in range(n):
                if spans[p][1]:
                    deliver(k, p, 2**t).start()
        own[k].start()
    ride_start()
    for k, p in parts:
        core(k, p, 0).start()
    for m in range(1, count):
        for k, p in parts:
            arrived(block(k, here.dims(p, m), p, s), recv.at[k, p, m])
            for t in range(m.bit_length(), n):
                deliver(k, p, m + 2**t).start()
            core(k, p, m).start()
    for copy in own:
        copy.wait()
    for m in range(count):
        for k, p in parts:
            arrived(block(k, here.dims(p, m), p, 1 - s), core_recv.at[k, p, m])
    for m in range(count):
        for k, p in parts:
            core(k, p, m).wait_send()
            if m:
                deliver(k, p, m).wait_send()
    ride_end()


def gather_call(bits, cid, shards, riders=(), shares=None, us=35):
    rows, width = shards[0].shape
    n = len(bits)
    count = 2**n
    dma = pltpu.SemaphoreType.DMA
    sems = dma((len(shards), n, count))
    shapes = [jax.ShapeDtypeStruct((2, count, rows, width), shard.dtype) for shard in shards]
    scratch = [dma((len(shards),)), sems, sems, sems, sems]
    arrays, more_shapes, more_scratch = rider_shapes(bits, riders)
    shapes += more_shapes
    out = pl.pallas_call(
        functools.partial(gather_kernel, bits, len(shards), tuple(kind for kind, _ in riders), shares),
        out_shape=shapes,
        in_specs=[pl.BlockSpec(memory_space=pl.ANY)] * len(shapes),
        out_specs=[pl.BlockSpec(memory_space=pl.ANY)] * len(shapes),
        scratch_shapes=scratch + more_scratch,
        compiler_params=pltpu.CompilerParams(collective_id=cid, has_side_effects=True),
        cost_estimate=lasting(us),
    )(*shards, *arrays)
    return [o.reshape((-1, width)) for o in out[: len(shards)]] + list(out[len(shards) :])


def add_rows(place, terms, out=None):
    step = 32
    out = place if out is None else out

    @pl.loop(0, place.shape[0] // step)
    def _(r):
        lines = pl.ds(pl.multiple_of(r * step, step), step)
        total = place[lines, :].astype(F32)
        for term in terms:
            total = total + term[lines, :].astype(F32)
        out[lines, :] = total.astype(out.dtype)


class Scatter:
    def __init__(self, here, turned, shares, a_refs, b_refs, out_ref, scratch):
        self.here, self.turned, self.a_refs, self.b_refs, self.out_ref = here, turned, a_refs, b_refs, out_ref
        self.mine, self.give, self.core_in, self.landed, self.core_send, self.core_recv, self.send, self.recv = scratch
        self.rows, self.width = out_ref.shape
        self.spans = spans_of(self.width, here.n, shares)
        self.parts = [p for p in range(here.n) if self.spans[p][1]]
        self.peers = [here.names(2**d) for d in range(here.n)] + [("section",)]

    def core(self, chip):
        sems = self.core_send.at[chip], self.core_recv.at[chip]
        return remote(self.give.at[chip], self.core_in.at[chip], *sems, {"section": 1 - self.here.s})

    def hand(self, p, m, t):
        n = self.here.n
        e = sum(2 ** ((p + u) % n) * (m // 2**u % 2) for u in range(n))
        cols = pl.ds(*self.spans[p])
        return remote(
            self.mine.at[self.here.other(e), :, cols], self.landed.at[m, :, cols], self.send.at[p, m], self.recv.at[p, m],
            self.here.toward(2 ** ((p + t) % n)),
        )

    def produce(self, low, high):
        here, rows, width = self.here, self.rows, self.width
        s, n, count = here.s, here.n, here.count
        tile = min(width, 512)

        @pl.loop(low, high)
        def _(i):
            @pl.when(i < count)
            def _():
                chip = here.other(count - 1 - i)

                def lines(s_of):
                    return pl.ds(pl.multiple_of((s_of * count + chip) * rows, rows), rows)

                lefts = [jnp.concatenate([a[lines(1 - s), :], a[lines(s), :]], axis=0) for a in self.a_refs]
                for c in range(0, width, tile):
                    if self.turned:
                        values = [back_dot(left, b[c : c + tile, :]) for left, b in zip(lefts, self.b_refs)]
                    else:
                        values = [forward_dot(left, b[:, c : c + tile]) for left, b in zip(lefts, self.b_refs)]
                    value = functools.reduce(jnp.add, values).astype(BF)
                    self.give[chip, :, c : c + tile] = value[:rows]
                    self.mine[chip, :, c : c + tile] = value[rows:]
                self.core(chip).start()

            @pl.when(i > 0)
            def _():
                e = count - i
                chip = here.other(e)
                arrived(self.core_in.at[chip], self.core_recv.at[chip])
                add_rows(self.mine.at[chip], [self.core_in.at[chip]])
                for p in self.parts:
                    pl.when(e // 2 ** ((p + n - 1) % n) % 2 == 1)(
                        lambda p=p: self.hand(p, here.positions(p, e), n - 1).start()
                    )

    def waiting(self, p, m):
        cols = pl.ds(*self.spans[p])
        terms = [m + 2**t for t in range(m.bit_length(), self.here.n)]
        for term in terms:
            arrived(self.landed.at[term, :, cols], self.recv.at[p, term])
        place = self.mine.at[self.here.other(self.here.dims(p, m)), :, cols]
        return place, [self.landed.at[term, :, cols] for term in terms]

    def pass_on(self, m):
        for p in self.parts:
            add_rows(*self.waiting(p, m))
            self.hand(p, m, m.bit_length() - 1).start()

    def settle(self):
        for p in self.parts:
            place, terms = self.waiting(p, 0)
            add_rows(place, terms, self.out_ref.at[:, pl.ds(*self.spans[p])])

    def drain(self):
        for chip in range(self.here.count):
            self.core(chip).wait_send()
        for m in range(1, self.here.count):
            for p in self.parts:
                self.hand(p, m, m.bit_length() - 1).wait_send()


def scatter_scratch(bits, block):
    n, count = len(bits), 2 ** len(bits)
    dma = pltpu.SemaphoreType.DMA
    return [pltpu.VMEM((count,) + block, BF)] * 4 + [dma((count,))] * 2 + [dma((n, count))] * 2


def scatter_kernel(bits, turned, homing, kinds, shares, terms, *refs):
    here = Place(bits)
    s, count = here.s, here.count
    along = len(kinds)
    a_refs, b_refs, refs = refs[:terms], refs[terms : 2 * terms], refs[2 * terms :]
    if homing:
        grad, refs = refs[0], refs[1:]
    rider_in, refs = refs[:along], refs[along:]
    out_ref, refs = refs[0], refs[1:]
    if homing:
        home, other_home = refs[:2]
        refs = refs[2:]
    rider_out, refs = refs[:along], refs[along:]
    work = Scatter(here, turned, shares, a_refs, b_refs, out_ref, refs[:8])
    if homing:
        q_in, ready, kept, kept_sem, q_send, q_recv, home_send, home_recv, over_send, over_recv = refs[8:18]
        keep = pltpu.make_async_copy(grad.at[lax.axis_index("q")], kept, kept_sem)
    ride_start, ride_end = ride(here, kinds, rider_in + rider_out + refs[len(refs) - 2 * along :])

    def to_q(e):
        q, chip = lax.axis_index("q"), here.other(e)
        return remote(grad.at[1 - q, chip], q_in.at[chip], q_send.at[e], q_recv.at[e], {"q": 1 - q})

    def to_chip(e):
        return remote(ready.at[here.other(e)], home.at[here.other(0)], home_send.at[e], home_recv.at[e], here.toward(e))

    def to_core(e):
        chip = here.other(e)
        return remote(home.at[chip], other_home.at[chip], over_send.at[e], over_recv.at[e], {"section": 1 - s})

    def home_step(e):
        chip = here.other(e)
        arrived(q_in.at[chip], q_recv.at[e])
        place = ready.at[chip] if e else home.at[chip]
        add_rows(q_in.at[chip], [kept.at[chip]], place)
        (to_chip(e) if e else to_core(0)).start()

    def home_end(e):
        if e:
            arrived(home.at[here.other(e)], home_recv.at[e])
            to_core(e).start()

    peers = work.peers
    if homing:
        peers = [here.names(e) for e in range(1, count)] + [("section",), ("q",)]
    here.meet(peers + rider_peers(here, kinds))
    if homing:
        for e in range(count):
            to_q(e).start()
        keep.start()
    ride_start()
    work.produce(0, count + 1)
    if homing:
        keep.wait()
    steps = count // 2
    for m in range(steps - 1, 0, -1):
        if homing:
            home_step(2 * (steps - 1 - m))
            home_step(2 * (steps - 1 - m) + 1)
        work.pass_on(m)
    work.settle()
    if homing:
        for e in range(count - 2, count):
            home_step(e)
        for e in range(count):
            home_end(e)
        for e in range(count):
            arrived(other_home.at[here.other(e)], over_recv.at[e])
            to_core(e).wait_send()
            to_q(e).wait_send()
            if e:
                to_chip(e).wait_send()
    ride_end()
    work.drain()


def scatter_columns(bits, cid, a, b, turned, grad=None, riders=(), shares=None):
    tokens, width = a[0].shape[0], b[0].shape[0 if turned else 1]
    count = 2 ** len(bits)
    block = (tokens // (2 * count), width)
    dma = pltpu.SemaphoreType.DMA
    operands = list(a) + list(b)
    shapes = [jax.ShapeDtypeStruct(block, F32)]
    scratch = scatter_scratch(bits, block)
    if grad is not None:
        operands += [grad]
        shapes += [jax.ShapeDtypeStruct(grad.shape[1:], BF)] * 2
        scratch += [pltpu.VMEM(grad.shape[1:], BF)] * 3 + [dma] + [dma((count,))] * 6
    arrays, more_shapes, more_scratch = rider_shapes(bits, riders)
    inside, outside = pl.BlockSpec(memory_space=pltpu.VMEM), pl.BlockSpec(memory_space=pl.ANY)
    return pl.pallas_call(
        functools.partial(
            scatter_kernel, bits, turned, grad is not None, tuple(kind for kind, _ in riders), shares, len(a)
        ),
        out_shape=shapes + more_shapes,
        in_specs=[inside] * (2 * len(a)) + [outside] * (len(operands) - 2 * len(a) + len(arrays)),
        out_specs=[inside] * len(shapes) + [outside] * len(arrays),
        scratch_shapes=scratch + more_scratch,
        compiler_params=pltpu.CompilerParams(
            collective_id=cid, has_side_effects=True, vmem_limit_bytes=56 * 2**20
        ),
        cost_estimate=lasting(40 if grad is None else 60),
    )(*operands, *arrays)


def scatter_dot(bits, cid, a, b, turned, grad=None, riders=(), shares=None):
    tokens, width = a[0].shape[0], b[0].shape[0 if turned else 1]
    pieces = max(1, tokens * width // 2**22)
    size = width // pieces
    cuts = [
        [f[i * size : (i + 1) * size] if turned else f[:, i * size : (i + 1) * size] for f in b] for i in range(pieces)
    ]
    first = scatter_columns(bits, cid, a, cuts[0], turned, grad, riders, shares)
    rest = [scatter_columns(bits, 14 + turned, a, cut, turned)[0] for cut in cuts[1:]]
    return [jnp.concatenate([first[0]] + rest, axis=1)] + list(first[1:])


def total_kernel(bits, kinds, x_ref, *refs):
    here = Place(bits)
    s, count = here.s, here.count
    along = len(kinds)
    rider_in, out_ref, rider_out, refs = refs[:along], refs[along], refs[along + 1 : 2 * along + 1], refs[2 * along + 1 :]
    part, core_in, ready, landed, done, pair_send, pair_recv, send, recv, back_send, back_recv = refs[:11]
    ride_start, ride_end = ride(here, kinds, rider_in + rider_out + refs[11:])
    lanes = part.shape[3]

    def span(s_of, chip):
        at = (s_of * count + chip) * lanes
        return slice(at, at + lanes)

    for s_of in range(2):
        for chip in range(count):
            part[s_of, chip] = x_ref[:, span(s_of, chip)]
    here.meet([here.names(e) for e in range(1, count)] + [("section",)] + rider_peers(here, kinds))
    first = remote(part.at[1 - s], core_in, pair_send.at[0], pair_recv.at[0], {"section": 1 - s})
    first.start()
    first.wait_recv()
    for chip in range(count):
        total = part[s, chip] + core_in[chip]
        part[s, chip] = total
        ready[chip] = total.astype(BF)

    def out(e):
        return remote(ready.at[here.other(e)], landed.at[e], send.at[e], recv.at[e], here.toward(e))

    def back(e):
        place = done.at[s, here.other(0)]
        return remote(place, place, back_send.at[e], back_recv.at[e], here.toward(e))

    others = range(1, count)
    for e in others:
        out(e).start()
    ride_start()
    total = part[s, here.other(0)]
    for e in others:
        out(e).wait_recv()
        total = total + landed[e].astype(F32)
    done[s, here.other(0)] = total.astype(BF)
    for e in others:
        back(e).start()
    for e in others:
        place = done.at[s, here.other(e)]
        arrived(place, back_recv.at[e])
    last = remote(done.at[s], done.at[s], pair_send.at[1], pair_recv.at[1], {"section": 1 - s})
    last.start()
    last.wait_recv()
    for s_of in range(2):
        for chip in range(count):
            out_ref[:, span(s_of, chip)] = done[s_of, chip]
    ride_end()
    first.wait_send()
    last.wait_send()
    for e in others:
        out(e).wait_send()
        back(e).wait_send()


def sum_columns(bits, cid, x, riders=()):
    rows, tokens = x.shape
    count = 2 ** len(bits)
    block = (rows, tokens // (2 * count))
    dma, vmem = pltpu.SemaphoreType.DMA, pltpu.VMEM
    arrays, more_shapes, more_scratch = rider_shapes(bits, riders)
    inside, outside = pl.BlockSpec(memory_space=pltpu.VMEM), pl.BlockSpec(memory_space=pl.ANY)
    return pl.pallas_call(
        functools.partial(total_kernel, bits, tuple(kind for kind, _ in riders)),
        out_shape=[jax.ShapeDtypeStruct((rows, tokens), BF)] + more_shapes,
        in_specs=[inside] + [outside] * len(arrays),
        out_specs=[inside] + [outside] * len(arrays),
        scratch_shapes=[
            vmem((2, count) + block, F32),
            vmem((count,) + block, F32),
            vmem((count,) + block, BF),
            vmem((count,) + block, BF),
            vmem((2, count) + block, BF),
        ]
        + [dma((2,))] * 2
        + [dma((count,))] * 4
        + more_scratch,
        compiler_params=pltpu.CompilerParams(
            collective_id=cid, has_side_effects=True, vmem_limit_bytes=56 * 2**20
        ),
        cost_estimate=lasting(22),
    )(x, *arrays)


def spread_kernel(bits, kinds, count_blocks, shard_ref, *refs):
    here = Place(bits)
    along = len(kinds)
    blocks, small, refs = refs[:count_blocks], refs[count_blocks], refs[count_blocks + 1 :]
    rider_in, refs = refs[:along], refs[along:]
    out_ref, rows, own_small, refs = refs[0], refs[1:3], refs[3], refs[4:]
    rider_out, refs = refs[:along], refs[along:]
    send, recv, pair_send, pair_recv, piece_send, piece_recv, small_send, small_recv = refs[:8]
    ride_start, ride_end = ride(here, kinds, rider_in + rider_out + refs[8:])
    s, q, chip, count = here.s, lax.axis_index("q"), here.other(0), here.count
    others = range(1, count)
    peers = [here.names(e) + extra for e in range(count) for extra in ((), ("section",)) if e or extra]
    here.meet(peers + [("q",), ("q", "section")])

    def block(i, s_of, chip_of):
        if count_blocks == 2:
            return blocks[i].at[s_of, chip_of]
        wide = blocks[0].shape[1] // (4 * count)
        return blocks[0].at[:, pl.ds(pl.multiple_of(((i * 2 + s_of) * count + chip_of) * wide, 128), wide)]

    def piece(i, r, e):
        where = dict(here.toward(e), **({"section": 1 - s} if r else {}))
        src = block(i, 1 - s if r else s, here.other(e))
        return remote(src, rows[i].at[chip], piece_send.at[i, r, e], piece_recv.at[i, e], where)

    def hand_small(k, where):
        return remote(small, own_small, small_send.at[k], small_recv, where)

    keep_pieces = [pltpu.make_async_copy(block(i, s, chip), rows[i].at[chip], piece_recv.at[i, 0]) for i in range(2)]
    keep_small = pltpu.make_async_copy(small, own_small, small_recv)
    at_layer = s == 0
    stays, leaves = jnp.logical_and(at_layer, q == s), jnp.logical_and(at_layer, q != s)

    out_ref[s, q, chip] = shard_ref[...]
    own = out_ref.at[s, q, chip]
    copies = [remote(own, own, send.at[e], recv.at[e], here.toward(e)) for e in others]
    for copy in copies:
        copy.start()
    ride_start()

    @pl.when(at_layer)
    def _():
        for i in range(2):
            keep_pieces[i].start()
            for e in range(count):
                for r in range(2):
                    if e or r:
                        piece(i, r, e).start()

    @pl.when(stays)
    def _():
        keep_small.start()
        hand_small(0, {"q": 1 - q}).start()

    @pl.when(leaves)
    def _():
        hand_small(0, {"section": 1 - s}).start()
        hand_small(1, {"section": 1 - s, "q": 1 - q}).start()

    for e in others:
        arrived(out_ref.at[s, q, here.other(e)], recv.at[e])
    place = out_ref.at[s, q]
    first = remote(place, place, pair_send.at[0], pair_recv.at[0], {"q": 1 - q})
    first.start()
    first.wait_recv()
    place = out_ref.at[s]
    second = remote(place, place, pair_send.at[1], pair_recv.at[1], {"section": 1 - s})
    second.start()
    second.wait_recv()
    ride_end()
    arrived(own_small, small_recv)
    for i in range(2):
        for e in range(count):
            arrived(rows[i].at[here.other(e)], piece_recv.at[i, e])
    for copy in copies + [first, second]:
        copy.wait_send()

    @pl.when(at_layer)
    def _():
        for i in range(2):
            for e in range(count):
                for r in range(2):
                    if e or r:
                        piece(i, r, e).wait_send()

    pl.when(stays)(lambda: hand_small(0, {"q": 1 - q}).wait_send())

    @pl.when(leaves)
    def _():
        hand_small(0, {"section": 1 - s}).wait_send()
        hand_small(1, {"section": 1 - s, "q": 1 - q}).wait_send()


def spread(bits, shard, blocks, small, riders):
    arrays, more_shapes, more_scratch = rider_shapes(bits, riders)
    width, count = shard.shape[0], 2 ** len(bits)
    block = (16, max(width, 128))
    padded = jnp.pad(shard[None, :], ((0, block[0] - 1), (0, block[1] - width)))
    dma = pltpu.SemaphoreType.DMA
    shapes = [jax.ShapeDtypeStruct((2, 2, count) + block, shard.dtype)]
    if len(blocks) == 2:
        piece = blocks[0].shape[1:]
    else:
        piece = (count, blocks[0].shape[0], blocks[0].shape[1] // (4 * count))
    shapes += [jax.ShapeDtypeStruct(piece, b.dtype) for b in (blocks[0], blocks[0])] + [jax.ShapeDtypeStruct(small.shape, small.dtype)]
    inside, outside = pl.BlockSpec(memory_space=pltpu.VMEM), pl.BlockSpec(memory_space=pl.ANY)
    out, *gots = pl.pallas_call(
        functools.partial(spread_kernel, bits, tuple(kind for kind, _ in riders), len(blocks)),
        out_shape=shapes + more_shapes,
        in_specs=[inside] + [outside] * (len(blocks) + 1 + len(arrays)),
        out_specs=[inside] + [outside] * (3 + len(arrays)),
        scratch_shapes=[dma((count,)), dma((count,)), dma((2,)), dma((2,))]
        + [dma((2, 2, count)), dma((2, count)), dma((2,)), dma]
        + more_scratch,
        compiler_params=pltpu.CompilerParams(collective_id=0, has_side_effects=True),
        cost_estimate=lasting(12),
    )(padded, *blocks, small, *arrays)
    return [out[:, :, :, 0, :width].reshape((2, -1))] + gots


def chips(bits):
    return tuple(reversed(bits))


def at_home():
    return lax.axis_index("q") == lax.axis_index("section")


def low_first(mine, other):
    low = lax.axis_index("q") == 0
    return jnp.stack([jnp.where(low, mine, other), jnp.where(low, other, mine)])


def by_q(pair):
    low = lax.axis_index("q") == 0
    return jnp.where(low, pair[0], pair[1]), jnp.where(low, pair[1], pair[0])


def leave(value):
    return lax.ppermute(value, ("section", "q"), [(0, 1), (3, 2)])


def home(value):
    return lax.ppermute(value, ("section", "q"), [(1, 0), (2, 3)])


def swap(value):
    return lax.ppermute(value, "q", [(0, 1), (1, 0)])


def after(value, *earlier):
    return lax.optimization_barrier((value,) + earlier)[0]


def column_blocks(bits, rows):
    parts = rows.reshape((rows.shape[0], 2, 2, 2 ** len(bits), -1))
    return [jnp.transpose(parts[:, i], (1, 2, 0, 3)) for i in range(2)]


def assemble_kernel(lower_refs, upper_refs, weight_ref, out_ref, gain_ref):
    depth = weight_ref.shape[0]
    step = min(depth, 32)

    def fill(parts):
        chips, _, wide = parts[0].shape

        @pl.loop(0, depth // step)
        def _(r):
            lines = pl.ds(pl.multiple_of(r * step, step), step)
            total = jnp.zeros((step, wide), F32)
            for i, part in enumerate(parts):
                for chip in range(chips):
                    at = (i * chips + chip) * wide
                    value = part[chip, lines, :].astype(F32)
                    out_ref[lines, at : at + wide] = value
                    total = total + value * weight_ref[lines, at : at + wide].astype(F32)
            gain_ref[lines, :] = jnp.sum(total, axis=1, keepdims=True)

    upper = lax.axis_index("section") == 1
    pl.when(jnp.logical_not(upper))(lambda: fill(lower_refs))
    pl.when(upper)(lambda: fill(upper_refs))


def assemble(lower, upper, weight):
    inside = pl.BlockSpec(memory_space=pltpu.VMEM)
    return pl.pallas_call(
        assemble_kernel,
        out_shape=[jax.ShapeDtypeStruct(weight.shape, F32), jax.ShapeDtypeStruct((weight.shape[0], 1), F32)],
        in_specs=[[inside] * 4, [inside] * 4, inside],
        out_specs=[inside, inside],
        compiler_params=pltpu.CompilerParams(vmem_limit_bytes=40 * 2**20),
    )(lower, upper, weight)


def silu_slope(v):
    gate = jax.nn.sigmoid(v)
    return gate, gate * (1.0 + v * (1.0 - gate))


def normalize(stream, gain):
    inverse = lax.rsqrt(jnp.mean(stream * stream, axis=-1, keepdims=True) + norm_eps)
    return inverse, (stream * inverse * gain[None, :]).astype(BF)


class Small:
    def __init__(self, packed):
        self.taps = packed[:KC].astype(F32)
        self.conv_bias = packed[KC].astype(F32)
        self.dt_bias = packed[KC + 1].astype(F32)
        self.skip = packed[KC + 2].astype(F32)
        self.dt = packed[KC + 3 : KC + 3 + R]
        self.xproj = packed[KC + 3 + R : KC + 3 + 2 * R + 2 * N]


def mixer_inputs(normed, in_inner, small):
    inner = forward_dot(normed, in_inner).astype(BF).astype(F32)
    tokens, channels = inner.shape
    extended = jnp.concatenate([jnp.zeros((KC - 1, channels), F32), inner], axis=0)
    conv = jnp.broadcast_to(small.conv_bias[None, :], (tokens, channels))
    for tap in range(KC):
        conv = conv + small.taps[tap][None, :] * extended[tap : tap + tokens]
    act = jax.nn.silu(conv)
    return extended, conv, act, back_dot(small.xproj, act.astype(BF))


def mixer(xproj, act, normed, in_gate, small):
    gate_in = forward_dot(normed, in_gate).astype(BF).astype(F32)
    key_t, query_t = xproj[R : R + N].astype(F32), xproj[R + N :].astype(F32)
    key_norm = jnp.sum(key_t * key_t, axis=0)[:, None]
    write = jax.nn.sigmoid(cross_dot(xproj[:R], small.dt) + small.dt_bias[None, :])
    rate = write / (1.0 + write * key_norm)
    recur, before, last = recur_forward(rate, act, key_t, query_t)
    recur = recur + small.skip[None, :] * act
    gated = (recur * jax.nn.silu(gate_in)).astype(BF)
    return gate_in, key_t, query_t, key_norm, write, rate, recur, gated, before, last


def gate_back(grad_low, out_weight, kept):
    gate_in, recur = kept[0], kept[6]
    d_gated = back_dot(grad_low, out_weight).astype(BF).astype(F32)
    gate, slope = silu_slope(gate_in)
    return d_gated * (gate_in * gate), (d_gated * recur * slope).astype(BF)


def mixer_back(bits, cid, d_recur, act, xproj, kept, small, riders, product=(), shares=None):
    key_t, query_t, key_norm, write, rate, recur, gated, before, last = kept[1:]
    d_skip = jnp.sum(d_recur * act, axis=0)
    d_rate, d_act_rec, d_key_t, d_query_t, *gots = recur_backward(
        bits, cid, rate, act, d_recur, key_t, query_t, before, last, riders, product, shares
    )
    share = 1.0 / (1.0 + write * key_norm)
    pulled = d_rate * share * share
    d_pre = pulled * write * (1.0 - write)
    d_key_rate = -2.0 * key_t * jnp.sum(pulled * write * write, axis=1)[None, :]
    d_dt_bias = jnp.sum(d_pre, axis=0)
    d_delta = d_pre.astype(BF)
    d_dt = forward_dot(xproj[:R], d_delta)
    d_xproj = jnp.concatenate([back_dot(small.dt, d_delta), d_key_t + d_key_rate, d_query_t], axis=0)
    return d_act_rec, d_xproj, (d_dt_bias[None], d_skip[None], d_dt), gots


def inputs_back(d_xproj, d_recur, d_act_rec, extended, conv, act, small):
    tokens = act.shape[0]
    d_act = cross_dot(d_xproj, small.xproj) + small.skip[None, :] * d_recur + d_act_rec
    d_conv = d_act * silu_slope(conv)[1]
    d_taps = jnp.stack([jnp.sum(d_conv * extended[tap : tap + tokens], axis=0) for tap in range(KC)])
    d_bias = jnp.sum(d_conv, axis=0)
    later = jnp.concatenate([d_conv, jnp.zeros((KC - 1, d_conv.shape[1]), F32)], axis=0)
    d_inner = sum(small.taps[tap][None, :] * later[KC - 1 - tap : KC - 1 - tap + tokens] for tap in range(KC))
    return d_inner.astype(BF), (d_taps, d_bias[None]), forward_dot(d_xproj, act.astype(BF))


def norm_back(grad_out, d_normed, stream, inverse, gain):
    scaled = gain[None, :] * d_normed
    mean = jnp.mean(stream * scaled, axis=-1, keepdims=True)
    return grad_out + inverse * scaled - stream * inverse**3 * mean


def pack(first, second, third):
    packed = jnp.concatenate(first + second + (third,), axis=0)
    return jnp.pad(packed, ((0, -packed.shape[0] % 16), (0, 0)))


def on_device(
    bits, hidden_in, cotangent, norm_gain, in_weight, conv_weight, conv_bias, xproj_weight, dt_weight, dt_bias, skip_gain, out_weight
):
    packed = pack(
        (conv_weight[0], conv_bias),
        (dt_bias, skip_gain, dt_weight[0]),
        jnp.swapaxes(xproj_weight[0], 0, 1),
    )
    rows = in_weight[0]
    channels = conv_bias.shape[1]
    aligned = channels % 128 == 0
    blocks = [rows] if aligned else column_blocks(bits, rows)
    tight = (2, 5, 9)

    def weight(pair):
        return pair.reshape((-1, pair.shape[-1]))

    def weight_grad(normed, d_out):
        return cross_dot(normed, d_out).astype(BF).reshape((2, 2 ** len(bits), rows.shape[0], channels))

    mine, others = by_q(hidden_in)
    gains, inner, gate, packed0, got = spread(bits, norm_gain[0], blocks, packed, [("leave", others)])
    gains = gains.astype(F32)
    stream0 = jnp.where(at_home(), mine, got).astype(F32)

    inverse0, normed = normalize(stream0, gains[0])
    normed0, inner, gate, *sent = gather_call(
        bits, 1, [normed], shares=tight, us=60,
        riders=[("stack", inner), ("stack", gate)] + ([("over_cols0", rows), ("over_cols1", rows)] if aligned else [("over_at", b) for b in blocks])
        + [("out1", packed)] + [("out%d" % l, out_weight[0]) for l in range(2)],
    )
    upper = lax.axis_index("section") == 1
    if aligned:
        slab = rows.shape[1] // 4
        columns = [("cube_cols", jnp.where(upper, rows[:, slab : 2 * slab], sent[0]))]
        columns += [("cube_cols", jnp.where(upper, rows[:, 3 * slab :], sent[1]))]
    else:
        columns = [("cube", jnp.where(upper, b[1], got)) for b, got in zip(blocks, sent)]
    packed_held = jnp.where(upper, packed, sent[2])
    out_held = jnp.where(upper, sent[3], out_weight[0]), jnp.where(upper, out_weight[0], sent[4])
    inner0, small0 = weight(inner), Small(packed0)
    extended0, conv0, act0, part = mixer_inputs(normed0, inner0, small0)
    part = after(part, out_held[0])
    xproj0, inner, late_gate = sum_columns(bits, 4, part, columns)
    gate0 = weight(gate)
    out0 = jnp.where(at_home(), out_held[0], leave(after(out_held[0], xproj0)))
    kept0 = mixer(xproj0, act0, normed0, gate0, small0)
    grad_mine, grad_others = by_q(cotangent)
    added, got, grad_got, gate = scatter_dot(
        bits, 8, [kept0[7]], [out0], False, shares=(3, 5, 8),
        riders=[("leave", packed_held), ("leave", grad_others.astype(BF)), ("stack", late_gate)],
    )
    gate1 = weight(gate)
    grad1 = jnp.where(at_home(), grad_mine, grad_got.astype(F32))
    small1 = Small(jnp.where(at_home(), packed_held, got))
    output0 = (stream0 + added).astype(BF)

    stream1 = output0.astype(F32)
    inverse1, normed = normalize(stream1, gains[1])
    normed1, grad_low1, inner = gather_call(
        bits, 2, [normed, grad1.astype(BF)], riders=[("stack", inner)], shares=(4, 5, 7), us=65
    )
    inner1 = weight(inner)
    extended1, conv1, act1, part = mixer_inputs(normed1, inner1, small1)
    xproj1, output0_home = sum_columns(bits, 5, after(part, out_held[1]), [("home", output0)])
    out1 = jnp.where(at_home(), out_held[1], leave(after(out_held[1], xproj1)))
    kept1 = mixer(xproj1, act1, normed1, gate1, small1)

    d_out1 = cross_dot(kept1[7], grad_low1).astype(BF)
    d_recur, d_gate1 = gate_back(grad_low1, out1, kept1)
    keep, give = by_q(weight_grad(normed1, d_gate1))
    beside = kept1[7].shape[0] * out1.shape[1] <= 2**22 and kept1[7].shape[0] >= 16 * BLOCK
    if beside:
        d_act_rec, part, d_small, (added, got) = mixer_back(
            bits, 16, d_recur, act1, xproj1, kept1, small1, [("swap", give)], (kept1[7], out1), (4, 5, 7)
        )
    else:
        (added,) = scatter_dot(bits, 10, [kept1[7]], [out1], False)
        d_act_rec, part, d_small, (got,) = mixer_back(bits, 16, d_recur, act1, xproj1, kept1, small1, [("swap", give)])
    output1 = (stream1 + added).astype(BF)
    d_xproj, output1_home = sum_columns(bits, 6, part, [("home", output1)])
    d_gate_in1 = (keep.astype(F32) + got.astype(F32)).astype(BF)
    d_inner, d_conv, d_xproj_weight = inputs_back(d_xproj, d_recur, d_act_rec, extended1, conv1, act1, small1)
    d_packed1 = pack(d_conv, d_small, d_xproj_weight)
    d_normed, d_gate_in1, d_packed1_home, d_out1_home = scatter_dot(
        bits, 11, [d_inner, d_gate1], [inner1, gate1], True,
        riders=[("cube", d_gate_in1), ("home", d_packed1.astype(BF)), ("home", d_out1)], shares=(4, 5, 7),
    )
    keep, give = by_q(weight_grad(normed1, d_inner))
    input_grad1 = norm_back(grad1, d_normed, stream1, inverse1, gains[1])
    grad0 = input_grad1.astype(BF)
    grad_low0, got, grad1_home = gather_call(
        bits, 3, [grad0], riders=[("swap", give), ("home", grad0)], shares=(3, 5, 8), us=45
    )
    d_inner1 = (keep.astype(F32) + got.astype(F32)).astype(BF)

    d_out0 = cross_dot(kept0[7], grad_low0).astype(BF)
    d_recur, d_gate0 = gate_back(grad_low0, out0, kept0)
    keep, give = by_q(weight_grad(normed0, d_gate0))
    d_act_rec, part, d_small, (got, d_inner1) = mixer_back(
        bits, 17, d_recur, act0, xproj0, kept0, small0, [("swap", give), ("cube", d_inner1)]
    )
    d_gate_in0 = (keep.astype(F32) + got.astype(F32)).astype(BF)
    d_xproj, d_gate_in0, d_out0_home = sum_columns(
        bits, 7, part, [("cube", d_gate_in0), ("home", d_out0)]
    )
    d_inner, d_conv, d_xproj_weight = inputs_back(d_xproj, d_recur, d_act_rec, extended0, conv0, act0, small0)
    d_packed0 = pack(d_conv, d_small, d_xproj_weight)
    d_out = [
        (mine.astype(F32) + other.astype(F32)).astype(BF) for mine, other in ((d_out0, d_out0_home), (d_out1, d_out1_home))
    ]
    d_packed1 = (d_packed1 + d_packed1_home.astype(F32)).astype(BF)
    gate_over = jnp.where(upper, d_gate_in0, d_gate_in1)
    d_normed, d_inner0, d_inner0_other, d_packed0_home, inner_other, gate_other, *backs = scatter_dot(
        bits, 13, [d_inner, d_gate0], [inner0, gate0], True, weight_grad(normed0, d_inner), shares=(3, 5, 8),
        riders=[
            ("home", d_packed0.astype(BF)), ("over", d_inner1), ("over", gate_over), ("back0", d_out[0]), ("back1", d_out[1]),
            ("back1", d_packed1), ("back0", output0), ("back0", output0_home), ("back1", output1), ("back1", output1_home),
            ("back1", grad0), ("back1", grad1_home),
        ],
    )
    input_grad0 = norm_back(grad0.astype(F32), d_normed, stream0, inverse0, gains[0]).astype(BF)

    def settled(lower, upper_one, lower_back, upper_back):
        return jnp.where(at_home(), jnp.where(upper, upper_one, lower), jnp.where(upper, upper_back, lower_back))

    d_out = settled(*d_out, *backs[:2]).astype(F32)
    d_packed0 = (d_packed0 + d_packed0_home.astype(F32)).astype(BF)
    d_packed = settled(d_packed0, d_packed1, lax.ppermute(d_packed0, ("section", "q"), [(3, 1)]), backs[2]).astype(F32)
    low = lax.axis_index("q") == 0
    mine, other = settled(output0, output1, backs[3], backs[5]), settled(output0_home, output1_home, backs[4], backs[6])
    layer_outputs = low_first(mine, other).astype(F32)
    mine, other = jnp.where(at_home(), grad0, backs[7]), jnp.where(at_home(), grad1_home, backs[8])
    grads1 = low_first(mine, other)
    of_first = lax.ppermute(input_grad0, ("section", "q"), [(2, 1)])
    of_second = lax.ppermute(input_grad0, ("section", "q"), [(1, 0), (3, 1)])
    grads0 = jnp.stack([jnp.where(low, input_grad0, of_first), of_second])
    input_grads = jnp.where(upper, grads1, grads0).astype(F32)
    d_in, d_gain = assemble(
        [d_inner0, d_inner0_other, d_gate_in0, gate_other], [inner_other, d_inner1, gate_other, d_gate_in1], in_weight[0]
    )
    d_gain = d_gain[:, 0] / norm_gain[0].astype(F32)
    return (
        layer_outputs[None],
        input_grads[None],
        d_gain[None],
        d_in[None],
        d_packed[None, :KC],
        d_packed[None, KC],
        jnp.swapaxes(d_packed[KC + 3 + R : KC + 3 + 2 * R + 2 * N], 0, 1)[None],
        d_packed[None, KC + 3 : KC + 3 + R],
        d_packed[None, KC + 1],
        d_packed[None, KC + 2],
        d_out[None],
    )


def solution(mesh):
    sections, chip_count = mesh.devices.shape
    n = chip_count.bit_length() - 2
    bits = tuple("c%d" % d for d in range(n))
    split = Mesh(mesh.devices.reshape((sections,) + (2,) * (n + 1)), ("section", "q") + chips(bits))
    seq = ("q",) + chips(bits)
    placed = (
        P(None, seq, None),
        P(None, seq, None),
        P("section", seq),
        P("section", seq, None),
        P("section", None, seq),
        P("section", seq),
        P("section", seq, None),
        P("section", None, seq),
        P("section", seq),
        P("section", seq),
        P("section", seq, None),
    )
    return jax.shard_map(
        functools.partial(on_device, bits),
        mesh=split,
        in_specs=placed,
        out_specs=(P("section", None, seq, None), P("section", None, seq, None)) + placed[2:],
        check_vma=False,
    )
```
